32 devices in a mesh: rep: 8 (over y, x, core), shard: 4 (over z).
Axes of the slice: x: 2, y: 2, z: 4, core: 2. Of those that a mesh axis runs over, the one named last changes fastest.
Arguments:
- tokens: bfloat16 [16384, 1536], P(('rep', 'shard')), may hold values from -6 to 6
- cotangent: bfloat16 [16384, 1536], P(('rep', 'shard'))
- seg_ids: int32 [32, 512], P(('rep', 'shard')), may hold values from 0 to 12, as said below
- parents: int32 [32, 13], P(('rep', 'shard')), may hold values from -1 to 4, as said below
- positions: int32 [32, 512], P(('rep', 'shard')), may hold values from 0 to 1023, as said below
- routes: int32 [16384, 4], P(('rep', 'shard')), may hold values from 0 to 7, all different within a row
- query_weight: float32 [1536, 1536], P('shard', 'rep'), may hold values from -0.15625 to 0.15625
- pair_weight: float32 [2, 1536, 256], P(None, 'shard', 'rep'), may hold values from -0.15625 to 0.15625
- output_weight: float32 [1536, 1536], P('shard', 'rep'), may hold values from -1.75 to 1.75
- inner_weight: float32 [2, 8, 1536, 768], P(None, None, 'shard', 'rep'), may hold values from -0.15625 to 0.15625
- outer_weight: float32 [8, 768, 1536], P(None, 'shard', 'rep'), may hold values from -0.3125 to 0.3125
- router_weight: float32 [1536, 8], P('shard'), may hold values from -0.0546875 to 0.0546875
- norm_gains: float32 [2, 1536], P(None, 'shard'), may hold values from 0 to 3
- query_moment: float32 [1536, 1536], P('shard', 'rep'), may hold values from -0.75 to 0.75
- pair_moment: float32 [2, 1536, 256], P(None, 'shard', 'rep'), may hold values from -0.75 to 0.75
- output_moment: float32 [1536, 1536], P('shard', 'rep'), may hold values from -0.75 to 0.75
- inner_moment: float32 [2, 8, 1536, 768], P(None, None, 'shard', 'rep'), may hold values from -0.75 to 0.75
- outer_moment: float32 [8, 768, 1536], P(None, 'shard', 'rep'), may hold values from -0.75 to 0.75
- router_moment: float32 [1536, 8], P('shard'), may hold values from -0.75 to 0.75
- gains_moment: float32 [2, 1536], P(None, 'shard'), may hold values from -0.75 to 0.75
- query_error: float32 [8, 1536, 1536], P('rep', 'shard')
- pair_error: float32 [8, 2, 1536, 256], P('rep', None, 'shard')
- output_error: float32 [8, 1536, 1536], P('rep', 'shard')
- inner_error: float32 [8, 2, 8, 1536, 768], P('rep', None, None, 'shard')
- outer_error: float32 [8, 8, 768, 1536], P('rep', None, 'shard')
- query_start: float32 [1536, 8], replicated, may hold values from -6 to 6
- pair_start: float32 [2, 256, 8], replicated, may hold values from -6 to 6
- output_start: float32 [1536, 8], replicated, may hold values from -6 to 6
- inner_start: float32 [2, 8, 768, 8], replicated, may hold values from -6 to 6
- outer_start: float32 [8, 1536, 8], replicated, may hold values from -6 to 6
Outputs:
- output: bfloat16 [16384, 1536], P(('rep', 'shard'))
- input_grad: bfloat16 [16384, 1536], P(('rep', 'shard'))
- query_left: float32 [1536, 8], P('shard')
- pair_left: float32 [2, 1536, 8], P(None, 'shard')
- output_left: float32 [1536, 8], P('shard')
- inner_left: float32 [2, 8, 1536, 8], P(None, None, 'shard')
- outer_left: float32 [8, 768, 8], P(None, 'shard')
- query_right: float32 [1536, 8], replicated
- pair_right: float32 [2, 256, 8], replicated
- output_right: float32 [1536, 8], replicated
- inner_right: float32 [2, 8, 768, 8], replicated
- outer_right: float32 [8, 1536, 8], replicated
- query_feedback: float32 [8, 1536, 1536], P('rep', 'shard')
- pair_feedback: float32 [8, 2, 1536, 256], P('rep', None, 'shard')
- output_feedback: float32 [8, 1536, 1536], P('rep', 'shard')
- inner_feedback: float32 [8, 2, 8, 1536, 768], P('rep', None, None, 'shard')
- outer_feedback: float32 [8, 8, 768, 1536], P('rep', None, 'shard')
- query_momentum: float32 [1536, 1536], P('shard', 'rep')
- pair_momentum: float32 [2, 1536, 256], P(None, 'shard', 'rep')
- output_momentum: float32 [1536, 1536], P('shard', 'rep')
- inner_momentum: float32 [2, 8, 1536, 768], P(None, None, 'shard', 'rep')
- outer_momentum: float32 [8, 768, 1536], P(None, 'shard', 'rep')
- router_momentum: float32 [1536, 8], P('shard')
- gains_momentum: float32 [2, 1536], P(None, 'shard')
- query_master: float32 [1536, 1536], P('shard', 'rep')
- pair_master: float32 [2, 1536, 256], P(None, 'shard', 'rep')
- output_master: float32 [1536, 1536], P('shard', 'rep')
- inner_master: float32 [2, 8, 1536, 768], P(None, None, 'shard', 'rep')
- outer_master: float32 [8, 768, 1536], P(None, 'shard', 'rep')
- router_master: float32 [1536, 8], P('shard')
- gains_master: float32 [2, 1536], P(None, 'shard')
- feedback_rms: float32 [28], replicated
The draws below stay inside these ranges and needn't reach their ends.
Inputs may be any that keep to these rules, and one draw needn't show every extreme that they name: `seg_ids`: each row holds one tree's 13 segments in order, never falling: 0 the trunk, 1 to 4 branches, 5 to 12 leaves. `parents`: a tree's row: -1 for the trunk, 0 for the branches, each branch parent of two leaves. `positions`: a tree's offset plus the number of tokens before a token on its path.
All inputs are finite; a program needn't handle non-finite values.
Results may differ from the reference program's by a relative error of at most 0.023.
The reference program's roundings to bfloat16 on the way count: a program that leaves them out, or rounds other values in their place, can miss the bound.
Values may be sent and summed in bfloat16 or wider, within the bound.
A program may use at most 448 MiB of HBM per device.

```python
import math
import jax
import jax.numpy as jnp
from jax import lax

D = 1536
HQ = 12
HK = 2
HD = 128
F = 768
E = 8
TOPK = 4
RANK = 8
SEGS = 13
TOK_DEV = 512
QW = 1536
KVW = 256
REPLICAS = 8
SHARDS = 4
TREES = 32
TOKENS = 16384


def rising(count, growth):
    return jnp.sqrt(1.0 + growth * jnp.arange(count, dtype=jnp.float32) / max(count - 1, 1))


def feedback_field(base_draw, row_dim, growth):
    extent = base_draw.shape
    lead_shape = (extent[0],) + (1,) * (len(extent) - 1)
    row_shape = tuple((extent[dim_index] if dim_index == row_dim else 1 for dim_index in range(len(extent))))
    return base_draw * rising(extent[0], growth).reshape(lead_shape) * rising(extent[row_dim], growth).reshape(row_shape) * math.sqrt(TOK_DEV * SHARDS)


def tree_layout(key):
    subkeys = jax.random.split(key, 3)
    trunk_weight = jax.random.randint(subkeys[0], (TREES, 1), 4, 13, dtype=jnp.int32)
    other_weight = jax.random.randint(subkeys[1], (TREES, SEGS - 1), 1, 5, dtype=jnp.int32)
    weights = jnp.concatenate([trunk_weight, other_weight], axis=1)
    seg_index = jnp.arange(SEGS, dtype=jnp.int32)
    base_length = jnp.where(seg_index == 0, TOK_DEV // 8, TOK_DEV // 32).astype(jnp.int32)
    spare_tokens = TOK_DEV - TOK_DEV // 8 - (SEGS - 1) * (TOK_DEV // 32)
    extra_tokens = spare_tokens * weights // jnp.sum(weights, axis=1, keepdims=True)
    extra_tokens = extra_tokens + jnp.where(seg_index[None, :] == 0, spare_tokens - jnp.sum(extra_tokens, axis=1, keepdims=True), 0)
    lengths = base_length[None, :] + extra_tokens
    starts = jnp.cumsum(lengths, axis=1) - lengths
    token_order = jnp.arange(TOK_DEV, dtype=jnp.int32)
    segment = jnp.sum((token_order[None, :, None] >= starts[:, None, 1:]).astype(jnp.int32), axis=2)
    leaves = SEGS - 5
    scores = jax.random.randint(subkeys[2], (TREES, leaves), 0, 1 << 20, dtype=jnp.int32) * leaves + jnp.arange(leaves, dtype=jnp.int32)[None, :]
    shuffle = jnp.argsort(scores, axis=1, stable=True).astype(jnp.int32)
    parent = jnp.concatenate([jnp.full((TREES, 1), -1, jnp.int32), jnp.zeros((TREES, 4), jnp.int32), 1 + shuffle // 2], axis=1)
    parent_length = jnp.sum(jnp.where(parent[:, :, None] == seg_index[None, None, :], lengths[:, None, :], 0), axis=2)
    depth_before = jnp.where(seg_index[None, :] >= 1, lengths[:, :1], 0) + jnp.where(seg_index[None, :] >= 5, parent_length, 0)
    onehot = segment[:, :, None] == seg_index[None, None, :]
    seg_start = jnp.sum(jnp.where(onehot, starts[:, None, :], 0), axis=2)
    seg_depth = jnp.sum(jnp.where(onehot, depth_before[:, None, :], 0), axis=2)
    depth_index = seg_depth + token_order[None, :] - seg_start
    return (segment.astype(jnp.int32), parent, depth_index.astype(jnp.int32))


def draw_seg_ids(key, part):
    segment, parent, depth_index = tree_layout(key)
    key = jax.random.fold_in(key, 21)
    return segment


def draw_parents(key, part):
    segment, parent, depth_index = tree_layout(key)
    key = jax.random.fold_in(key, 22)
    return parent


def draw_positions(key, part):
    segment, parent, depth_index = tree_layout(key)
    key = jax.random.fold_in(key, 23)
    deepest = jnp.max(depth_index, axis=1, keepdims=True)
    limit = 2 * TOK_DEV - 1 - deepest
    raw = jax.random.randint(key, (TREES, 1), 0, TOK_DEV, dtype=jnp.int32)
    tree_order = jnp.arange(TREES, dtype=jnp.int32)[:, None]
    raw = jnp.where(tree_order == 0, 0, jnp.where(tree_order == 1, TOK_DEV - 1, raw))
    offset = raw * limit // (TOK_DEV - 1)
    return (offset + depth_index).astype(jnp.int32)


def draw_cotangent(key, part):
    key = jax.random.fold_in(key, 3)
    extent = (REPLICAS, SHARDS * TOK_DEV, D)
    base_draw = jax.random.normal(key, extent, jnp.float32)
    growth = 2.0
    return (base_draw * rising(REPLICAS, growth)[:, None, None]).reshape(TOKENS, D).astype(jnp.bfloat16)


def draw_norm_gains(key, part):
    key = jax.random.fold_in(key, 5)
    jitter = jax.random.uniform(key, (2, D), jnp.float32, 0.85, 1.15)
    growth = 2.0
    return jitter * rising(D, growth)[None, :]


def draw_query_error(key, part):
    key = jax.random.fold_in(key, 11)
    extent = (REPLICAS, D, QW)
    return feedback_field(jax.random.normal(key, extent, jnp.float32), 1, 2.0)


def draw_pair_error(key, part):
    key = jax.random.fold_in(key, 12)
    extent = (REPLICAS, 2, D, KVW)
    return feedback_field(jax.random.normal(key, extent, jnp.float32), 2, 2.0)


def draw_output_error(key, part):
    key = jax.random.fold_in(key, 13)
    extent = (REPLICAS, QW, D)
    return feedback_field(jax.random.normal(key, extent, jnp.float32), 1, 2.0)


def draw_inner_error(key, part):
    key = jax.random.fold_in(key, 14)
    extent = (REPLICAS, 2, E, D, F)
    return feedback_field(jax.random.normal(key, extent, jnp.float32), 3, 2.0)


def draw_outer_error(key, part):
    key = jax.random.fold_in(key, 15)
    extent = (REPLICAS, E, F, D)
    return feedback_field(jax.random.normal(key, extent, jnp.float32), 2, 2.0)


def level_of(rng, shape, shards, low, high):
    factor_of, own = 1.0, jax.random.fold_in(rng, 6)
    for dim, shards_of in shards:
        steps = jnp.exp(jax.random.uniform(jax.random.fold_in(own, dim), (shards_of,), jnp.float32, low / len(shards), high / len(shards)))
        factor_of = factor_of * jnp.repeat(steps, shape[dim] // shards_of).reshape([-1 if axis == dim else 1 for axis in range(len(shape))])
    return factor_of


def distinct(stream_key, rows, number_of, top, lift):
    ranking = jax.random.permutation(jax.random.fold_in(stream_key, 1), number_of)
    boost = ranking
    for power in range(3):
        boost = boost * boost // number_of
    boost = boost * lift // number_of
    tickets = jax.random.randint(jax.random.fold_in(stream_key, 2), (rows, number_of), 0, 4096) + boost
    fixed_rows = jax.random.permutation(jax.random.fold_in(stream_key, 3), rows)[jnp.arange(number_of) % rows]
    tickets = jnp.where(jnp.arange(rows)[:, None] == fixed_rows[None, :], 1 << 14, tickets)
    merit = tickets * number_of + jnp.arange(number_of)
    return lax.top_k(merit.astype(jnp.int32), top)[1].astype(jnp.int32)


def gaussian(rng, shape, deviation, most, cuts=(), kind=jnp.bfloat16):
    drawn = deviation * jax.random.normal(rng, shape, jnp.float32)
    if cuts:
        drawn = drawn * level_of(rng, shape, cuts, -0.22, 0.18)
    return jnp.clip(drawn, -most, most).astype(kind)


def setup_inputs(seed: int = 0) -> dict:
    seeds = jax.random.split(jax.random.key(seed), 31)
    return {
        "tokens": gaussian(seeds[0], (TOKENS, D), 1.0, 6.0, ((0, 32),)),
        "cotangent": draw_cotangent(jax.random.fold_in(seeds[30], 71), 0),
        "seg_ids": draw_seg_ids(jax.random.fold_in(seeds[30], 71), 0),
        "parents": draw_parents(jax.random.fold_in(seeds[30], 71), 0),
        "positions": draw_positions(jax.random.fold_in(seeds[30], 71), 0),
        "routes": distinct(seeds[5], TOKENS, E, TOPK, 0),
        "query_weight": gaussian(seeds[6], (D, QW), D ** -0.5, 0.15625, ((0, 4), (1, 8)), jnp.float32),
        "pair_weight": gaussian(seeds[7], (2, D, KVW), D ** -0.5, 0.15625, ((1, 4), (2, 8)), jnp.float32),
        "output_weight": gaussian(seeds[8], (QW, D), (QW * 4 // TOK_DEV + 1) ** -0.5, 1.75, ((0, 4), (1, 8)), jnp.float32),
        "inner_weight": gaussian(seeds[9], (2, E, D, F), D ** -0.5, 0.15625, ((2, 4), (3, 8)), jnp.float32),
        "outer_weight": gaussian(seeds[10], (E, F, D), (F // 2) ** -0.5, 0.3125, ((1, 4), (2, 8)), jnp.float32),
        "router_weight": gaussian(seeds[11], (D, E), (8 * D) ** -0.5, 0.0546875, ((0, 4),), jnp.float32),
        "norm_gains": draw_norm_gains(jax.random.fold_in(seeds[30], 71), 0),
        "query_moment": gaussian(seeds[13], (D, QW), 0.12, 0.75, ((0, 4), (1, 8)), jnp.float32),
        "pair_moment": gaussian(seeds[14], (2, D, KVW), 0.12, 0.75, ((1, 4), (2, 8)), jnp.float32),
        "output_moment": gaussian(seeds[15], (QW, D), 0.12, 0.75, ((0, 4), (1, 8)), jnp.float32),
        "inner_moment": gaussian(seeds[16], (2, E, D, F), 0.12, 0.75, ((2, 4), (3, 8)), jnp.float32),
        "outer_moment": gaussian(seeds[17], (E, F, D), 0.12, 0.75, ((1, 4), (2, 8)), jnp.float32),
        "router_moment": gaussian(seeds[18], (D, E), 0.12, 0.75, ((0, 4),), jnp.float32),
        "gains_moment": gaussian(seeds[19], (2, D), 0.12, 0.75, ((1, 4),), jnp.float32),
        "query_error": draw_query_error(jax.random.fold_in(seeds[30], 71), 0),
        "pair_error": draw_pair_error(jax.random.fold_in(seeds[30], 71), 0),
        "output_error": draw_output_error(jax.random.fold_in(seeds[30], 71), 0),
        "inner_error": draw_inner_error(jax.random.fold_in(seeds[30], 71), 0),
        "outer_error": draw_outer_error(jax.random.fold_in(seeds[30], 71), 0),
        "query_start": gaussian(seeds[25], (QW, RANK), 1.0, 6.0, (), jnp.float32),
        "pair_start": gaussian(seeds[26], (2, KVW, RANK), 1.0, 6.0, (), jnp.float32),
        "output_start": gaussian(seeds[27], (D, RANK), 1.0, 6.0, (), jnp.float32),
        "inner_start": gaussian(seeds[28], (2, E, F, RANK), 1.0, 6.0, (), jnp.float32),
        "outer_start": gaussian(seeds[29], (E, D, RANK), 1.0, 6.0, (), jnp.float32),
    }


@jax.custom_vjp
def low(v):
    return lax.optimization_barrier(v.astype(jnp.bfloat16)).astype(jnp.float32)

@jax.custom_vjp
def low_back(v):
    return v

def low_keep(v):
    return (low(v), None)

def low_pass(kept, grad):
    return (grad,)

def back_keep(v):
    return (v, None)

def back_low(kept, grad):
    return (low(grad),)
low.defvjp(low_keep, low_pass)
low_back.defvjp(back_keep, back_low)
EPSILON = 1e-05
ROPE_BASE = 1000000.0
MOMENTUM_DECAY = 0.9
WEIGHT_DECAY = 0.01
STEP_RATE = 4.0
GAIN_RATE = 3.0
HIGHEST = lax.Precision.HIGHEST

def rms_norm(hidden, gain_row):
    return hidden * lax.rsqrt(lax.optimization_barrier(jnp.mean(hidden * hidden, axis=-1, keepdims=True)) + EPSILON) * gain_row

def rotate(heads_in, position, handed):
    half_size = heads_in.shape[-1] // 2
    frequency = ROPE_BASE ** (-2.0 * jnp.arange(half_size, dtype=jnp.float32) / heads_in.shape[-1])
    angles = position.astype(jnp.float32)[:, None] * frequency[None, :]
    cosine = jnp.cos(angles)[:, None, :]
    sine_part = handed * jnp.sin(angles)[:, None, :]
    former = heads_in[..., :half_size]
    latter = heads_in[..., half_size:]
    return jnp.concatenate([former * cosine - latter * sine_part, latter * cosine + former * sine_part], axis=-1)

def path_mask(segment, parent_row):
    table_ids = jnp.arange(parent_row.shape[0], dtype=jnp.int32)
    parent_one = lax.optimization_barrier(jnp.sum(jnp.where(segment[:, None] == table_ids[None, :], parent_row[None, :], 0), axis=1))
    parent_two = jnp.where(parent_one >= 0, lax.optimization_barrier(jnp.sum(jnp.where(parent_one[:, None] == table_ids[None, :], parent_row[None, :], 0), axis=1)), -1)
    token_order = jnp.arange(segment.shape[0], dtype=jnp.int32)
    same_path = (segment[:, None] == segment[None, :]) & (token_order[None, :] <= token_order[:, None])
    return same_path | (segment[None, :] == parent_one[:, None]) | (segment[None, :] == parent_two[:, None])

def attend(query_rot, key_rot, values, allowed):
    length = query_rot.shape[0]
    block_rows = min(512, length)
    query_blocks = query_rot.reshape(length // block_rows, block_rows, HK, HQ // HK, HD)
    mask_blocks = allowed.reshape(length // block_rows, block_rows, length)

    def one_block(block_pair):
        query_block, mask_block = block_pair
        raw = low_back(jnp.einsum('qkgd,tkd->kgqt', query_block, key_rot, precision=HIGHEST) * HD ** (-0.5))
        masked = jnp.where(mask_block[None, None], raw, -1e+30)
        top_score = lax.optimization_barrier(jnp.max(masked, axis=-1, keepdims=True))
        raised = jnp.exp(masked - top_score)
        attention = raised / lax.optimization_barrier(jnp.sum(raised, axis=-1, keepdims=True))
        mixed_block = jnp.einsum('kgqt,tkd->qkgd', low(attention), values, precision=HIGHEST)
        return mixed_block.reshape(block_rows, HQ * HD)
    return lax.map(jax.checkpoint(one_block), (query_blocks, mask_blocks)).reshape(length, HQ * HD)

def forward_layer(hidden, weights, allowed, position, route_mask):
    query_weight, pair_weight, output_weight, inner_weight, outer_weight, router_weight, gain_rows = weights
    length = hidden.shape[0]
    first = low(rms_norm(hidden, gain_rows[0]))
    query_pre = low_back(jnp.dot(first, query_weight, precision=HIGHEST))
    pair_pre = low_back(jnp.einsum('td,adw->atw', first, pair_weight, precision=HIGHEST))
    query_rot = low(rotate(query_pre.reshape(length, HQ, HD), position, 1.0))
    key_rot = low(rotate(pair_pre[0].reshape(length, HK, HD), position, 1.0))
    values = low(pair_pre[1].reshape(length, HK, HD))
    mixed = low_back(low(attend(query_rot, key_rot, values, allowed)))
    middle = hidden + low_back(jnp.dot(mixed, output_weight, precision=HIGHEST))
    second = low(rms_norm(middle, gain_rows[1]))
    logits = low_back(jnp.dot(second, router_weight, precision=HIGHEST))
    route_top = lax.optimization_barrier(jnp.max(jnp.where(route_mask, logits, -1e+30), axis=-1, keepdims=True))
    raised = jnp.where(route_mask, jnp.exp(logits - route_top), 0.0)
    shares = raised / lax.optimization_barrier(jnp.sum(raised, axis=-1, keepdims=True))
    gate_up = low_back(jnp.einsum('td,aedf->aetf', second, inner_weight, precision=HIGHEST))
    activated = low(jax.nn.gelu(gate_up[0]) * gate_up[1])
    expert_out = low_back(jnp.einsum('etf,efd->etd', activated, outer_weight, precision=HIGHEST))
    return middle + jnp.einsum('te,etd->td', shares, expert_out, precision=HIGHEST)

def compress(group_sum, error, start):
    merged = group_sum + error
    left_sum = jnp.einsum('r...mn,...nk->...mk', merged, start, precision=HIGHEST)
    gram_matrix = jnp.einsum('...mk,...ml->...kl', left_sum, left_sum, precision=HIGHEST)
    lower_factor = jnp.linalg.cholesky(gram_matrix)
    solved = jax.scipy.linalg.solve_triangular(lower_factor, jnp.swapaxes(left_sum, -1, -2), lower=True)
    basis_rows = jnp.swapaxes(solved, -1, -2)
    right_factor = jnp.einsum('r...mn,...mk->...nk', merged, basis_rows, precision=HIGHEST)
    approx = jnp.einsum('...mk,...nk->...mn', basis_rows, right_factor, precision=HIGHEST)
    feedback = merged - approx[None] / REPLICAS
    entries = merged.shape[-2] * merged.shape[-1]
    scale_norm = jnp.sqrt(lax.optimization_barrier(jnp.sum(right_factor * right_factor, axis=(-2, -1), keepdims=True)) / entries + 1e-06)
    squares = lax.optimization_barrier(jnp.sum(feedback * feedback, axis=(0, -2, -1)))
    spread = jnp.sqrt(squares / (REPLICAS * entries))
    return (basis_rows, right_factor, feedback, approx / scale_norm, spread)

def advance(weight_now, moment_now, direction, step_rate, decay_rate):
    moment_new = MOMENTUM_DECAY * moment_now + (1.0 - MOMENTUM_DECAY) * direction
    return (weight_now - step_rate * (moment_new + decay_rate * weight_now), moment_new)

def reference(tokens, cotangent, seg_ids, parents, positions, routes, query_weight, pair_weight, output_weight, inner_weight, outer_weight, router_weight, norm_gains, query_moment, pair_moment, output_moment, inner_moment, outer_moment, router_moment, gains_moment, query_error, pair_error, output_error, inner_error, outer_error, query_start, pair_start, output_start, inner_start, outer_start):
    masters = (query_weight, pair_weight, output_weight, inner_weight, outer_weight, router_weight, norm_gains)
    params = tuple((low(master) for master in masters))
    token_rows = tokens.reshape(REPLICAS, SHARDS, TOK_DEV, D)
    upstream_rows = cotangent.reshape(REPLICAS, SHARDS, TOK_DEV, D)
    segment_rows = seg_ids.reshape(REPLICAS, SHARDS, TOK_DEV)
    parent_rows = parents.reshape(REPLICAS, SHARDS, SEGS)
    position_rows = positions.reshape(REPLICAS, SHARDS, TOK_DEV)
    route_rows = routes.reshape(REPLICAS, SHARDS, TOK_DEV, TOPK)
    expert_ids = jnp.arange(E, dtype=jnp.int32)

    def one_tree(running, tree_item):
        tree_tokens, tree_upstream, tree_segment, tree_parent, tree_position, tree_route = tree_item
        allowed = path_mask(tree_segment, tree_parent)
        route_mask = jnp.any(tree_route[:, :, None] == expert_ids[None, None, :], axis=1)

        def apply_layer(hidden, *weights):
            return forward_layer(hidden, weights, allowed, tree_position, route_mask)
        result, pull_back = jax.vjp(apply_layer, tree_tokens.astype(jnp.float32), *params)
        gradients = pull_back(tree_upstream.astype(jnp.float32))
        summed = tuple((before + after for before, after in zip(running, gradients[1:])))
        return (summed, (result.astype(jnp.bfloat16), gradients[0].astype(jnp.bfloat16)))

    def one_group(running, group_item):
        zeroes = tuple((jnp.zeros_like(weight) for weight in params))
        group_sum, tree_outputs = lax.scan(one_tree, zeroes, group_item)
        return (running, (group_sum, tree_outputs[0], tree_outputs[1]))
    _, (group_sums, outputs, input_backs) = lax.scan(one_group, jnp.zeros((), jnp.float32), (token_rows, upstream_rows, segment_rows, parent_rows, position_rows, route_rows))
    errors = (query_error, pair_error, output_error, inner_error, outer_error)
    starts = (query_start, pair_start, output_start, inner_start, outer_start)
    moments = (query_moment, pair_moment, output_moment, inner_moment, outer_moment)
    step_rates = (STEP_RATE * D ** (-0.5), STEP_RATE * D ** (-0.5), STEP_RATE * (QW * 4 // TOK_DEV + 1) ** (-0.5), STEP_RATE * D ** (-0.5), STEP_RATE * (F // 2) ** (-0.5))
    lefts = []
    rights = []
    feedbacks = []
    momenta = []
    new_masters = []
    spreads = []
    for matrix_index in range(5):
        basis_rows, right_factor, feedback, direction, spread = compress(group_sums[matrix_index], errors[matrix_index], starts[matrix_index])
        new_master, new_moment = advance(masters[matrix_index], moments[matrix_index], direction, step_rates[matrix_index], WEIGHT_DECAY)
        lefts.append(basis_rows)
        rights.append(right_factor)
        feedbacks.append(feedback)
        momenta.append(new_moment)
        new_masters.append(new_master)
        spreads.append(spread.reshape(-1))
    router_total = lax.optimization_barrier(jnp.sum(group_sums[5], axis=0))
    gains_total = lax.optimization_barrier(jnp.sum(group_sums[6], axis=0))
    router_direction = router_total / jnp.sqrt(jnp.mean(router_total * router_total) + 1e-06)
    gains_direction = gains_total / jnp.sqrt(lax.optimization_barrier(jnp.mean(gains_total * gains_total, axis=1, keepdims=True)) + 1e-06)
    router_master, router_momentum = advance(router_weight, router_moment, router_direction, STEP_RATE * (8 * D) ** (-0.5), WEIGHT_DECAY)
    gains_master, gains_momentum = advance(norm_gains, gains_moment, gains_direction, GAIN_RATE, 0.0)
    feedback_rms = jnp.concatenate(spreads)
    return (outputs.reshape(TOKENS, D), input_backs.reshape(TOKENS, D), lefts[0], lefts[1], lefts[2], lefts[3], lefts[4], rights[0], rights[1], rights[2], rights[3], rights[4], feedbacks[0], feedbacks[1], feedbacks[2], feedbacks[3], feedbacks[4], momenta[0], momenta[1], momenta[2], momenta[3], momenta[4], router_momentum, gains_momentum, new_masters[0], new_masters[1], new_masters[2], new_masters[3], new_masters[4], router_master, gains_master, feedback_rms)
```

```python
import functools

import jax
import jax.numpy as jnp
from jax import lax
from jax.experimental import pallas as pl
from jax.experimental.pallas import tpu as pltpu
from jax.sharding import PartitionSpec as P

D = 1536
HQ = 12
HK = 2
HD = 128
F = 768
E = 8
TOK_DEV = 512
QW = 1536


EPSILON = 1e-05
ROPE_BASE = 1000000.0
MOMENTUM_DECAY = 0.9
WEIGHT_DECAY = 0.01
STEP_RATE = 4.0
GAIN_RATE = 3.0
HIGHEST = lax.Precision.HIGHEST


def rms_norm(hidden, gain_row):
    return (
        hidden * lax.rsqrt(jnp.mean(hidden * hidden, axis=-1, keepdims=True) + EPSILON) * gain_row
    )


def rotate(heads_in, position, handed):
    half_size = heads_in.shape[-1] // 2
    frequency = ROPE_BASE ** (-2.0 * jnp.arange(half_size, dtype=jnp.float32) / heads_in.shape[-1])
    angles = position.astype(jnp.float32)[:, None] * frequency[None, :]
    cosine = jnp.cos(angles)[:, None, :]
    sine_part = handed * jnp.sin(angles)[:, None, :]
    former = heads_in[..., :half_size]
    latter = heads_in[..., half_size:]
    return jnp.concatenate(
        [former * cosine - latter * sine_part, latter * cosine + former * sine_part], axis=-1
    )


def path_mask(segment, parent_row):
    table_ids = jnp.arange(parent_row.shape[0], dtype=jnp.int32)
    parent_one = jnp.sum(
        jnp.where(segment[:, None] == table_ids[None, :], parent_row[None, :], 0), axis=1
    )
    parent_two = jnp.where(
        parent_one >= 0,
        jnp.sum(
            jnp.where(parent_one[:, None] == table_ids[None, :], parent_row[None, :], 0), axis=1
        ),
        -1,
    )
    token_order = jnp.arange(segment.shape[0], dtype=jnp.int32)
    same_path = (segment[:, None] == segment[None, :]) & (
        token_order[None, :] <= token_order[:, None]
    )
    return (
        same_path
        | (segment[None, :] == parent_one[:, None])
        | (segment[None, :] == parent_two[:, None])
    )


def scores_of(query_block, key_rot, mask_block):
    rows_here = query_block.shape[0]
    key_heads = key_rot.shape[1]
    shaped = query_block.reshape(
        rows_here, key_heads, query_block.shape[1] // key_heads, query_block.shape[2]
    )
    raw = jnp.einsum(
        "qkgd,tkd->kgqt", shaped, key_rot, preferred_element_type=jnp.float32
    ) * query_block.shape[2] ** (-0.5)
    return (jnp.where(mask_block[None, None], raw, -1e30), shaped)


def advance(weight_now, moment_now, direction, step_rate, decay_rate):
    moment_new = MOMENTUM_DECAY * moment_now + (1.0 - MOMENTUM_DECAY) * direction
    return (weight_now - step_rate * (moment_new + decay_rate * weight_now), moment_new)


CHUNKS = 4
GELU_C = 0.7978845608028654
GELU_A = 0.044715
MESH = pl.DeviceIdType.MESH
VMEM_LIMIT = 60 * 1024 * 1024
F32 = jnp.float32
BF16 = jnp.bfloat16


def z_ring(block):
    size = lax.axis_size("shard")
    here = lax.axis_index("shard")
    up = down = block
    ups, downs = [block], [block]
    for _ in range(size - 1):
        up = lax.ppermute(up, "shard", [(i, i + 1) for i in range(size - 1)])
        down = lax.ppermute(down, "shard", [(i + 1, i) for i in range(size - 1)])
        ups.append(up)
        downs.append(down)
    return here, ups, downs


def z_gather(block):
    here, ups, downs = z_ring(block)
    size = len(ups)
    parts = []
    for k in range(size):
        part = ups[0]
        for other in range(size):
            if other > k:
                part = jnp.where(here == other, ups[other - k], part)
            elif other < k:
                part = jnp.where(here == other, downs[k - other], part)
        parts.append(part)
    return jnp.stack(parts)


def z_slots(block):
    here, ups, downs = z_ring(block)
    size = len(ups)
    return jnp.stack([block] + [jnp.where(here >= j, ups[j], downs[size - j]) for j in range(1, size)])


def nn(a, b, precision=None):
    return jnp.dot(a, b, preferred_element_type=F32, precision=precision)


def nt(a, b, precision=None):
    return lax.dot_general(
        a, b, (((1,), (1,)), ((), ())), preferred_element_type=F32, precision=precision
    )


def tn(a, b):
    return lax.dot_general(a, b, (((0,), (0,)), ((), ())), preferred_element_type=F32)


def up_to(count, unit):
    return -(-count // unit) * unit


def two_terms(value):
    high = value.astype(BF16)
    return high, (value - high.astype(F32)).astype(BF16)


def three_terms(value):
    high = value.astype(BF16)
    rest = value - high.astype(F32)
    middle = rest.astype(BF16)
    low = (rest - middle.astype(F32)).astype(BF16)
    return jnp.concatenate([high.astype(F32), middle.astype(F32), low.astype(F32)], axis=0).astype(BF16)


def folded(value, rows=8):
    return value[:rows] + value[rows : 2 * rows] + value[2 * rows : 3 * rows]


def exact_nn(value, other):
    return folded(nn(three_terms(value), other))


def exact_nt(value, other):
    return folded(nt(three_terms(value), other))


def padded(value, width):
    if value.shape[1] == width:
        return value
    return jnp.concatenate(
        [value, jnp.zeros((value.shape[0], width - value.shape[1]), value.dtype)], axis=1
    )


def params(**more):
    return pltpu.CompilerParams(vmem_limit_bytes=VMEM_LIMIT, **more)


def vmem_specs(count):
    return [pl.BlockSpec(memory_space=pltpu.VMEM)] * count


def struct(shape, dtype=F32):
    return jax.ShapeDtypeStruct(shape, dtype)


def expert_kernel(
    first_expert,
    aliased,
    x_ref,
    u_ref,
    up_ref,
    w1_ref,
    w2_ref,
    err_in_ref,
    err_out_ref,
    start_in_ref,
    start_out_ref,
    *rest,
):
    if aliased:
        rest = rest[2:]
    min_ref, mout_ref, y_ref, sg_ref, cg_ref, lin_ref, lout_ref, gt_ref, act_ref, br_ref = rest
    expert = first_expert + pl.program_id(0)
    tree = pl.program_id(1)
    width = up_ref.shape[1]
    groups, lanes, _, double, span1 = w1_ref.shape
    f_cols = double // 2
    hidden = groups * f_cols
    lanes2, _, groups2, _, f_rows, span2 = w2_ref.shape
    rows = min_ref.shape[2]
    out_rows = mout_ref.shape[1]
    here = lax.axis_index("shard")

    def first_weight(a, low, high):
        parts = [
            w1_ref[low:high, k, 0, a * f_cols : (a + 1) * f_cols, :].reshape(
                (high - low) * f_cols, span1
            )
            for k in range(lanes)
        ]
        return parts[0] if lanes == 1 else jnp.concatenate(parts, axis=1)

    def second_weight(low, high):
        parts = [
            w2_ref[k, 0, low:high, 0, :, :].reshape((high - low) * f_rows, span2)
            for k in range(lanes2)
        ]
        return parts[0] if lanes2 == 1 else jnp.concatenate(parts, axis=1)

    x = x_ref[0, :width, :]
    tail = x_ref[0, width:, :].astype(F32)
    shares8 = tail[:E] + tail[E:]
    picked = lax.broadcasted_iota(jnp.int32, shares8.shape, 0) == expert
    share = jnp.sum(jnp.where(picked, shares8, 0.0), axis=0, keepdims=True)
    br_ref[...] = (share * u_ref[0].astype(F32)).astype(BF16)
    halves = 2 if groups % 2 == 0 and groups2 % 2 == 0 else 1
    half = hidden // halves
    for part in range(halves):
        span = slice(part * half, (part + 1) * half)
        g_low, g_high = part * groups // halves, (part + 1) * groups // halves
        h_low, h_high = part * groups2 // halves, (part + 1) * groups2 // halves
        gate = nn(first_weight(0, g_low, g_high), x)
        up = nn(first_weight(1, g_low, g_high), x)
        act_grad = nn(second_weight(h_low, h_high), br_ref[...])
        square = gate * gate
        bent = jnp.tanh(GELU_C * (gate + GELU_A * (square * gate)))
        lifted = 0.5 * (1.0 + bent)
        gelu = gate * lifted
        slope = lifted + 0.5 * gate * (1.0 - bent * bent) * (
            GELU_C * (1.0 + 3.0 * GELU_A * square)
        )
        act_ref[span, :] = (gelu * up).astype(BF16)
        gt_ref[span, :] = (act_grad * up * slope).astype(BF16)
        gt_ref[hidden + part * half : hidden + (part + 1) * half, :] = (act_grad * gelu).astype(
            BF16
        )

    @pl.when(tree == 0)
    def _():
        min_ref[...] = err_in_ref[...]
        mout_ref[...] = err_out_ref[...]

    own_x = x_ref[0, pl.ds(pl.multiple_of(here * rows, 16), rows), :]
    min_ref[0, 0] += nt(own_x, gt_ref[:hidden, :])
    min_ref[1, 0] += nt(own_x, gt_ref[hidden:, :])
    own_act = act_ref[pl.ds(pl.multiple_of(here * out_rows, 16), out_rows), :]
    mout_ref[0] += nt(own_act, br_ref[...])

    @pl.when(tree == 0)
    def _():
        expert_out = tn(act_ref[...], second_weight(0, groups2))
        cg_ref[0] = jnp.sum(up_ref[...].astype(F32) * expert_out, axis=1, keepdims=True)
        share_col = jnp.transpose(jnp.broadcast_to(share, (8, share.shape[1])))[:, :1]
        added = share_col * expert_out
        grown = tn(gt_ref[:hidden, :], first_weight(0, 0, groups)) + tn(
            gt_ref[hidden:, :], first_weight(1, 0, groups)
        )
        first = pl.program_id(0) == 0
        y_ref[...] = jnp.where(first, added, y_ref[...] + added)
        sg_ref[...] = jnp.where(first, grown, sg_ref[...] + grown)

    @pl.when(tree == pl.num_programs(1) - 1)
    def _():
        lin_ref[...] = jnp.zeros_like(lin_ref)
        lout_ref[...] = jnp.zeros_like(lout_ref)
        for a in range(2):
            lin_ref[0, a, :, :rows] = nt(start_in_ref[a, 0], min_ref[a, 0], HIGHEST)
        lout_ref[0, :, :out_rows] = nt(start_out_ref[0], mout_ref[0], HIGHEST)


def expert_chunk(
    first_expert, x4, u4, upstream, w1, w2, err_in, err_out, start_in, start_out, merged
):
    count = w2.shape[1]
    hidden = err_in.shape[3]
    trees, width, length = u4.shape
    rows, out_rows = err_in.shape[2], err_out.shape[1]
    last_block = w2.shape[3] - 1
    one = pl.Buffered(1)

    def spec(block, index, **more):
        return pl.BlockSpec(block, index, **more)

    in_specs = [
        spec((1, x4.shape[1], length), lambda e, t: (t, 0, 0)),
        spec((1, width, length), lambda e, t: (t, 0, 0)),
        spec((length, width), lambda e, t: (0, 0), pipeline_mode=one),
        spec((*w1.shape[:2], 1, *w1.shape[3:]), lambda e, t: (0, 0, e, 0, 0)),
        spec(
            (w2.shape[0], 1, w2.shape[2], 1, *w2.shape[4:]),
            lambda e, t: (0, e, 0, last_block, 0, 0),
        ),
        spec((2, 1, rows, hidden), lambda e, t: (0, first_expert + e, 0, 0)),
        spec((1, out_rows, width), lambda e, t: (first_expert + e, 0, 0)),
        spec((2, 1, 8, hidden), lambda e, t: (0, first_expert + e, 0, 0)),
        spec((1, 8, width), lambda e, t: (first_expert + e, 0, 0)),
    ]
    operands = [x4, u4, upstream, w1, w2, err_in, err_out, start_in, start_out]
    aliases = {}
    if merged is not None:
        in_specs += [pl.BlockSpec(memory_space=pl.ANY)] * 2
        aliases = {len(operands): 0, len(operands) + 1: 1}
        operands += list(merged)
    wide, wide_out = up_to(rows, 128), up_to(out_rows, 128)
    out_specs = [
        spec((2, 1, rows, hidden), lambda e, t: (0, first_expert + e, 0, 0)),
        spec((1, out_rows, width), lambda e, t: (first_expert + e, 0, 0)),
        spec((length, width), lambda e, t: (0, 0), pipeline_mode=one),
        spec((length, width), lambda e, t: (0, 0), pipeline_mode=one),
        spec((1, length, 1), lambda e, t: (e, 0, 0)),
        spec((1, 2, 8, wide), lambda e, t: (e, 0, 0, 0)),
        spec((1, 8, wide_out), lambda e, t: (e, 0, 0)),
    ]
    out_shape = [
        struct(err_in.shape),
        struct(err_out.shape),
        struct((length, width)),
        struct((length, width)),
        struct((count, length, 1)),
        struct((count, 2, 8, wide)),
        struct((count, 8, wide_out)),
    ]
    flops = 2 * count * hidden * width * length * (3 * trees + 3) + 2 * count * trees * length * (
        2 * rows * hidden + out_rows * width
    )
    return pl.pallas_call(
        functools.partial(expert_kernel, first_expert, merged is not None),
        grid=(count, trees),
        in_specs=in_specs,
        out_specs=out_specs,
        out_shape=out_shape,
        scratch_shapes=[
            pltpu.VMEM((2 * hidden, length), BF16),
            pltpu.VMEM((hidden, length), BF16),
            pltpu.VMEM((width, length), BF16),
        ],
        input_output_aliases=aliases,
        cost_estimate=pl.CostEstimate(
            flops=flops,
            bytes_accessed=count * (2 * 3 * hidden * width + 8 * 3 * rows * hidden),
            transcendentals=count * trees * length * hidden,
        ),
        compiler_params=params(),
        name="experts",
    )(*operands)


def left_parts_kernel(
    shards, rows, wide, first_ref, joint_ref, mixed_ref, middle_ref, sq_ref, sk_ref, sv_ref, so_ref,
    eq_ref, ep_ref, eo_ref, router_ref, gains_ref, z_ref, own_ref,
):
    qw, kv = sq_ref.shape[1], sk_ref.shape[1]
    first = first_ref[...]
    pieces = []
    for start_ref, low in ((sq_ref, 0), (sk_ref, qw), (sv_ref, qw + kv)):
        high = low + start_ref.shape[1]
        pieces.append(exact_nn(exact_nt(start_ref[...], joint_ref[:, low:high]), first))
    pieces.append(exact_nn(exact_nt(so_ref[...], middle_ref[...]), mixed_ref[...]))
    pieces.append(router_ref[...])
    pieces.append(gains_ref[...])
    for shard in range(shards):
        for k, piece in enumerate(pieces):
            z_ref[shard, :, k * wide : (k + 1) * wide] = padded(
                piece[:, shard * rows : (shard + 1) * rows], wide
            )
    errors = (
        nt(sq_ref[...], eq_ref[...], HIGHEST),
        nt(sk_ref[...], ep_ref[0], HIGHEST),
        nt(sv_ref[...], ep_ref[1], HIGHEST),
        nt(so_ref[...], eo_ref[...], HIGHEST),
    )
    for k, piece in enumerate(errors):
        own_ref[:, k * wide : (k + 1) * wide] = padded(piece, wide)


def left_parts(shards, rows, operands):
    wide = up_to(rows, 128)
    return pl.pallas_call(
        functools.partial(left_parts_kernel, shards, rows, wide),
        in_specs=vmem_specs(len(operands)),
        out_specs=vmem_specs(2),
        out_shape=[struct((shards, 8, 6 * wide)), struct((8, 4 * wide))],
        compiler_params=params(),
        name="left_parts",
    )(*operands)


def greet(reps, shards):
    rep, shard = lax.axis_index("rep"), lax.axis_index("shard")
    barrier = pltpu.get_barrier_semaphore()
    for step in range(1, shards):
        pl.semaphore_signal(
            barrier, inc=1, device_id={"shard": lax.rem(shard + step, shards)}, device_id_type=MESH
        )
    for step in range(1, reps):
        pl.semaphore_signal(
            barrier, inc=1, device_id={"rep": lax.rem(rep + step, reps)}, device_id_type=MESH
        )
    pl.semaphore_wait(barrier, reps + shards - 2)


def send_all(axis, size, source, target, send, recv):
    here = lax.axis_index(axis)
    copies = []
    for step in range(1, size):
        to = lax.rem(here + step, size)
        copy = pltpu.make_async_remote_copy(
            src_ref=source(to),
            dst_ref=target(step),
            send_sem=send.at[step - 1],
            recv_sem=recv.at[step - 1],
            device_id={axis: to},
            device_id_type=MESH,
        )
        copy.start()
        copies.append(copy)
    for copy in copies:
        copy.wait()


def blocks_on_diagonal(square):
    size = square.shape[0]
    row = lax.broadcasted_iota(jnp.int32, (size, size), 0) // 8
    lane = lax.broadcasted_iota(jnp.int32, (size, size), 1) // 8
    kept = jnp.where(row == lane, square, 0.0)
    total = kept[:8]
    for k in range(1, size // 8):
        total = total + kept[8 * k : 8 * k + 8]
    return total


def spread_on_diagonal(flat):
    size = flat.shape[1]
    tall = jnp.concatenate([flat] * (size // 8), axis=0)
    row = lax.broadcasted_iota(jnp.int32, (size, size), 0) // 8
    lane = lax.broadcasted_iota(jnp.int32, (size, size), 1) // 8
    return jnp.transpose(jnp.where(row == lane, tall, 0.0))


def left_sync_kernel(reps, shards, wide, wide_out, piece, count, *refs):
    z_ref, own_ref = refs[:2]
    lin_refs, lout_refs = refs[2 : 2 + count], refs[2 + count : 2 + 2 * count]
    left_ref, left_out_ref, totals_ref, squares_ref, leftz_ref = refs[2 + 2 * count : 7 + 2 * count]
    (zbuf, parts, heard, total, grams, lanes_z, zs, zr, ps, pr, gs, gr, hs, hr, ls, lr) = refs[
        7 + 2 * count :
    ]
    rep, shard = lax.axis_index("rep"), lax.axis_index("shard")
    greet(reps, shards)
    send_all("shard", shards, lambda to: z_ref.at[to], lambda step: zbuf.at[step - 1], zs, zr)
    front = z_ref[shard]
    for step in range(shards - 1):
        front = front + zbuf[step]
    ins = [ref[e, a] for a in range(2) for ref in lin_refs for e in range(ref.shape[0])]
    outs = [ref[e] for ref in lout_refs for e in range(ref.shape[0])]
    line = jnp.concatenate(
        [front[:, : 4 * wide] + own_ref[...], front[:, 4 * wide :], *ins, *outs], axis=1
    )
    line = padded(line, reps * piece)
    for k in range(reps):
        parts[k] = line[:, k * piece : (k + 1) * piece]
    send_all("rep", reps, lambda to: parts.at[to], lambda step: heard.at[step - 1], ps, pr)
    mine = parts[rep]
    for step in range(reps - 1):
        mine = mine + heard[step]
    total[rep] = mine
    send_all("rep", reps, lambda to: total.at[rep], lambda step: total.at[rep], gs, gr)
    line = jnp.concatenate([total[k] for k in range(reps)], axis=1)
    inner = len(ins)
    matrices = [line[:, k * wide : (k + 1) * wide] for k in range(4)]
    matrices += [line[:, (6 + k) * wide : (7 + k) * wide] for k in range(inner)]
    base = (6 + inner) * wide
    outers = [line[:, base + k * wide_out : base + (k + 1) * wide_out] for k in range(len(outs))]
    router, gains = line[:, 4 * wide : 5 * wide], line[:, 5 * wide : 6 * wide]
    size, size_out = up_to(8 * len(matrices), 128), up_to(8 * len(outers), 128)
    stack = jnp.concatenate(
        matrices + [jnp.zeros((size - 8 * len(matrices), wide), F32)], axis=0
    )
    stack_out = jnp.concatenate(
        outers + [jnp.zeros((size_out - 8 * len(outers), wide_out), F32)], axis=0
    )
    gram = blocks_on_diagonal(nt(stack, stack, HIGHEST))
    gram_out = blocks_on_diagonal(nt(stack_out, stack_out, HIGHEST))
    row = lax.broadcasted_iota(jnp.int32, (8, 128), 0)
    lane = lax.broadcasted_iota(jnp.int32, (8, 128), 1)
    more = jnp.where(lane == 0, jnp.sum(router * router, axis=1, keepdims=True), 0.0)
    more = jnp.where(lane == 1, jnp.sum(gains * gains, axis=1, keepdims=True), more)
    grams[shard] = jnp.concatenate([gram, gram_out, more], axis=1)
    send_all("shard", shards, lambda to: grams.at[shard], lambda step: grams.at[shard], hs, hr)
    gram = grams[0]
    for k in range(1, shards):
        gram = gram + grams[k]
    both = size + size_out
    squares_ref[...] = gram[:, both:]
    totals_ref[0] = router
    totals_ref[1] = gains
    where_from = lax.broadcasted_iota(jnp.int32, (both, 1024), 0)
    where_to = lax.broadcasted_iota(jnp.int32, (both, 1024), 1)
    chosen = jnp.where(
        (where_from % 8 == where_to // 128) & (where_from // 8 == where_to % 128), 1.0, 0.0
    ).astype(BF16)
    lines = exact_nn(gram[:, :both], chosen)
    used = (lane < len(matrices)) | ((lane >= size // 8) & (lane < size // 8 + len(outers)))
    table = [
        jnp.where(used, lines[:, 128 * k : 128 * k + 128], jnp.where(row == k, 1.0, 0.0))
        for k in range(8)
    ]
    inverse = [jnp.where(row == k, 1.0, 0.0) for k in range(8)]
    for k in range(8):
        pivot = table[k][k : k + 1]
        over = 1.0 / pivot
        for i in range(k + 1, 8):
            factor = table[i][k : k + 1] * over
            table[i] = table[i] - factor * table[k]
            inverse[i] = inverse[i] - factor * inverse[k]
        inverse[k] = inverse[k] / jnp.sqrt(pivot)
    flat = exact_nt(jnp.concatenate(inverse, axis=1), chosen)
    lefts = nn(spread_on_diagonal(flat[:, :size]), stack, HIGHEST)
    lefts_out = nn(spread_on_diagonal(flat[:, size:]), stack_out, HIGHEST)
    left_ref[...] = lefts[: left_ref.shape[0]]
    left_out_ref[...] = lefts_out[: left_out_ref.shape[0]]
    lanes_z[shard] = lefts[:32]
    send_all("shard", shards, lambda to: lanes_z.at[shard], lambda step: lanes_z.at[shard], ls, lr)
    leftz_ref[...] = lanes_z[...]


def left_sync(reps, shards, z_part, own, lins, louts):
    wide, wide_out = lins[0].shape[3], louts[0].shape[2]
    inner, outer = 2 * sum(x.shape[0] for x in lins), sum(x.shape[0] for x in louts)
    piece = up_to(-(-((6 + inner) * wide + outer * wide_out) // reps), 128)
    matrices = 4 + inner
    size, size_out = up_to(8 * matrices, 128), up_to(8 * outer, 128)
    dma = pltpu.SemaphoreType.DMA
    operands = [z_part, own, *lins, *louts]
    return pl.pallas_call(
        functools.partial(left_sync_kernel, reps, shards, wide, wide_out, piece, len(lins)),
        in_specs=vmem_specs(len(operands)),
        out_specs=vmem_specs(5),
        out_shape=[
            struct((8 * matrices, wide)),
            struct((8 * outer, wide_out)),
            struct((2, 8, wide)),
            struct((8, 128)),
            struct((shards, 32, wide)),
        ],
        scratch_shapes=[
            pltpu.VMEM((shards - 1, 8, 6 * wide), F32),
            pltpu.VMEM((reps, 8, piece), F32),
            pltpu.VMEM((reps - 1, 8, piece), F32),
            pltpu.VMEM((reps, 8, piece), F32),
            pltpu.VMEM((shards, 8, size + size_out + 128), F32),
            pltpu.VMEM((shards, 32, wide), F32),
            dma((shards - 1,)),
            dma((shards - 1,)),
            dma((reps - 1,)),
            dma((reps - 1,)),
            dma((reps - 1,)),
            dma((reps - 1,)),
            dma((shards - 1,)),
            dma((shards - 1,)),
            dma((shards - 1,)),
            dma((shards - 1,)),
        ],
        compiler_params=params(collective_id=1, has_side_effects=True),
        name="left_sync",
    )(*operands)


def right_expert_kernel(left_ref, left_out_ref, min_ref, mout_ref, right_ref):
    rows, out_rows = min_ref.shape[2], mout_ref.shape[1]
    hidden = min_ref.shape[3]

    def product(left, matrix):
        high, low = two_terms(left)
        both = jnp.concatenate([high.astype(F32), low.astype(F32)], axis=0).astype(BF16)
        top, rest = two_terms(matrix)
        first = nn(both, top)
        return first[:8] + first[8:] + nn(both, rest)[:8]

    for a in range(2):
        right_ref[0, :, a * hidden : (a + 1) * hidden] = product(
            left_ref[a, 0, :, :rows], min_ref[a, 0]
        )
    right_ref[0, :, 2 * hidden :] = product(left_out_ref[0, :, :out_rows], mout_ref[0])


def right_experts(lefts, lefts_out, merged_in, merged_out):
    count, rows, hidden = merged_in.shape[1:]
    out_rows, width = merged_out.shape[1:]
    wide, wide_out = lefts.shape[3], lefts_out.shape[2]
    return pl.pallas_call(
        right_expert_kernel,
        grid=(count,),
        in_specs=[
            pl.BlockSpec((2, 1, 8, wide), lambda e: (0, e, 0, 0)),
            pl.BlockSpec((1, 8, wide_out), lambda e: (e, 0, 0)),
            pl.BlockSpec((2, 1, rows, hidden), lambda e: (0, e, 0, 0)),
            pl.BlockSpec((1, out_rows, width), lambda e: (e, 0, 0)),
        ],
        out_specs=pl.BlockSpec((1, 8, 2 * hidden + width), lambda e: (e, 0, 0)),
        out_shape=struct((count, 8, 2 * hidden + width)),
        compiler_params=params(),
        name="right_experts",
    )(lefts, lefts_out, merged_in, merged_out)


def right_attention_kernel(
    shards, rows, left_ref, leftz_ref, first_ref, joint_ref, mixed_ref, middle_ref, eq_ref, ep_ref,
    eo_ref, right_ref,
):
    qw, kv = eq_ref.shape[1], ep_ref.shape[2]
    width = eo_ref.shape[1]

    def whole(k):
        return jnp.concatenate(
            [leftz_ref[z, 8 * k : 8 * k + 8, :rows] for z in range(shards)], axis=1
        )

    def own(k):
        return left_ref[8 * k : 8 * k + 8, :rows]

    first = first_ref[...]
    at = 0
    for k, error in ((0, eq_ref[...]), (1, ep_ref[0]), (2, ep_ref[1])):
        grown = exact_nn(exact_nt(whole(k), first), joint_ref[:, at : at + error.shape[1]])
        right_ref[:, at : at + error.shape[1]] = grown + nn(own(k), error, HIGHEST)
        at += error.shape[1]
    grown = exact_nn(exact_nt(whole(3), mixed_ref[...]), middle_ref[...])
    right_ref[:, at : at + width] = grown + nn(own(3), eo_ref[...], HIGHEST)


def right_attention(shards, rows, operands):
    width = operands[6].shape[1] + 2 * operands[7].shape[2] + operands[8].shape[1]
    return pl.pallas_call(
        functools.partial(right_attention_kernel, shards, rows),
        in_specs=vmem_specs(len(operands)),
        out_specs=pl.BlockSpec(memory_space=pltpu.VMEM),
        out_shape=struct((8, width)),
        compiler_params=params(),
        name="right_attention",
    )(*operands)


def right_sync_kernel(
    reps, shards, piece, experts_ref, attention_ref, out_ref, parts, heard, across, total, ps, pr,
    zs, zr, gs, gr,
):
    rep, shard = lax.axis_index("rep"), lax.axis_index("shard")
    half = piece // 2
    greet(reps, shards)
    line = jnp.concatenate(
        [experts_ref[e] for e in range(experts_ref.shape[0])] + [attention_ref[...]], axis=1
    )
    line = padded(line, reps * piece)
    for k in range(reps):
        at = k * piece
        parts[k] = jnp.concatenate(
            [line[:, at : at + half], line[:, at + half : at + piece]], axis=0
        ).astype(BF16)
    send_all("rep", reps, lambda to: parts.at[to], lambda step: heard.at[step - 1], ps, pr)
    mine = parts[rep].astype(F32)
    for step in range(reps - 1):
        mine = mine + heard[step].astype(F32)
    across[shard] = mine.astype(BF16)
    send_all("shard", shards, lambda to: across.at[shard], lambda step: across.at[shard], zs, zr)
    summed = across[0].astype(F32)
    for k in range(1, shards):
        summed = summed + across[k].astype(F32)
    total[rep] = summed.astype(BF16)
    send_all("rep", reps, lambda to: total.at[rep], lambda step: total.at[rep], gs, gr)
    for k in range(reps):
        block = total[k].astype(F32)
        out_ref[:, k * piece : k * piece + half] = block[:8]
        out_ref[:, k * piece + half : (k + 1) * piece] = block[8:]


def right_sync(reps, shards, experts, attention):
    columns = experts.shape[0] * experts.shape[2] + attention.shape[1]
    piece = up_to(-(-columns // reps), 256)
    dma = pltpu.SemaphoreType.DMA
    return pl.pallas_call(
        functools.partial(right_sync_kernel, reps, shards, piece),
        in_specs=vmem_specs(2),
        out_specs=pl.BlockSpec(memory_space=pltpu.VMEM),
        out_shape=struct((8, reps * piece)),
        scratch_shapes=[
            pltpu.VMEM((reps, 16, piece // 2), BF16),
            pltpu.VMEM((reps - 1, 16, piece // 2), BF16),
            pltpu.VMEM((shards, 16, piece // 2), BF16),
            pltpu.VMEM((reps, 16, piece // 2), BF16),
            dma((reps - 1,)),
            dma((reps - 1,)),
            dma((shards - 1,)),
            dma((shards - 1,)),
            dma((reps - 1,)),
            dma((reps - 1,)),
        ],
        compiler_params=params(collective_id=2, has_side_effects=True),
        name="right_sync",
    )(experts, attention)


def low_rank(left, right):
    high, low = two_terms(left)
    lefts = jnp.concatenate([high.astype(F32), low.astype(F32)], axis=0).astype(BF16)
    rights = jnp.concatenate([right, right], axis=0).astype(BF16)
    return tn(lefts, rights)


def feedback_expert_kernel(
    replicas, left_ref, left_out_ref, right_ref, min_ref, mout_ref, fin_ref, fout_ref, sq_ref
):
    expert = pl.program_id(0)
    rows, hidden = min_ref.shape[2:]
    out_rows = mout_ref.shape[1]
    row = lax.broadcasted_iota(jnp.int32, (8, 128), 0)
    lane = lax.broadcasted_iota(jnp.int32, (8, 128), 1)

    @pl.when(expert == 0)
    def _():
        sq_ref[...] = jnp.zeros_like(sq_ref)

    added = jnp.zeros((8, 128), F32)
    for a in range(2):
        approx = low_rank(
            left_ref[a, 0, :, :rows], right_ref[:, a * hidden : (a + 1) * hidden]
        )
        left_over = min_ref[a, 0] - approx * (1.0 / replicas)
        fin_ref[a, 0] = left_over
        added = jnp.where(lane == a, jnp.sum(left_over * left_over), added)
    approx = low_rank(left_out_ref[0, :, :out_rows], right_ref[:, 2 * hidden :])
    left_over = mout_ref[0] - approx * (1.0 / replicas)
    fout_ref[0] = left_over
    added = jnp.where(lane == 2, jnp.sum(left_over * left_over), added)
    sq_ref[...] += jnp.where(row == expert, added, 0.0)


def feedback_experts(replicas, lefts, lefts_out, rights, merged_in, merged_out):
    count, rows, hidden = merged_in.shape[1:]
    out_rows, width = merged_out.shape[1:]
    wide, wide_out = lefts.shape[3], lefts_out.shape[2]
    in_block = pl.BlockSpec((2, 1, rows, hidden), lambda e: (0, e, 0, 0))
    out_block = pl.BlockSpec((1, out_rows, width), lambda e: (e, 0, 0))
    return pl.pallas_call(
        functools.partial(feedback_expert_kernel, replicas),
        grid=(count,),
        in_specs=[
            pl.BlockSpec((2, 1, 8, wide), lambda e: (0, e, 0, 0)),
            pl.BlockSpec((1, 8, wide_out), lambda e: (e, 0, 0)),
            pl.BlockSpec((8, 2 * hidden + width), lambda e: (0, e)),
            in_block,
            out_block,
        ],
        out_specs=[in_block, out_block, pl.BlockSpec((8, 128), lambda e: (0, 0))],
        out_shape=[struct(merged_in.shape), struct(merged_out.shape), struct((8, 128))],
        compiler_params=params(),
        name="feedback_experts",
    )(lefts, lefts_out, rights, merged_in, merged_out)


def feedback_attention_kernel(
    replicas, rows, left_ref, right_ref, gj_ref, go_ref, eq_ref, ep_ref, eo_ref, fq_ref, fp_ref,
    fo_ref, sq_ref,
):
    qw, kv = eq_ref.shape[1], ep_ref.shape[2]
    lane = lax.broadcasted_iota(jnp.int32, (8, 128), 1)
    row = lax.broadcasted_iota(jnp.int32, (8, 128), 0)
    added = jnp.zeros((8, 128), F32)
    at = 0
    jobs = (
        (gj_ref, 0, eq_ref, fq_ref),
        (gj_ref, qw, ep_ref.at[0], fp_ref.at[0]),
        (gj_ref, qw + kv, ep_ref.at[1], fp_ref.at[1]),
        (go_ref, 0, eo_ref, fo_ref),
    )
    for k, (grad_ref, low, error_ref, out_ref) in enumerate(jobs):
        width = error_ref.shape[1]
        approx = low_rank(left_ref[8 * k : 8 * k + 8, :rows], right_ref[:, at : at + width])
        merged = grad_ref[:, low : low + width].astype(F32) + error_ref[...]
        left_over = merged - approx * (1.0 / replicas)
        out_ref[...] = left_over
        added = jnp.where(lane == 3 + k, jnp.sum(left_over * left_over), added)
        at += width
    sq_ref[...] = jnp.where(row == 0, added, 0.0)


def feedback_attention(replicas, rows, operands):
    shapes = [operands[k].shape for k in (4, 5, 6)]
    return pl.pallas_call(
        functools.partial(feedback_attention_kernel, replicas, rows),
        in_specs=vmem_specs(len(operands)),
        out_specs=vmem_specs(4),
        out_shape=[struct(shape) for shape in shapes] + [struct((8, 128))],
        compiler_params=params(),
        name="feedback_attention",
    )(*operands)


def squares_sync_kernel(reps, shards, a_ref, b_ref, out_ref, plane, line, ps, pr, zs, zr):
    rep, shard = lax.axis_index("rep"), lax.axis_index("shard")
    greet(reps, shards)
    plane[rep] = a_ref[...] + b_ref[...]
    send_all("rep", reps, lambda to: plane.at[rep], lambda step: plane.at[rep], ps, pr)
    summed = plane[0]
    for k in range(1, reps):
        summed = summed + plane[k]
    line[shard] = summed
    send_all("shard", shards, lambda to: line.at[shard], lambda step: line.at[shard], zs, zr)
    summed = line[0]
    for k in range(1, shards):
        summed = summed + line[k]
    out_ref[...] = summed


def squares_sync(reps, shards, first, second):
    dma = pltpu.SemaphoreType.DMA
    return pl.pallas_call(
        functools.partial(squares_sync_kernel, reps, shards),
        in_specs=vmem_specs(2),
        out_specs=pl.BlockSpec(memory_space=pltpu.VMEM),
        out_shape=struct((8, 128)),
        scratch_shapes=[
            pltpu.VMEM((reps, 8, 128), F32),
            pltpu.VMEM((shards, 8, 128), F32),
            dma((reps - 1,)),
            dma((reps - 1,)),
            dma((shards - 1,)),
            dma((shards - 1,)),
        ],
        compiler_params=params(collective_id=3, has_side_effects=True),
        name="squares_sync",
    )(first, second)


def per_device(
    tokens,
    cotangent,
    seg_ids,
    parents,
    positions,
    routes,
    query_weight,
    pair_weight,
    output_weight,
    inner_weight,
    outer_weight,
    router_weight,
    norm_gains,
    query_moment,
    pair_moment,
    output_moment,
    inner_moment,
    outer_moment,
    router_moment,
    gains_moment,
    query_error,
    pair_error,
    output_error,
    inner_error,
    outer_error,
    query_start,
    pair_start,
    output_start,
    inner_start,
    outer_start,
):
    replicas = lax.axis_size("rep")
    shard_count = lax.axis_size("shard")
    here = lax.axis_index("shard")
    both = ("rep", "shard")
    bf16 = jnp.bfloat16
    query_t = jnp.swapaxes(query_weight, 0, 1).astype(bf16)
    pair_t = jnp.swapaxes(pair_weight, 1, 2).astype(bf16)
    output_t = jnp.swapaxes(output_weight, 0, 1).astype(bf16)
    inner_t = jnp.transpose(inner_weight, (1, 0, 3, 2)).astype(bf16)
    outer_low = outer_weight.astype(bf16)
    router_t = jnp.swapaxes(router_weight, 0, 1).astype(bf16)
    gains_low = norm_gains.astype(bf16)
    own_rows = query_t.shape[1]
    q_cols, p_cols, f_cols = query_t.shape[0], pair_t.shape[1], inner_t.shape[2]
    f_rows = outer_low.shape[1]
    small = jnp.concatenate([router_t, gains_low], axis=0)
    small = jnp.pad(small, ((0, 16 - small.shape[0]), (0, 0)))
    packed = jnp.concatenate(
        [query_t, pair_t.reshape(2 * p_cols, own_rows), output_t, small], axis=0
    )
    spread = lax.all_gather(packed, both).reshape(replicas, shard_count, packed.shape[0], own_rows)

    per_chunk = E // CHUNKS
    outer_cols = outer_low.shape[2]
    paired = replicas % 2 == 0 and per_chunk == 2 and own_rows == 2 * outer_cols == 2 * f_rows
    paired = paired and 2 * f_cols == f_rows and f_cols % 16 == 0 and own_rows % 128 == 0

    def whole_weights(inner_all, outer_all):
        inner_all = inner_all.reshape(replicas, shard_count, per_chunk, 2, f_cols, own_rows)
        w1 = jnp.transpose(inner_all, (2, 3, 0, 4, 1, 5)).reshape(
            1, 1, per_chunk, 2 * replicas * f_cols, shard_count * own_rows
        )
        w2 = jnp.transpose(outer_all, (2, 1, 3, 0, 4)).reshape(
            1, per_chunk, 1, 1, shard_count * f_rows, replicas * outer_cols
        )
        return w1, w2

    if paired:
        core = lax.axis_index("rep") % 2
        outer_pairs = outer_low.reshape(CHUNKS, 2, f_rows, outer_cols)
        keep = jnp.where(core == 0, outer_pairs[:, 0], outer_pairs[:, 1])
        give = jnp.where(core == 0, outer_pairs[:, 1], outer_pairs[:, 0])
        got = lax.ppermute(give, "rep", [(i, i + 1 - 2 * (i % 2)) for i in range(replicas)])
        wide_outer = jnp.concatenate(
            [jnp.where(core == 0, keep, got), jnp.where(core == 0, got, keep)], axis=2
        )
        packs = jnp.concatenate(
            [inner_t.reshape(CHUNKS, per_chunk * 2 * f_cols, own_rows), wide_outer], axis=1
        )
        height = packs.shape[1]
        split = CHUNKS // 2
        early = z_gather(packs[:split].reshape(split * height, own_rows))
        held, spread = lax.optimization_barrier((packs[split:], spread))
        late = z_gather(held.reshape((CHUNKS - split) * height, own_rows))
        chunk_weights = []
        for index in range(CHUNKS):
            source = early if index < split else late
            at = (index % split) * height
            part = lax.all_gather(source[:, at : at + height], "rep")
            w1 = part.reshape(replicas, shard_count, 3, f_rows, own_rows)
            w2 = part.reshape(replicas // 2, 2, shard_count, 3, f_rows, own_rows)
            chunk_weights.append((w1, w2))
        _, cot_t = lax.optimization_barrier((late, jnp.transpose(cotangent)))
    else:
        chunk_weights = []
        for index in range(CHUNKS):
            span = slice(index * per_chunk, (index + 1) * per_chunk)
            chunk_weights.append(
                whole_weights(
                    lax.all_gather(inner_t[span], both),
                    lax.all_gather(outer_low[span], both).reshape(
                        replicas, shard_count, per_chunk, f_rows, outer_cols
                    ),
                )
            )
        cot_t = jnp.transpose(cotangent)

    def joined(piece):
        return jnp.transpose(piece, (0, 2, 1, 3)).reshape(-1, shard_count * own_rows)

    query_full = joined(spread[:, :, :q_cols])
    pair_full = jnp.stack(
        [
            joined(spread[:, :, q_cols + a * p_cols : q_cols + (a + 1) * p_cols])
            for a in range(2)
        ]
    )
    at = q_cols + 2 * p_cols
    output_full = joined(spread[:, :, at : at + q_cols])
    at += q_cols
    router_full = joined(spread[:1, :, at : at + E])
    gain_values = joined(spread[:1, :, at + E : at + E + 2]).astype(jnp.float32)

    upstream_slots = z_slots(cot_t)

    hidden = tokens.astype(jnp.float32)
    length = hidden.shape[0]
    position = positions[0]
    allowed = path_mask(seg_ids[0], parents[0])
    first_low = rms_norm(hidden, gain_values[0]).astype(bf16)
    query_pre = jnp.einsum("td,qd->tq", first_low, query_full, preferred_element_type=jnp.float32)
    pair_pre = jnp.einsum("td,awd->atw", first_low, pair_full, preferred_element_type=jnp.float32)
    query_rot = rotate(query_pre.reshape(length, HQ, HD), position, 1.0).astype(bf16)
    key_rot = rotate(pair_pre[0].reshape(length, HK, HD), position, 1.0).astype(bf16)
    values = pair_pre[1].reshape(length, HK, HD).astype(bf16)
    block_rows = min(512, length)
    masked, shaped = scores_of(query_rot, key_rot, allowed)
    top_score = jnp.max(masked, axis=-1, keepdims=True)
    raised = jnp.exp(masked - top_score)
    total_sum = jnp.sum(raised, axis=-1, keepdims=True)
    attention = (raised / total_sum).astype(bf16)
    lse_parts = top_score + jnp.log(total_sum)
    mixed_block = jnp.einsum(
        "kgqt,tkd->qkgd", attention, values, preferred_element_type=jnp.float32
    )
    mixed_low = mixed_block.reshape(block_rows, HQ * HD).astype(bf16)
    middle = hidden + jnp.einsum(
        "tq,dq->td", mixed_low, output_full, preferred_element_type=jnp.float32
    )
    second_low = rms_norm(middle, gain_values[1]).astype(bf16)
    logits = jnp.einsum("td,ed->te", second_low, router_full, preferred_element_type=jnp.float32)
    expert_ids = jnp.arange(E, dtype=jnp.int32)
    route_mask = jnp.any(routes[:, :, None] == expert_ids[None, None, :], axis=1)
    route_top = jnp.max(jnp.where(route_mask, logits, -1e30), axis=-1, keepdims=True)
    raised_gate = jnp.where(route_mask, jnp.exp(logits - route_top), 0.0)
    shares = raised_gate / jnp.sum(raised_gate, axis=-1, keepdims=True)
    shares_t = jnp.transpose(shares)
    shares_high = shares_t.astype(bf16)
    shares_rest = (shares_t - shares_high.astype(jnp.float32)).astype(bf16)
    second_slots = z_slots(
        jnp.concatenate([jnp.transpose(second_low), shares_high, shares_rest], axis=0)
    )

    upstream = cotangent.astype(jnp.float32)
    start_in = jnp.swapaxes(inner_start, 2, 3)
    start_out = jnp.swapaxes(outer_start, 1, 2)
    merged_experts = None
    combined = middle
    second_grad = None
    combine_parts, lins, louts = [], [], []
    for index in range(CHUNKS):
        w1, w2 = chunk_weights[index]
        done = expert_chunk(
            index * per_chunk,
            second_slots,
            upstream_slots,
            cotangent,
            w1,
            w2,
            inner_error[0],
            outer_error[0],
            start_in,
            start_out,
            merged_experts,
        )
        merged_experts = (done[0], done[1])
        combined = combined + done[2]
        second_grad = done[3] if second_grad is None else second_grad + done[3]
        combine_parts.append(done[4][:, :, 0])
        lins.append(done[5])
        louts.append(done[6])
    output = combined.astype(bf16)
    combine_grad = jnp.transpose(jnp.concatenate(combine_parts, axis=0))
    logit_low = (
        shares * (combine_grad - jnp.sum(shares * combine_grad, axis=-1, keepdims=True))
    ).astype(bf16)
    grad_router = jnp.einsum("td,te->de", second_low, logit_low, preferred_element_type=jnp.float32)
    second_grad = second_grad + jnp.einsum(
        "te,ed->td", logit_low, router_full, preferred_element_type=jnp.float32
    )
    _, second_pull = jax.vjp(rms_norm, middle, gain_values[1])
    middle_part, gain_two = second_pull(second_grad)
    middle_grad = upstream + middle_part
    middle_low = middle_grad.astype(bf16)
    grad_output = jnp.einsum("tq,td->qd", mixed_low, middle_low, preferred_element_type=jnp.float32)
    group_output = lax.psum_scatter(
        grad_output.astype(bf16), "shard", scatter_dimension=0, tiled=True
    )
    mixed_grad = jnp.einsum(
        "td,dq->tq", middle_low, output_full, preferred_element_type=jnp.float32
    ).astype(bf16)
    masked, shaped = scores_of(query_rot, key_rot, allowed)
    attention_full = jnp.exp(masked - lse_parts)
    upstream_block = mixed_grad.reshape(block_rows, HK, HQ // HK, HD)
    attn_grad = jnp.einsum(
        "qkgd,tkd->kgqt", upstream_block, values, preferred_element_type=jnp.float32
    )
    score_low = (
        attention_full * (attn_grad - jnp.sum(attention_full * attn_grad, axis=-1, keepdims=True))
    ).astype(bf16)
    query_block_grad = jnp.einsum(
        "kgqt,tkd->qkgd", score_low, key_rot, preferred_element_type=jnp.float32
    ) * HD ** (-0.5)
    query_parts = query_block_grad.reshape(block_rows, HQ, HD)
    key_rot_grad = jnp.einsum(
        "kgqt,qkgd->tkd", score_low, shaped, preferred_element_type=jnp.float32
    ) * HD ** (-0.5)
    value_grad = jnp.einsum(
        "kgqt,qkgd->tkd",
        attention_full.astype(bf16),
        upstream_block,
        preferred_element_type=jnp.float32,
    )
    query_grad = rotate(query_parts, position, -1.0).reshape(length, HQ * HD).astype(bf16)
    key_grad = rotate(key_rot_grad, position, -1.0).reshape(length, HK * HD).astype(bf16)
    value_low = value_grad.reshape(length, HK * HD).astype(bf16)
    joint_grad = jnp.concatenate([query_grad, key_grad, value_low], axis=1)
    grad_joint = jnp.einsum("td,tq->dq", first_low, joint_grad, preferred_element_type=jnp.float32)
    group_joint = lax.psum_scatter(
        grad_joint.astype(bf16), "shard", scatter_dimension=0, tiled=True
    )
    joint_full = jnp.concatenate([query_full, pair_full[0], pair_full[1]], axis=0)
    first_grad = jnp.dot(joint_grad, joint_full, preferred_element_type=jnp.float32)
    _, first_pull = jax.vjp(rms_norm, hidden, gain_values[0])
    hidden_part, gain_one = first_pull(first_grad)
    input_grad = (middle_grad + hidden_part).astype(bf16)
    grad_gains = jnp.stack([gain_one, gain_two])

    small_rows = [jnp.transpose(grad_router), jnp.pad(grad_gains, ((0, 6), (0, 0)))]
    start_q, start_o = jnp.transpose(query_start), jnp.transpose(output_start)
    start_p = jnp.swapaxes(pair_start, 1, 2)
    z_part, own_left = left_parts(
        shard_count,
        own_rows,
        (
            first_low, joint_grad, mixed_low, middle_low, start_q, start_p[0], start_p[1], start_o,
            query_error[0], pair_error[0], output_error[0], *small_rows,
        ),
    )
    left_flat, left_out_flat, totals, total_squares, left_lines = left_sync(
        replicas, shard_count, z_part, own_left, lins, louts
    )
    wide, wide_out = left_flat.shape[1], left_out_flat.shape[1]
    lefts = left_flat.reshape(-1, 8, wide)
    lefts_in = lefts[4:].reshape(2, E, 8, wide)
    lefts_out = left_out_flat.reshape(E, 8, wide_out)
    lefts_t = (
        lefts[0, :, :own_rows],
        lefts[1:3, :, :own_rows],
        lefts[3, :, :own_rows],
        lefts_in[..., :own_rows],
        lefts_out[..., :f_rows],
    )
    bases = tuple(jnp.swapaxes(left, -1, -2) for left in lefts_t)

    right_parts = right_experts(lefts_in, lefts_out, *merged_experts)
    right_rest = right_attention(
        shard_count,
        own_rows,
        (
            left_flat[:32], left_lines, first_low, joint_grad, mixed_low, middle_low,
            query_error[0], pair_error[0], output_error[0],
        ),
    )
    rights = right_sync(replicas, shard_count, right_parts, right_rest)
    hidden_units = merged_experts[0].shape[3]
    step = 2 * hidden_units + D
    by_expert = rights[:, : E * step].reshape(8, E, step)
    rest = rights[:, E * step :]
    kv = HK * HD
    rights_t = (
        rest[:, :QW],
        jnp.stack([rest[:, QW : QW + kv], rest[:, QW + kv : QW + 2 * kv]]),
        rest[:, QW + 2 * kv : QW + 2 * kv + D],
        jnp.transpose(by_expert[:, :, : 2 * hidden_units].reshape(8, E, 2, hidden_units), (2, 1, 0, 3)),
        jnp.transpose(by_expert[:, :, 2 * hidden_units :], (1, 0, 2)),
    )
    right_out = tuple(jnp.swapaxes(right, -1, -2) for right in rights_t)

    feedback_in, feedback_out, squares_experts = feedback_experts(
        replicas, lefts_in, lefts_out, rights, *merged_experts
    )
    feedback_q, feedback_p, feedback_o, squares_rest = feedback_attention(
        replicas,
        own_rows,
        (
            left_flat[:32], rest[:, : QW + 2 * kv + D], group_joint, group_output,
            query_error[0], pair_error[0], output_error[0],
        ),
    )
    feedbacks = tuple(
        part[None] for part in (feedback_q, feedback_p, feedback_o, feedback_in, feedback_out)
    )
    squares = squares_sync(replicas, shard_count, squares_experts, squares_rest)
    flat_squares = jnp.concatenate(
        [squares[0, 3:7], squares[:, 0], squares[:, 1], squares[:, 2]], axis=0
    )

    column_index = lax.axis_index("rep")
    weights_now = (query_weight, pair_weight, output_weight, inner_weight, outer_weight)
    moments_now = (query_moment, pair_moment, output_moment, inner_moment, outer_moment)
    step_rates = (
        STEP_RATE * D ** (-0.5),
        STEP_RATE * D ** (-0.5),
        STEP_RATE * (QW * 4 // TOK_DEV + 1) ** (-0.5),
        STEP_RATE * D ** (-0.5),
        STEP_RATE * (F // 2) ** (-0.5),
    )
    momenta = []
    new_masters = []
    entry_list = []
    for index in range(5):
        left, right = lefts_t[index], rights_t[index]
        columns = right.shape[-1]
        entries = left.shape[-1] * shard_count * columns
        own_columns = columns // replicas
        squared_right = jnp.sum(right * right, axis=(-2, -1))
        scale_norm = jnp.sqrt(squared_right / entries + 1e-06)
        own_right = lax.dynamic_slice_in_dim(
            right, column_index * own_columns, own_columns, axis=right.ndim - 1
        )
        direction = (
            jnp.einsum("...km,...kn->...mn", left, own_right, precision=HIGHEST)
            / scale_norm[..., None, None]
        )
        new_master, new_moment = advance(
            weights_now[index], moments_now[index], direction, step_rates[index], WEIGHT_DECAY
        )
        momenta.append(new_moment)
        new_masters.append(new_master)
        entry_list += [float(replicas * entries)] * (left.size // (8 * left.shape[-1]))
    feedback_rms = jnp.sqrt(flat_squares / jnp.array(entry_list, F32))
    router_total = jnp.transpose(totals[0, :, :own_rows])
    gains_total = totals[1, :2, :own_rows]
    router_square = jnp.sum(total_squares[:, 0])
    gains_square = total_squares[:2, 1]
    router_direction = router_total / jnp.sqrt(
        router_square / (router_total.shape[0] * shard_count * router_total.shape[1]) + 1e-06
    )
    gains_direction = (
        gains_total / jnp.sqrt(gains_square / (gains_total.shape[1] * shard_count) + 1e-06)[:, None]
    )
    router_master, router_momentum = advance(
        router_weight, router_moment, router_direction, STEP_RATE * (8 * D) ** (-0.5), WEIGHT_DECAY
    )
    gains_master, gains_momentum = advance(
        norm_gains, gains_moment, gains_direction, GAIN_RATE, 0.0
    )
    return (
        output,
        input_grad,
        *bases,
        *right_out,
        *feedbacks,
        *momenta,
        router_momentum,
        gains_momentum,
        *new_masters,
        router_master,
        gains_master,
        feedback_rms,
    )


def solution(mesh):
    in_specs = (
        P(("rep", "shard"), None),
        P(("rep", "shard"), None),
        P(("rep", "shard"), None),
        P(("rep", "shard"), None),
        P(("rep", "shard"), None),
        P(("rep", "shard"), None),
        P("shard", "rep"),
        P(None, "shard", "rep"),
        P("shard", "rep"),
        P(None, None, "shard", "rep"),
        P(None, "shard", "rep"),
        P("shard", None),
        P(None, "shard"),
        P("shard", "rep"),
        P(None, "shard", "rep"),
        P("shard", "rep"),
        P(None, None, "shard", "rep"),
        P(None, "shard", "rep"),
        P("shard", None),
        P(None, "shard"),
        P("rep", "shard", None),
        P("rep", None, "shard", None),
        P("rep", "shard", None),
        P("rep", None, None, "shard", None),
        P("rep", None, "shard", None),
        P(),
        P(),
        P(),
        P(),
        P(),
    )
    out_specs = (
        P(("rep", "shard"), None),
        P(("rep", "shard"), None),
        P("shard", None),
        P(None, "shard", None),
        P("shard", None),
        P(None, None, "shard", None),
        P(None, "shard", None),
        P(),
        P(),
        P(),
        P(),
        P(),
        P("rep", "shard", None),
        P("rep", None, "shard", None),
        P("rep", "shard", None),
        P("rep", None, None, "shard", None),
        P("rep", None, "shard", None),
        P("shard", "rep"),
        P(None, "shard", "rep"),
        P("shard", "rep"),
        P(None, None, "shard", "rep"),
        P(None, "shard", "rep"),
        P("shard", None),
        P(None, "shard"),
        P("shard", "rep"),
        P(None, "shard", "rep"),
        P("shard", "rep"),
        P(None, None, "shard", "rep"),
        P(None, "shard", "rep"),
        P("shard", None),
        P(None, "shard"),
        P(),
    )
    return jax.shard_map(
        per_device, mesh=mesh, in_specs=in_specs, out_specs=out_specs, check_vma=False
    )
```

```python
import functools

import jax
import jax.numpy as jnp
from jax import lax
from jax.experimental import pallas as pl
from jax.experimental.pallas import tpu as pltpu
from jax.sharding import PartitionSpec as P

D = 1536
HQ = 12
HK = 2
HD = 128
F = 768
E = 8
TOK_DEV = 512
QW = 1536


EPSILON = 1e-05
ROPE_BASE = 1000000.0
MOMENTUM_DECAY = 0.9
WEIGHT_DECAY = 0.01
STEP_RATE = 4.0
GAIN_RATE = 3.0
HIGHEST = lax.Precision.HIGHEST


def rms_norm(hidden, gain_row):
    return (
        hidden * lax.rsqrt(jnp.mean(hidden * hidden, axis=-1, keepdims=True) + EPSILON) * gain_row
    )


def path_mask(segment, parent_row):
    table_ids = jnp.arange(parent_row.shape[0], dtype=jnp.int32)
    parent_one = jnp.sum(
        jnp.where(segment[:, None] == table_ids[None, :], parent_row[None, :], 0), axis=1
    )
    parent_two = jnp.where(
        parent_one >= 0,
        jnp.sum(
            jnp.where(parent_one[:, None] == table_ids[None, :], parent_row[None, :], 0), axis=1
        ),
        -1,
    )
    token_order = jnp.arange(segment.shape[0], dtype=jnp.int32)
    same_path = (segment[:, None] == segment[None, :]) & (
        token_order[None, :] <= token_order[:, None]
    )
    return (
        same_path
        | (segment[None, :] == parent_one[:, None])
        | (segment[None, :] == parent_two[:, None])
    )


def advance(weight_now, moment_now, direction, step_rate, decay_rate):
    moment_new = MOMENTUM_DECAY * moment_now + (1.0 - MOMENTUM_DECAY) * direction
    return (weight_now - step_rate * (moment_new + decay_rate * weight_now), moment_new)


CHUNKS = 4
GELU_C = 0.7978845608028654
GELU_A = 0.044715
MESH = pl.DeviceIdType.MESH
VMEM_LIMIT = 60 * 1024 * 1024
F32 = jnp.float32
BF16 = jnp.bfloat16


def z_slots(block):
    size = lax.axis_size("shard")
    return [block] + [
        lax.ppermute(block, "shard", [(i, (i + step) % size) for i in range(size)])
        for step in range(1, size)
    ]


def nn(a, b, precision=None):
    return jnp.dot(a, b, preferred_element_type=F32, precision=precision)


def nt(a, b, precision=None):
    return lax.dot_general(
        a, b, (((1,), (1,)), ((), ())), preferred_element_type=F32, precision=precision
    )


def tn(a, b):
    return lax.dot_general(a, b, (((0,), (0,)), ((), ())), preferred_element_type=F32)


def up_to(count, unit):
    return -(-count // unit) * unit


def two_terms(value):
    high = value.astype(BF16)
    return high, (value - high.astype(F32)).astype(BF16)


def three_terms(value):
    high = value.astype(BF16)
    rest = value - high.astype(F32)
    middle = rest.astype(BF16)
    low = (rest - middle.astype(F32)).astype(BF16)
    return jnp.concatenate([high.astype(F32), middle.astype(F32), low.astype(F32)], axis=0).astype(BF16)


def folded(value, rows=8):
    return value[:rows] + value[rows : 2 * rows] + value[2 * rows : 3 * rows]


def exact_nn(value, other):
    return folded(nn(three_terms(value), other))


def exact_nt(value, other):
    return folded(nt(three_terms(value), other))


def padded(value, width):
    if value.shape[1] == width:
        return value
    return jnp.concatenate(
        [value, jnp.zeros((value.shape[0], width - value.shape[1]), value.dtype)], axis=1
    )


def params(**more):
    return pltpu.CompilerParams(vmem_limit_bytes=VMEM_LIMIT, **more)


def vmem_specs(count):
    return [pl.BlockSpec(memory_space=pltpu.VMEM)] * count


def struct(shape, dtype=F32):
    return jax.ShapeDtypeStruct(shape, dtype)


def turn_heads(value, cosine, sine):
    return value * cosine + pltpu.roll(value, HD // 2, 1) * sine


def softmax_of(query, key, mask):
    raw = nt(query, key) * HD ** (-0.5)
    masked = jnp.where(mask > 0, raw, -1e30)
    raised = jnp.exp(masked - jnp.max(masked, axis=-1, keepdims=True))
    return raised / jnp.sum(raised, axis=-1, keepdims=True)


def head_lanes(head):
    return pl.ds(pl.multiple_of(head * HD, HD), HD)


def attention_forward_kernel(
    first_ref, query_ref, key_ref, value_ref, output_ref, tokens_ref, cosine_ref, sine_ref, mask_ref,
    qrot_ref, krot_ref, values_ref, mixed_ref, middle_ref,
):
    first = first_ref[...]
    cosine, sine = cosine_ref[...], sine_ref[...]
    values_ref[...] = nt(first, value_ref[...]).astype(BF16)
    keys = nt(first, key_ref[...])
    for g in range(HK):
        span = slice(g * HD, (g + 1) * HD)
        krot_ref[:, span] = turn_heads(keys[:, span], cosine, sine).astype(BF16)
    queries = nt(first, query_ref[...])
    for h in range(HQ):
        span = slice(h * HD, (h + 1) * HD)
        qrot_ref[:, span] = turn_heads(queries[:, span], cosine, sine).astype(BF16)

    @pl.loop(0, HQ)
    def _(head):
        group = head_lanes(head // (HQ // HK))
        share = softmax_of(qrot_ref[:, head_lanes(head)], krot_ref[:, group], mask_ref[...])
        mixed_ref[:, head_lanes(head)] = nn(share.astype(BF16), values_ref[:, group]).astype(BF16)

    middle_ref[...] = tokens_ref[...].astype(F32) + nt(mixed_ref[...], output_ref[...])


def attention_forward(operands):
    length, width = operands[0].shape
    kv = HK * HD
    return pl.pallas_call(
        attention_forward_kernel,
        in_specs=vmem_specs(len(operands)),
        out_specs=vmem_specs(5),
        out_shape=[
            struct((length, HQ * HD), BF16),
            struct((length, kv), BF16),
            struct((length, kv), BF16),
            struct((length, HQ * HD), BF16),
            struct((length, width)),
        ],
        cost_estimate=pl.CostEstimate(
            flops=2 * length * width * (2 * HQ * HD + 2 * kv) + 4 * HQ * HD * length * length,
            bytes_accessed=14 * length * width + 4 * width * HQ * HD,
            transcendentals=HQ * length * length,
        ),
        compiler_params=params(),
        name="attention_forward",
    )(*operands)


def attention_backward_kernel(
    middle_ref, output_ref, qrot_ref, krot_ref, values_ref, cosine_ref, sine_ref, mask_ref, late_ref,
    joint_ref, mixed_ref, dk_ref, dv_ref,
):
    cosine, sine = cosine_ref[...], -sine_ref[...]
    mixed_ref[...] = nn(middle_ref[...], output_ref[...]).astype(BF16)
    dk_ref[...] = jnp.zeros_like(dk_ref)
    dv_ref[...] = jnp.zeros_like(dv_ref)

    @pl.loop(0, HQ)
    def _(head):
        lanes, group = head_lanes(head), head_lanes(head // (HQ // HK))
        query, key = qrot_ref[:, lanes], krot_ref[:, group]
        upstream = mixed_ref[:, lanes]
        share = softmax_of(query, key, mask_ref[...])
        grad = nt(upstream, values_ref[:, group])
        score = share * (grad - jnp.sum(share * grad, axis=-1, keepdims=True))
        score = score.astype(BF16)
        turned = nn(score, key) * HD ** (-0.5)
        joint_ref[:, lanes] = turn_heads(turned, cosine, sine).astype(BF16)
        dk_ref[:, group] += tn(score, query)
        dv_ref[:, group] += tn(share.astype(BF16), upstream)

    qw = HQ * HD
    for g in range(HK):
        span = slice(g * HD, (g + 1) * HD)
        turned = dk_ref[:, span] * HD ** (-0.5)
        joint_ref[:, qw + g * HD : qw + (g + 1) * HD] = turn_heads(turned, cosine, sine).astype(BF16)
    joint_ref[:, qw + HK * HD :] = dv_ref[...].astype(BF16)


def attention_backward(operands):
    length, width = operands[0].shape
    kv = HK * HD
    return pl.pallas_call(
        attention_backward_kernel,
        in_specs=vmem_specs(len(operands)),
        out_specs=pl.BlockSpec(memory_space=pltpu.VMEM),
        out_shape=struct((length, HQ * HD + 2 * kv), BF16),
        scratch_shapes=[
            pltpu.VMEM((length, HQ * HD), BF16),
            pltpu.VMEM((length, kv), F32),
            pltpu.VMEM((length, kv), F32),
        ],
        cost_estimate=pl.CostEstimate(
            flops=8 * length * width * HQ * HD, bytes_accessed=length * width, transcendentals=0
        ),
        compiler_params=params(),
        name="attention_backward",
    )(*operands)


def weights_of(w1_ref, w2_ref, turned):
    here = lax.axis_index("shard")
    groups, lanes, _, double, span1 = w1_ref.shape
    f_cols = double // 2
    lanes2, _, groups2, _, f_rows, span2 = w2_ref.shape

    def joined(parts):
        return parts[0] if len(parts) == 1 else jnp.concatenate(parts, axis=1)

    def place(k, count):
        return lax.rem(here + (count - k), count) if turned else k

    def both():
        return joined(
            [
                w1_ref[:, place(k, lanes), 0].reshape(groups * double, span1)
                for k in range(lanes)
            ]
        )

    def first(a):
        return joined(
            [
                w1_ref[:, place(k, lanes), 0, a * f_cols : (a + 1) * f_cols, :].reshape(
                    groups * f_cols, span1
                )
                for k in range(lanes)
            ]
        )

    def second():
        if not turned:
            return joined(
                [w2_ref[k, 0, :, 0].reshape(groups2 * f_rows, span2) for k in range(lanes2)]
            )
        return jnp.concatenate(
            [
                joined([w2_ref[k, 0, place(g, groups2), 0] for k in range(lanes2)])
                for g in range(groups2)
            ],
            axis=0,
        )

    return groups, f_cols, both, first, second


def share_of(x_ref, expert, width):
    tail = x_ref[width : width + 2 * E, :].astype(F32)
    shares8 = tail[:E] + tail[E:]
    picked = lax.broadcasted_iota(jnp.int32, shares8.shape, 0) == expert
    return jnp.sum(jnp.where(picked, shares8, 0.0), axis=0, keepdims=True)


def hidden_backward(x, w1_ref, w2_ref, turned, br, act_ref, gt_ref, lanes):
    groups, f_cols, both, _, second = weights_of(w1_ref, w2_ref, turned)
    hidden = groups * f_cols
    units = nn(both(), x)
    act_grads = nn(second(), br)
    for r in range(groups):
        gate = units[2 * r * f_cols : (2 * r + 1) * f_cols]
        up = units[(2 * r + 1) * f_cols : (2 * r + 2) * f_cols]
        act_grad = act_grads[r * f_cols : (r + 1) * f_cols]
        square = gate * gate
        bent = jnp.tanh(GELU_C * (gate + GELU_A * (square * gate)))
        lifted = 0.5 * (1.0 + bent)
        gelu = gate * lifted
        slope = lifted + 0.5 * gate * (1.0 - bent * bent) * (
            GELU_C * (1.0 + 3.0 * GELU_A * square)
        )
        act_ref[r * f_cols : (r + 1) * f_cols, lanes] = (gelu * up).astype(BF16)
        gt_ref[r * f_cols : (r + 1) * f_cols, lanes] = (act_grad * up * slope).astype(BF16)
        gt_ref[hidden + r * f_cols : hidden + (r + 1) * f_cols, lanes] = (
            act_grad * gelu
        ).astype(BF16)


def start_product(start, matrix):
    high, low = two_terms(start)
    both = jnp.concatenate([high.astype(F32), low.astype(F32)], axis=0).astype(BF16)
    top, rest = two_terms(matrix)
    first = nt(both, top)
    return first[:8] + first[8:] + nt(both, rest)[:8]


def own_kernel(
    first_expert, turned, x_ref, u_ref, up_ref, w1_ref, w2_ref, err_in_ref, err_out_ref, gate_ref,
    min_ref, mout_ref, y_ref, sg_ref, cg_ref, gt_ref, act_ref, br_ref,
):
    expert = first_expert + pl.program_id(0)
    width = up_ref.shape[1]
    _, _, _, first_weight, second_weight = weights_of(w1_ref, w2_ref, turned)
    rows, out_rows = min_ref.shape[2], mout_ref.shape[1]
    hidden = min_ref.shape[3]
    here = lax.axis_index("shard")
    share = share_of(x_ref, expert, width)
    br_ref[...] = (share * u_ref[...].astype(F32)).astype(BF16)
    hidden_backward(
        x_ref[:width, :], w1_ref, w2_ref, turned, br_ref[...], act_ref, gt_ref, slice(None)
    )
    own_x = x_ref[pl.ds(pl.multiple_of(here * rows, 16), rows), :]
    for a in range(2):
        min_ref[a, 0] = err_in_ref[a, 0] + nt(own_x, gt_ref[a * hidden : (a + 1) * hidden, :])
    own_act = act_ref[pl.ds(pl.multiple_of(here * out_rows, 16), out_rows), :]
    mout_ref[0] = err_out_ref[0] + nt(own_act, br_ref[...])
    expert_out = tn(act_ref[...], second_weight())
    cg_ref[0] = jnp.sum(up_ref[...].astype(F32) * expert_out, axis=1, keepdims=True)
    share_col = jnp.transpose(jnp.broadcast_to(share, (8, share.shape[1])))[:, :1]
    added = share_col * expert_out
    grown = tn(gt_ref[:hidden, :], first_weight(0)) + tn(gt_ref[hidden:, :], first_weight(1))

    @pl.when(pl.program_id(0) == 0)
    def _():
        y_ref[...] = added
        sg_ref[...] = grown

    @pl.when(pl.program_id(0) > 0)
    def _():
        y_ref[...] += added
        sg_ref[...] += grown


def rest_kernel(
    first_expert, trees, last, turned, w1_ref, w2_ref, start_in_ref, start_out_ref, min_in_ref,
    mout_in_ref, *rest,
):
    x_refs, u_refs = rest[:trees], rest[trees : 2 * trees]
    min_ref, mout_ref = rest[2 * trees + 1 : 2 * trees + 3]
    gt_ref, act_ref, br_ref = rest[-3:]
    expert = first_expert + pl.program_id(0)
    rows, out_rows = min_ref.shape[2], mout_ref.shape[1]
    hidden, width = min_ref.shape[3], mout_ref.shape[2]
    length = x_refs[0].shape[1]
    here = lax.axis_index("shard")
    for tree in range(trees):
        x_ref = x_refs[tree]
        lanes = slice(tree * length, (tree + 1) * length)
        share = share_of(x_ref, expert, width)
        br_ref[:, lanes] = (share * u_refs[tree][...].astype(F32)).astype(BF16)
        hidden_backward(
            x_ref[:width, :], w1_ref, w2_ref, turned, br_ref[:, lanes], act_ref, gt_ref, lanes
        )
    own_x = jnp.concatenate(
        [x_ref[pl.ds(pl.multiple_of(here * rows, 16), rows), :] for x_ref in x_refs], axis=1
    )
    for a in range(2):
        min_ref[a, 0] = min_in_ref[a, 0] + nt(own_x, gt_ref[a * hidden : (a + 1) * hidden, :])
    own_act = act_ref[pl.ds(pl.multiple_of(here * out_rows, 16), out_rows), :]
    mout_ref[0] = mout_in_ref[0] + nt(own_act, br_ref[...])
    if last:
        lin_ref, lout_ref = rest[2 * trees + 3 : 2 * trees + 5]
        lin_ref[...] = jnp.zeros_like(lin_ref)
        lout_ref[...] = jnp.zeros_like(lout_ref)
        for a in range(2):
            lin_ref[0, a, :, :rows] = start_product(start_in_ref[a, 0], min_ref[a, 0])
        lout_ref[0, :, :out_rows] = start_product(start_out_ref[0], mout_ref[0])


def whole_block(shape):
    return pl.BlockSpec(shape, lambda e: (0,) * len(shape), pipeline_mode=pl.Buffered(1))


def weight_blocks(w1, w2):
    last_block = w2.shape[3] - 1
    return [
        pl.BlockSpec((*w1.shape[:2], 1, *w1.shape[3:]), lambda e: (0, 0, e, 0, 0)),
        pl.BlockSpec(
            (w2.shape[0], 1, w2.shape[2], 1, *w2.shape[4:]), lambda e: (0, e, 0, last_block, 0, 0)
        ),
    ]


def matrix_blocks(first_expert, shape_in, shape_out):
    return [
        pl.BlockSpec(
            (shape_in[0], 1, *shape_in[2:]), lambda e: (0, first_expert + e, 0, 0)
        ),
        pl.BlockSpec((1, *shape_out[1:]), lambda e: (first_expert + e, 0, 0)),
    ]


def own_experts(first_expert, x, u, upstream, weights, err_in, err_out, gate):
    w1, w2, turned = weights
    count = w2.shape[1]
    hidden, rows = err_in.shape[3], err_in.shape[2]
    length, width = upstream.shape
    matrices = matrix_blocks(first_expert, err_in.shape, err_out.shape)
    in_specs = [
        whole_block(x.shape),
        whole_block(u.shape),
        whole_block(upstream.shape),
        *weight_blocks(w1, w2),
        *matrices,
        pl.BlockSpec(memory_space=pl.ANY),
    ]
    operands = [x, u, upstream, w1, w2, err_in, err_out, gate]
    part_in, part_out = (2, count, rows, hidden), (count, *err_out.shape[1:])
    return pl.pallas_call(
        functools.partial(own_kernel, first_expert, turned),
        grid=(count,),
        in_specs=in_specs,
        out_specs=[
            *matrix_blocks(0, part_in, part_out),
            whole_block((length, width)),
            whole_block((length, width)),
            pl.BlockSpec((1, length, 1), lambda e: (e, 0, 0)),
        ],
        out_shape=[
            struct(part_in),
            struct(part_out),
            struct((length, width)),
            struct((length, width)),
            struct((count, length, 1)),
        ],
        scratch_shapes=[
            pltpu.VMEM((2 * hidden, length), BF16),
            pltpu.VMEM((hidden, length), BF16),
            pltpu.VMEM((width, length), BF16),
        ],
        cost_estimate=pl.CostEstimate(
            flops=28 * count * hidden * width * length,
            bytes_accessed=count * (6 * hidden * width + 24 * rows * hidden) + 12 * length * width,
            transcendentals=0,
        ),
        compiler_params=params(),
        name="own_experts",
    )(*operands)


def rest_experts(first_expert, last, xs, us, weights, start_in, start_out, merged_in, merged_out, gate):
    w1, w2, turned = weights
    count, trees = w2.shape[1], len(xs)
    hidden, rows = merged_in.shape[3], merged_in.shape[2]
    out_rows = merged_out.shape[1]
    width, length = merged_out.shape[2], xs[0].shape[1]
    matrices = matrix_blocks(0, merged_in.shape, merged_out.shape)
    wide, wide_out = up_to(rows, 128), up_to(out_rows, 128)
    out_specs = list(matrices)
    out_shape = [struct(merged_in.shape), struct(merged_out.shape)]
    if last:
        out_specs += [
            pl.BlockSpec((1, 2, 8, wide), lambda e: (e, 0, 0, 0)),
            pl.BlockSpec((1, 8, wide_out), lambda e: (e, 0, 0)),
        ]
        out_shape += [struct((count, 2, 8, wide)), struct((count, 8, wide_out))]
    return pl.pallas_call(
        functools.partial(rest_kernel, first_expert, trees, last, turned),
        grid=(count,),
        in_specs=[
            *weight_blocks(w1, w2),
            *matrix_blocks(first_expert, start_in.shape, start_out.shape),
            *matrices,
            *[whole_block(x.shape) for x in (*xs, *us)],
            pl.BlockSpec(memory_space=pl.ANY),
        ],
        out_specs=out_specs,
        out_shape=out_shape,
        scratch_shapes=[
            pltpu.VMEM((2 * hidden, trees * length), BF16),
            pltpu.VMEM((hidden, trees * length), BF16),
            pltpu.VMEM((width, trees * length), BF16),
        ],
        input_output_aliases={4: 0, 5: 1},
        cost_estimate=pl.CostEstimate(
            flops=14 * count * trees * hidden * width * length,
            bytes_accessed=count * (6 * hidden * width + 24 * rows * hidden),
            transcendentals=0,
        ),
        compiler_params=params(),
        name="rest_experts",
    )(w1, w2, start_in, start_out, merged_in, merged_out, *xs, *us, gate)


def open_kernel(reps, shards, pieces, extra, *refs):
    count = len(pieces)
    sources, targets = refs[: count + 1 + extra], refs[count + 1 + extra : 2 * (count + 1 + extra)]
    local_sem, up_send, up_recv, down_send, down_recv, chip_send, chip_recv, core_send, core_recv = refs[
        2 * (count + 1 + extra) :
    ]
    rep, shard = lax.axis_index("rep"), lax.axis_index("shard")
    chips, core = reps // 2, rep % 2
    chip = rep // 2
    total = count + 1 + extra

    def slot(k, which):
        if k > count:
            return targets[k].at[which]
        span = sources[k].shape[1]
        lanes = pl.ds(pl.multiple_of(which * span, span), span)
        height = sources[k].shape[0]
        if k == count:
            return targets[k].at[:, lanes]
        row = pieces[k] + rep * height
        return targets[k].at[pl.ds(pl.multiple_of(row, 16), height), lanes]

    def band(k, which):
        height = sources[k].shape[0]
        row = pieces[k] + which * height
        return targets[k].at[pl.ds(pl.multiple_of(row, 16), height), :]

    barrier = pltpu.get_barrier_semaphore()
    for step in range(1, shards):
        pl.semaphore_signal(
            barrier, inc=1, device_id={"shard": lax.rem(shard + step, shards)}, device_id_type=MESH
        )
    for step in range(1, chips):
        to = lax.rem(chip + step, chips) * 2 + core
        pl.semaphore_signal(barrier, inc=1, device_id={"rep": to}, device_id_type=MESH)
    pl.semaphore_signal(barrier, inc=1, device_id={"rep": rep + 1 - 2 * core}, device_id_type=MESH)
    pl.semaphore_wait(barrier, shards - 1 + chips)

    locals_ = []
    for k in range(total):
        copy = pltpu.make_async_copy(sources[k], slot(k, shard), local_sem.at[k])
        copy.start()
        locals_.append(copy)

    def up_copy(k, step):
        source = sources[k] if step == 0 else slot(k, shard - step)
        return pltpu.make_async_remote_copy(
            src_ref=source,
            dst_ref=slot(k, shard - step),
            send_sem=up_send.at[k, step],
            recv_sem=up_recv.at[k, step],
            device_id={"shard": lax.rem(shard + 1, shards)},
            device_id_type=MESH,
        )

    def down_copy(k, step):
        source = sources[k] if step == 0 else slot(k, shard + step)
        return pltpu.make_async_remote_copy(
            src_ref=source,
            dst_ref=slot(k, shard + step),
            send_sem=down_send.at[k, step],
            recv_sem=down_recv.at[k, step],
            device_id={"shard": lax.rem(shard + shards - 1, shards)},
            device_id_type=MESH,
        )

    def line_step(group, step):
        @pl.when((shard < shards - 1) & (step <= shard))
        def _():
            for k in group:
                up_copy(k, step).start()

        @pl.when((shard > 0) & (step <= shards - 1 - shard))
        def _():
            for k in group:
                down_copy(k, step).start()

    def line_arrive(group, step):
        @pl.when(step <= shard - 1)
        def _():
            for k in group:
                pltpu.make_async_remote_copy(
                    src_ref=slot(k, shard - 1 - step),
                    dst_ref=slot(k, shard - 1 - step),
                    send_sem=up_send.at[k, step],
                    recv_sem=up_recv.at[k, step],
                    device_id={"shard": lax.rem(shard + 1, shards)},
                    device_id_type=MESH,
                ).wait_recv()

        @pl.when(step <= shards - 2 - shard)
        def _():
            for k in group:
                pltpu.make_async_remote_copy(
                    src_ref=slot(k, shard + 1 + step),
                    dst_ref=slot(k, shard + 1 + step),
                    send_sem=down_send.at[k, step],
                    recv_sem=down_recv.at[k, step],
                    device_id={"shard": lax.rem(shard + 1, shards)},
                    device_id_type=MESH,
                ).wait_recv()

    def line_sent(group, step):
        @pl.when((shard < shards - 1) & (step <= shard))
        def _():
            for k in group:
                up_copy(k, step).wait_send()

        @pl.when((shard > 0) & (step <= shards - 1 - shard))
        def _():
            for k in group:
                down_copy(k, step).wait_send()

    first = list(range(count + 1))
    later = list(range(count + 1, total))
    for step in range(shards - 1):
        line_step(first, step)
        line_arrive(first, step)
    line_step(later, 0)
    for copy in locals_:
        copy.wait()

    def chip_copy(k, step):
        to = lax.rem(chip + step, chips) * 2 + core
        return pltpu.make_async_remote_copy(
            src_ref=band(k, rep),
            dst_ref=band(k, rep),
            send_sem=chip_send.at[k, step - 1],
            recv_sem=chip_recv.at[k, step - 1],
            device_id={"rep": to},
            device_id_type=MESH,
        )

    def core_copy(k, step):
        owner = lax.rem(chip + chips - step, chips) * 2 + core
        return pltpu.make_async_remote_copy(
            src_ref=band(k, owner),
            dst_ref=band(k, owner),
            send_sem=core_send.at[k, step],
            recv_sem=core_recv.at[k, step],
            device_id={"rep": rep + 1 - 2 * core},
            device_id_type=MESH,
        )

    for step in range(1, chips):
        for k in range(count):
            chip_copy(k, step).start()
    for k in range(count):
        core_copy(k, 0).start()
    for step in range(1, shards - 1):
        line_arrive(later, step - 1)
        line_step(later, step)
    for step in range(1, chips):
        for k in range(count):
            chip_copy(k, step).wait_recv()
            core_copy(k, step).start()
    if shards > 1:
        line_arrive(later, shards - 2)
    for step in range(chips):
        for k in range(count):
            core_copy(k, step).wait()
            if step:
                chip_copy(k, step).wait_send()
    for step in range(shards - 1):
        line_sent(first + later, step)


def open_gather(reps, shards, bands, small, lines):
    operands = [operand for _, operand in bands] + [small] + list(lines)
    dma = pltpu.SemaphoreType.DMA
    count, total, chips = len(bands), len(operands), reps // 2
    span = small.shape[1]
    shapes = [struct((reps * operand.shape[0], shards * span), BF16) for _, operand in bands]
    shapes.append(struct((small.shape[0], shards * span), BF16))
    shapes += [struct((shards, *line.shape), BF16) for line in lines]
    anywhere = pl.BlockSpec(memory_space=pl.ANY)
    return pl.pallas_call(
        functools.partial(open_kernel, reps, shards, [at for at, _ in bands], len(lines)),
        in_specs=[anywhere] * total,
        out_specs=[anywhere] * total,
        out_shape=shapes,
        scratch_shapes=[
            dma((total,)),
            dma((total, shards - 1)),
            dma((total, shards - 1)),
            dma((total, shards - 1)),
            dma((total, shards - 1)),
            dma((count, chips)),
            dma((count, chips)),
            dma((count, chips)),
            dma((count, chips)),
        ],
        compiler_params=params(collective_id=4, has_side_effects=True),
        name="open_gather",
    )(*operands)


def left_parts_kernel(
    shards, rows, wide, first_ref, joint_ref, mixed_ref, middle_ref, sq_ref, sk_ref, sv_ref, so_ref,
    eq_ref, ep_ref, eo_ref, router_ref, gains_ref, z_ref, own_ref,
):
    qw, kv = sq_ref.shape[1], sk_ref.shape[1]
    first = first_ref[...]
    pieces = []
    for start_ref, low in ((sq_ref, 0), (sk_ref, qw), (sv_ref, qw + kv)):
        high = low + start_ref.shape[1]
        pieces.append(exact_nn(exact_nt(start_ref[...], joint_ref[:, low:high]), first))
    pieces.append(exact_nn(exact_nt(so_ref[...], middle_ref[...]), mixed_ref[...]))
    pieces.append(router_ref[...])
    pieces.append(gains_ref[...])
    for shard in range(shards):
        for k, piece in enumerate(pieces):
            z_ref[shard, :, k * wide : (k + 1) * wide] = padded(
                piece[:, shard * rows : (shard + 1) * rows], wide
            )
    errors = (
        start_product(sq_ref[...], eq_ref[...]),
        start_product(sk_ref[...], ep_ref[0]),
        start_product(sv_ref[...], ep_ref[1]),
        start_product(so_ref[...], eo_ref[...]),
    )
    for k, piece in enumerate(errors):
        own_ref[:, k * wide : (k + 1) * wide] = padded(piece, wide)


def left_parts(shards, rows, operands):
    wide = up_to(rows, 128)
    return pl.pallas_call(
        functools.partial(left_parts_kernel, shards, rows, wide),
        in_specs=vmem_specs(len(operands)),
        out_specs=vmem_specs(2),
        out_shape=[struct((shards, 8, 6 * wide)), struct((8, 4 * wide))],
        compiler_params=params(),
        name="left_parts",
    )(*operands)


def greet(reps, shards):
    rep, shard = lax.axis_index("rep"), lax.axis_index("shard")
    barrier = pltpu.get_barrier_semaphore()
    for step in range(1, shards):
        pl.semaphore_signal(
            barrier, inc=1, device_id={"shard": lax.rem(shard + step, shards)}, device_id_type=MESH
        )
    for step in range(1, reps):
        pl.semaphore_signal(
            barrier, inc=1, device_id={"rep": lax.rem(rep + step, reps)}, device_id_type=MESH
        )
    pl.semaphore_wait(barrier, reps + shards - 2)


def start_all(axis, size, source, target, send, recv):
    here = lax.axis_index(axis)
    copies = []
    for step in range(1, size):
        to = lax.rem(here + step, size)
        copy = pltpu.make_async_remote_copy(
            src_ref=source(to),
            dst_ref=target(step),
            send_sem=send.at[step - 1],
            recv_sem=recv.at[step - 1],
            device_id={axis: to},
            device_id_type=MESH,
        )
        copy.start()
        copies.append(copy)
    return copies


def send_all(axis, size, source, target, send, recv):
    for copy in start_all(axis, size, source, target, send, recv):
        copy.wait()


def blocks_on_diagonal(square):
    size = square.shape[0]
    row = lax.broadcasted_iota(jnp.int32, (size, size), 0) // 8
    lane = lax.broadcasted_iota(jnp.int32, (size, size), 1) // 8
    kept = jnp.where(row == lane, square, 0.0)
    total = kept[:8]
    for k in range(1, size // 8):
        total = total + kept[8 * k : 8 * k + 8]
    return total


def spread_on_diagonal(flat):
    size = flat.shape[1]
    tall = jnp.concatenate([flat] * (size // 8), axis=0)
    row = lax.broadcasted_iota(jnp.int32, (size, size), 0) // 8
    lane = lax.broadcasted_iota(jnp.int32, (size, size), 1) // 8
    return jnp.transpose(jnp.where(row == lane, tall, 0.0))


def left_sync_kernel(reps, shards, wide, wide_out, piece, count, *refs):
    z_ref, own_ref = refs[:2]
    lin_refs, lout_refs = refs[2 : 2 + count], refs[2 + count : 2 + 2 * count]
    left_ref, left_out_ref, totals_ref, squares_ref, leftz_ref = refs[2 + 2 * count : 7 + 2 * count]
    (zbuf, parts, heard, total, grams, lanes_z, zs, zr, ps, pr, gs, gr, hs, hr, ls, lr) = refs[
        7 + 2 * count :
    ]
    rep, shard = lax.axis_index("rep"), lax.axis_index("shard")
    greet(reps, shards)
    send_all("shard", shards, lambda to: z_ref.at[to], lambda step: zbuf.at[step - 1], zs, zr)
    front = z_ref[shard]
    for step in range(shards - 1):
        front = front + zbuf[step]
    ins = [ref[e, a] for a in range(2) for ref in lin_refs for e in range(ref.shape[0])]
    outs = [ref[e] for ref in lout_refs for e in range(ref.shape[0])]
    line = jnp.concatenate(
        [front[:, : 4 * wide] + own_ref[...], front[:, 4 * wide :], *ins, *outs], axis=1
    )
    line = padded(line, reps * piece)
    for k in range(reps):
        parts[k] = line[:, k * piece : (k + 1) * piece]
    send_all("rep", reps, lambda to: parts.at[to], lambda step: heard.at[step - 1], ps, pr)
    mine = parts[rep]
    for step in range(reps - 1):
        mine = mine + heard[step]
    total[rep] = mine
    send_all("rep", reps, lambda to: total.at[rep], lambda step: total.at[rep], gs, gr)
    line = jnp.concatenate([total[k] for k in range(reps)], axis=1)
    inner = len(ins)
    matrices = [line[:, k * wide : (k + 1) * wide] for k in range(4)]
    matrices += [line[:, (6 + k) * wide : (7 + k) * wide] for k in range(inner)]
    base = (6 + inner) * wide
    outers = [line[:, base + k * wide_out : base + (k + 1) * wide_out] for k in range(len(outs))]
    router, gains = line[:, 4 * wide : 5 * wide], line[:, 5 * wide : 6 * wide]
    size, size_out = up_to(8 * len(matrices), 128), up_to(8 * len(outers), 128)
    stack = jnp.concatenate(
        matrices + [jnp.zeros((size - 8 * len(matrices), wide), F32)], axis=0
    )
    stack_out = jnp.concatenate(
        outers + [jnp.zeros((size_out - 8 * len(outers), wide_out), F32)], axis=0
    )
    gram = blocks_on_diagonal(nt(stack, stack, HIGHEST))
    gram_out = blocks_on_diagonal(nt(stack_out, stack_out, HIGHEST))
    row = lax.broadcasted_iota(jnp.int32, (8, 128), 0)
    lane = lax.broadcasted_iota(jnp.int32, (8, 128), 1)
    more = jnp.where(lane == 0, jnp.sum(router * router, axis=1, keepdims=True), 0.0)
    more = jnp.where(lane == 1, jnp.sum(gains * gains, axis=1, keepdims=True), more)
    grams[shard] = jnp.concatenate([gram, gram_out, more], axis=1)
    lanes_z[shard] = stack[:32]
    sent = start_all("shard", shards, lambda to: grams.at[shard], lambda step: grams.at[shard], hs, hr)
    sent += start_all(
        "shard", shards, lambda to: lanes_z.at[shard], lambda step: lanes_z.at[shard], ls, lr
    )
    for copy in sent:
        copy.wait()
    gram = grams[0]
    for k in range(1, shards):
        gram = gram + grams[k]
    both = size + size_out
    squares_ref[...] = gram[:, both:]
    totals_ref[0] = router
    totals_ref[1] = gains
    where_from = lax.broadcasted_iota(jnp.int32, (both, 1024), 0)
    where_to = lax.broadcasted_iota(jnp.int32, (both, 1024), 1)
    chosen = jnp.where(
        (where_from % 8 == where_to // 128) & (where_from // 8 == where_to % 128), 1.0, 0.0
    ).astype(BF16)
    lines = exact_nn(gram[:, :both], chosen)
    used = (lane < len(matrices)) | ((lane >= size // 8) & (lane < size // 8 + len(outers)))
    table = [
        jnp.where(used, lines[:, 128 * k : 128 * k + 128], jnp.where(row == k, 1.0, 0.0))
        for k in range(8)
    ]
    inverse = [jnp.where(row == k, 1.0, 0.0) for k in range(8)]
    for k in range(8):
        pivot = table[k][k : k + 1]
        over = 1.0 / pivot
        for i in range(k + 1, 8):
            factor = table[i][k : k + 1] * over
            table[i] = table[i] - factor * table[k]
            inverse[i] = inverse[i] - factor * inverse[k]
        inverse[k] = inverse[k] / jnp.sqrt(pivot)
    flat = exact_nt(jnp.concatenate(inverse, axis=1), chosen)
    solve = spread_on_diagonal(flat[:, :size])
    lefts = nn(solve, stack, HIGHEST)
    lefts_out = nn(spread_on_diagonal(flat[:, size:]), stack_out, HIGHEST)
    left_ref[...] = lefts[: left_ref.shape[0]]
    left_out_ref[...] = lefts_out[: left_out_ref.shape[0]]
    for k in range(shards):
        leftz_ref[k] = nn(solve[:32, :32], lanes_z[k], HIGHEST)


def left_sync(reps, shards, z_part, own, lins, louts):
    wide, wide_out = lins[0].shape[3], louts[0].shape[2]
    inner, outer = 2 * sum(x.shape[0] for x in lins), sum(x.shape[0] for x in louts)
    piece = up_to(-(-((6 + inner) * wide + outer * wide_out) // reps), 128)
    matrices = 4 + inner
    size, size_out = up_to(8 * matrices, 128), up_to(8 * outer, 128)
    dma = pltpu.SemaphoreType.DMA
    operands = [z_part, own, *lins, *louts]
    return pl.pallas_call(
        functools.partial(left_sync_kernel, reps, shards, wide, wide_out, piece, len(lins)),
        in_specs=vmem_specs(len(operands)),
        out_specs=vmem_specs(5),
        out_shape=[
            struct((8 * matrices, wide)),
            struct((8 * outer, wide_out)),
            struct((2, 8, wide)),
            struct((8, 128)),
            struct((shards, 32, wide)),
        ],
        scratch_shapes=[
            pltpu.VMEM((shards - 1, 8, 6 * wide), F32),
            pltpu.VMEM((reps, 8, piece), F32),
            pltpu.VMEM((reps - 1, 8, piece), F32),
            pltpu.VMEM((reps, 8, piece), F32),
            pltpu.VMEM((shards, 8, size + size_out + 128), F32),
            pltpu.VMEM((shards, 32, wide), F32),
            dma((shards - 1,)),
            dma((shards - 1,)),
            dma((reps - 1,)),
            dma((reps - 1,)),
            dma((reps - 1,)),
            dma((reps - 1,)),
            dma((shards - 1,)),
            dma((shards - 1,)),
            dma((shards - 1,)),
            dma((shards - 1,)),
        ],
        compiler_params=params(collective_id=1, has_side_effects=True),
        name="left_sync",
    )(*operands)


def left_product(left, matrix):
    high, low = two_terms(left)
    both = jnp.concatenate([high.astype(F32), low.astype(F32)], axis=0).astype(BF16)
    top, rest = two_terms(matrix)
    first = nn(both, top)
    return first[:8] + first[8:] + nn(both, rest)[:8]


def right_expert_kernel(left_ref, left_out_ref, min_ref, mout_ref, right_ref):
    rows, out_rows = min_ref.shape[2], mout_ref.shape[1]
    hidden = min_ref.shape[3]

    for a in range(2):
        right_ref[0, :, a * hidden : (a + 1) * hidden] = left_product(
            left_ref[a, 0, :, :rows], min_ref[a, 0]
        )
    right_ref[0, :, 2 * hidden :] = left_product(left_out_ref[0, :, :out_rows], mout_ref[0])


def right_experts(first_expert, lefts, lefts_out, merged_in, merged_out):
    count, rows, hidden = merged_in.shape[1:]
    out_rows, width = merged_out.shape[1:]
    wide, wide_out = lefts.shape[3], lefts_out.shape[2]
    return pl.pallas_call(
        right_expert_kernel,
        grid=(count,),
        in_specs=[
            pl.BlockSpec((2, 1, 8, wide), lambda e: (0, first_expert + e, 0, 0)),
            pl.BlockSpec((1, 8, wide_out), lambda e: (first_expert + e, 0, 0)),
            pl.BlockSpec((2, 1, rows, hidden), lambda e: (0, e, 0, 0)),
            pl.BlockSpec((1, out_rows, width), lambda e: (e, 0, 0)),
        ],
        out_specs=pl.BlockSpec((1, 8, 2 * hidden + width), lambda e: (e, 0, 0)),
        out_shape=struct((count, 8, 2 * hidden + width)),
        compiler_params=params(),
        name="right_experts",
    )(lefts, lefts_out, merged_in, merged_out)


def right_attention_kernel(
    shards, rows, left_ref, leftz_ref, first_ref, joint_ref, mixed_ref, middle_ref, eq_ref, ep_ref,
    eo_ref, right_ref,
):
    qw, kv = eq_ref.shape[1], ep_ref.shape[2]
    width = eo_ref.shape[1]

    def whole(k):
        return jnp.concatenate(
            [leftz_ref[z, 8 * k : 8 * k + 8, :rows] for z in range(shards)], axis=1
        )

    def own(k):
        return left_ref[8 * k : 8 * k + 8, :rows]

    first = first_ref[...]
    at = 0
    for k, error in ((0, eq_ref[...]), (1, ep_ref[0]), (2, ep_ref[1])):
        grown = exact_nn(exact_nt(whole(k), first), joint_ref[:, at : at + error.shape[1]])
        right_ref[:, at : at + error.shape[1]] = grown + left_product(own(k), error)
        at += error.shape[1]
    grown = exact_nn(exact_nt(whole(3), mixed_ref[...]), middle_ref[...])
    right_ref[:, at : at + width] = grown + left_product(own(3), eo_ref[...])


def right_attention(shards, rows, operands):
    width = operands[6].shape[1] + 2 * operands[7].shape[2] + operands[8].shape[1]
    return pl.pallas_call(
        functools.partial(right_attention_kernel, shards, rows),
        in_specs=vmem_specs(len(operands)),
        out_specs=pl.BlockSpec(memory_space=pltpu.VMEM),
        out_shape=struct((8, width)),
        compiler_params=params(),
        name="right_attention",
    )(*operands)


def right_sync_kernel(reps, shards, piece, count, *refs):
    experts_refs, attention_ref, out_ref = refs[:count], refs[count], refs[count + 1]
    parts, heard, across, total, ps, pr, zs, zr, gs, gr = refs[count + 2 :]
    rep, shard = lax.axis_index("rep"), lax.axis_index("shard")
    half = piece // 2
    greet(reps, shards)
    line = jnp.concatenate(
        [ref[e] for ref in experts_refs for e in range(ref.shape[0])] + [attention_ref[...]], axis=1
    )
    line = padded(line, reps * piece)
    for k in range(reps):
        at = k * piece
        parts[k] = jnp.concatenate(
            [line[:, at : at + half], line[:, at + half : at + piece]], axis=0
        ).astype(BF16)
    send_all("rep", reps, lambda to: parts.at[to], lambda step: heard.at[step - 1], ps, pr)
    mine = parts[rep].astype(F32)
    for step in range(reps - 1):
        mine = mine + heard[step].astype(F32)
    across[shard] = mine.astype(BF16)
    send_all("shard", shards, lambda to: across.at[shard], lambda step: across.at[shard], zs, zr)
    summed = across[0].astype(F32)
    for k in range(1, shards):
        summed = summed + across[k].astype(F32)
    total[rep] = summed.astype(BF16)
    send_all("rep", reps, lambda to: total.at[rep], lambda step: total.at[rep], gs, gr)
    for k in range(reps):
        block = total[k].astype(F32)
        out_ref[:, k * piece : k * piece + half] = block[:8]
        out_ref[:, k * piece + half : (k + 1) * piece] = block[8:]


def right_sync(reps, shards, experts, attention):
    columns = sum(part.shape[0] * part.shape[2] for part in experts) + attention.shape[1]
    piece = up_to(-(-columns // reps), 256)
    dma = pltpu.SemaphoreType.DMA
    return pl.pallas_call(
        functools.partial(right_sync_kernel, reps, shards, piece, len(experts)),
        in_specs=vmem_specs(len(experts) + 1),
        out_specs=pl.BlockSpec(memory_space=pltpu.VMEM),
        out_shape=struct((8, reps * piece)),
        scratch_shapes=[
            pltpu.VMEM((reps, 16, piece // 2), BF16),
            pltpu.VMEM((reps - 1, 16, piece // 2), BF16),
            pltpu.VMEM((shards, 16, piece // 2), BF16),
            pltpu.VMEM((reps, 16, piece // 2), BF16),
            dma((reps - 1,)),
            dma((reps - 1,)),
            dma((shards - 1,)),
            dma((shards - 1,)),
            dma((reps - 1,)),
            dma((reps - 1,)),
        ],
        compiler_params=params(collective_id=2, has_side_effects=True),
        name="right_sync",
    )(*experts, attention)


def low_rank(left, right):
    high, low = two_terms(left)
    lefts = jnp.concatenate([high.astype(F32), low.astype(F32)], axis=0).astype(BF16)
    rights = jnp.concatenate([right, right], axis=0).astype(BF16)
    return tn(lefts, rights)


def feedback_expert_kernel(
    replicas, first_expert, left_ref, left_out_ref, right_ref, min_ref, mout_ref, *rest
):
    fin_ref, fout_ref, sq_ref = rest[-3:]
    rows, hidden = min_ref.shape[2:]
    out_rows = mout_ref.shape[1]
    row = lax.broadcasted_iota(jnp.int32, (8, 128), 0)
    lane = lax.broadcasted_iota(jnp.int32, (8, 128), 1)

    @pl.when(pl.program_id(0) == 0)
    def _():
        sq_ref[...] = jnp.zeros_like(sq_ref)

    added = jnp.zeros((8, 128), F32)
    for a in range(2):
        approx = low_rank(
            left_ref[a, 0, :, :rows], right_ref[:, a * hidden : (a + 1) * hidden]
        )
        left_over = min_ref[a, 0] - approx * (1.0 / replicas)
        fin_ref[a, 0] = left_over
        added = jnp.where(lane == a, jnp.sum(left_over * left_over), added)
    approx = low_rank(left_out_ref[0, :, :out_rows], right_ref[:, 2 * hidden :])
    left_over = mout_ref[0] - approx * (1.0 / replicas)
    fout_ref[0] = left_over
    added = jnp.where(lane == 2, jnp.sum(left_over * left_over), added)
    sq_ref[...] += jnp.where(row == first_expert + pl.program_id(0), added, 0.0)


def feedback_experts(
    replicas, first_expert, lefts, lefts_out, rights, merged_in, merged_out, whole_in, whole_out
):
    count, rows, hidden = merged_in.shape[1:]
    out_rows, width = merged_out.shape[1:]
    wide, wide_out = lefts.shape[3], lefts_out.shape[2]
    shapes = (2, E, rows, hidden), (E, out_rows, width)
    operands = [lefts, lefts_out, rights, merged_in, merged_out]
    in_specs = [
        pl.BlockSpec((2, 1, 8, wide), lambda e: (0, first_expert + e, 0, 0)),
        pl.BlockSpec((1, 8, wide_out), lambda e: (first_expert + e, 0, 0)),
        pl.BlockSpec((8, 2 * hidden + width), lambda e: (0, first_expert + e)),
        *matrix_blocks(0, merged_in.shape, merged_out.shape),
    ]
    aliases = {}
    if whole_in is not None:
        operands += [whole_in, whole_out]
        in_specs += [pl.BlockSpec(memory_space=pl.ANY)] * 2
        aliases = {5: 0, 6: 1}
    return pl.pallas_call(
        functools.partial(feedback_expert_kernel, replicas, first_expert),
        grid=(count,),
        in_specs=in_specs,
        out_specs=[
            *matrix_blocks(first_expert, *shapes),
            pl.BlockSpec((8, 128), lambda e: (0, 0)),
        ],
        out_shape=[struct(shapes[0]), struct(shapes[1]), struct((8, 128))],
        input_output_aliases=aliases,
        compiler_params=params(),
        name="feedback_experts",
    )(*operands)


def feedback_attention_kernel(
    replicas, rows, left_ref, right_ref, gj_ref, go_ref, eq_ref, ep_ref, eo_ref, fq_ref, fp_ref,
    fo_ref, sq_ref,
):
    qw, kv = eq_ref.shape[1], ep_ref.shape[2]
    lane = lax.broadcasted_iota(jnp.int32, (8, 128), 1)
    row = lax.broadcasted_iota(jnp.int32, (8, 128), 0)
    added = jnp.zeros((8, 128), F32)
    at = 0
    jobs = (
        (gj_ref, 0, eq_ref, fq_ref),
        (gj_ref, qw, ep_ref.at[0], fp_ref.at[0]),
        (gj_ref, qw + kv, ep_ref.at[1], fp_ref.at[1]),
        (go_ref, 0, eo_ref, fo_ref),
    )
    for k, (grad_ref, low, error_ref, out_ref) in enumerate(jobs):
        width = error_ref.shape[1]
        approx = low_rank(left_ref[8 * k : 8 * k + 8, :rows], right_ref[:, at : at + width])
        merged = grad_ref[:, low : low + width].astype(F32) + error_ref[...]
        left_over = merged - approx * (1.0 / replicas)
        out_ref[...] = left_over
        added = jnp.where(lane == 3 + k, jnp.sum(left_over * left_over), added)
        at += width
    sq_ref[...] = jnp.where(row == 0, added, 0.0)


def feedback_attention(replicas, rows, operands):
    shapes = [operands[k].shape for k in (4, 5, 6)]
    return pl.pallas_call(
        functools.partial(feedback_attention_kernel, replicas, rows),
        in_specs=vmem_specs(len(operands)),
        out_specs=vmem_specs(4),
        out_shape=[struct(shape) for shape in shapes] + [struct((8, 128))],
        compiler_params=params(),
        name="feedback_attention",
    )(*operands)


def squares_sync_kernel(reps, shards, count, *refs):
    out_ref, plane, line, ps, pr, zs, zr = refs[count:]
    rep, shard = lax.axis_index("rep"), lax.axis_index("shard")
    greet(reps, shards)
    added = refs[0][...]
    for ref in refs[1:count]:
        added = added + ref[...]
    plane[rep] = added
    send_all("rep", reps, lambda to: plane.at[rep], lambda step: plane.at[rep], ps, pr)
    summed = plane[0]
    for k in range(1, reps):
        summed = summed + plane[k]
    line[shard] = summed
    send_all("shard", shards, lambda to: line.at[shard], lambda step: line.at[shard], zs, zr)
    summed = line[0]
    for k in range(1, shards):
        summed = summed + line[k]
    out_ref[...] = summed


def squares_sync(reps, shards, parts):
    dma = pltpu.SemaphoreType.DMA
    return pl.pallas_call(
        functools.partial(squares_sync_kernel, reps, shards, len(parts)),
        in_specs=vmem_specs(len(parts)),
        out_specs=pl.BlockSpec(memory_space=pltpu.VMEM),
        out_shape=struct((8, 128)),
        scratch_shapes=[
            pltpu.VMEM((reps, 8, 128), F32),
            pltpu.VMEM((shards, 8, 128), F32),
            dma((reps - 1,)),
            dma((reps - 1,)),
            dma((shards - 1,)),
            dma((shards - 1,)),
        ],
        compiler_params=params(collective_id=3, has_side_effects=True),
        name="squares_sync",
    )(*parts)


def per_device(
    tokens,
    cotangent,
    seg_ids,
    parents,
    positions,
    routes,
    query_weight,
    pair_weight,
    output_weight,
    inner_weight,
    outer_weight,
    router_weight,
    norm_gains,
    query_moment,
    pair_moment,
    output_moment,
    inner_moment,
    outer_moment,
    router_moment,
    gains_moment,
    query_error,
    pair_error,
    output_error,
    inner_error,
    outer_error,
    query_start,
    pair_start,
    output_start,
    inner_start,
    outer_start,
):
    replicas = lax.axis_size("rep")
    shard_count = lax.axis_size("shard")
    here = lax.axis_index("shard")
    both = ("rep", "shard")
    bf16 = jnp.bfloat16
    query_t = jnp.swapaxes(query_weight, 0, 1).astype(bf16)
    pair_t = jnp.swapaxes(pair_weight, 1, 2).astype(bf16)
    output_t = jnp.swapaxes(output_weight, 0, 1).astype(bf16)
    inner_t = jnp.transpose(inner_weight, (1, 0, 3, 2)).astype(bf16)
    outer_low = outer_weight.astype(bf16)
    router_t = jnp.swapaxes(router_weight, 0, 1).astype(bf16)
    gains_low = norm_gains.astype(bf16)
    own_rows = query_t.shape[1]
    q_cols, p_cols, f_cols = query_t.shape[0], pair_t.shape[1], inner_t.shape[2]
    f_rows = outer_low.shape[1]
    small = jnp.concatenate([router_t, gains_low], axis=0)
    small = jnp.pad(small, ((0, 16 - small.shape[0]), (0, 0)))
    per_chunk = E // CHUNKS
    outer_cols = outer_low.shape[2]
    paired = replicas % 2 == 0 and per_chunk == 2 and own_rows == 2 * outer_cols == 2 * f_rows
    paired = paired and 2 * f_cols == f_rows and own_rows % 128 == 0
    paired = paired and q_cols % 16 == 0 and p_cols % 16 == 0 and f_cols % 16 == 0

    def whole_weights(inner_all, outer_all):
        inner_all = inner_all.reshape(replicas, shard_count, per_chunk, 2, f_cols, own_rows)
        w1 = jnp.transpose(inner_all, (2, 3, 0, 4, 1, 5)).reshape(
            1, 1, per_chunk, 2 * replicas * f_cols, shard_count * own_rows
        )
        w2 = jnp.transpose(outer_all, (2, 1, 3, 0, 4)).reshape(
            1, per_chunk, 1, 1, shard_count * f_rows, replicas * outer_cols
        )
        return w1, w2, False

    cot_t = jnp.transpose(cotangent)
    chunk_weights = []
    if paired:
        core = lax.axis_index("rep") % 2
        outer_pairs = outer_low.reshape(CHUNKS, 2, f_rows, outer_cols)
        keep = jnp.where(core == 0, outer_pairs[:, 0], outer_pairs[:, 1])
        give = jnp.where(core == 0, outer_pairs[:, 1], outer_pairs[:, 0])
        got = lax.ppermute(give, "rep", [(i, i + 1 - 2 * (i % 2)) for i in range(replicas)])
        wide_outer = jnp.concatenate(
            [jnp.where(core == 0, keep, got), jnp.where(core == 0, got, keep)], axis=2
        )
        inner_packs = inner_t.reshape(CHUNKS, per_chunk * 2 * f_cols, own_rows)
        packs = [
            jnp.concatenate([inner_packs[k], wide_outer[k]], axis=0) for k in range(CHUNKS)
        ]
        opened = open_gather(
            replicas,
            shard_count,
            [(0, query_t), (0, pair_t[0]), (0, pair_t[1]), (0, output_t)],
            small,
            packs[:1],
        )
        query_full, key_full, value_full, output_full, small_full = opened[:5]
        height = packs[0].shape[0]
        near = z_slots(packs[1])
        first_line = opened[5]
    else:
        packed = jnp.concatenate(
            [query_t, pair_t.reshape(2 * p_cols, own_rows), output_t, small], axis=0
        )
        spread = lax.all_gather(packed, both).reshape(
            replicas, shard_count, packed.shape[0], own_rows
        )

        def joined(low, high):
            piece = jnp.transpose(spread[:, :, low:high], (0, 2, 1, 3))
            return piece.reshape(-1, shard_count * own_rows)

        at = q_cols + 2 * p_cols
        query_full = joined(0, q_cols)
        key_full, value_full = joined(q_cols, q_cols + p_cols), joined(q_cols + p_cols, at)
        output_full = joined(at, at + q_cols)
        small_full = joined(at + q_cols, packed.shape[0])[: small.shape[0]]
        for index in range(CHUNKS):
            span = slice(index * per_chunk, (index + 1) * per_chunk)
            chunk_weights.append(
                whole_weights(
                    lax.all_gather(inner_t[span], both),
                    lax.all_gather(outer_low[span], both).reshape(
                        replicas, shard_count, per_chunk, f_rows, outer_cols
                    ),
                )
            )
    router_full = small_full[:E]
    gain_values = small_full[E : E + 2].astype(jnp.float32)

    hidden = tokens.astype(jnp.float32)
    length = hidden.shape[0]
    position = positions[0]
    allowed = path_mask(seg_ids[0], parents[0])
    first_low = rms_norm(hidden, gain_values[0]).astype(bf16)
    half_head = HD // 2
    frequency = ROPE_BASE ** (-2.0 * jnp.arange(half_head, dtype=jnp.float32) / HD)
    angles = position.astype(jnp.float32)[:, None] * frequency[None, :]
    cosine = jnp.concatenate([jnp.cos(angles), jnp.cos(angles)], axis=1)
    sine = jnp.concatenate([-jnp.sin(angles), jnp.sin(angles)], axis=1)
    mask = allowed.astype(bf16)
    query_rot, key_rot, values, mixed_low, middle = attention_forward(
        (
            first_low, query_full, key_full, value_full, output_full, tokens, cosine, sine, mask,
        )
    )
    second_low = rms_norm(middle, gain_values[1]).astype(bf16)
    logits = jnp.einsum("td,ed->te", second_low, router_full, preferred_element_type=jnp.float32)
    expert_ids = jnp.arange(E, dtype=jnp.int32)
    route_mask = jnp.any(routes[:, :, None] == expert_ids[None, None, :], axis=1)
    route_top = jnp.max(jnp.where(route_mask, logits, -1e30), axis=-1, keepdims=True)
    raised_gate = jnp.where(route_mask, jnp.exp(logits - route_top), 0.0)
    shares = raised_gate / jnp.sum(raised_gate, axis=-1, keepdims=True)
    shares_t = jnp.transpose(shares)
    shares_high = shares_t.astype(bf16)
    shares_rest = (shares_t - shares_high.astype(jnp.float32)).astype(bf16)
    tree_x = jnp.concatenate([jnp.transpose(second_low), shares_high, shares_rest], axis=0)

    token = tree_x[:16, :128]
    far = None

    def gathered(line, turned):
        part = lax.all_gather(line, "rep")
        w1 = part.reshape(replicas, shard_count, 3, f_rows, own_rows)
        w2 = part.reshape(replicas // 2, 2, shard_count, 3, f_rows, own_rows)
        chunk_weights.append((w1, w2, turned))

    if paired:
        near, held, token = lax.optimization_barrier(
            (near, jnp.concatenate(packs[2:], axis=0), token)
        )
        far = z_slots(held)
        gathered(first_line, False)
        gathered(jnp.stack(near), True)

    upstream = cotangent.astype(jnp.float32)
    start_in = jnp.swapaxes(inner_start, 2, 3)
    start_out = jnp.swapaxes(outer_start, 1, 2)
    chunks = range(CHUNKS)
    merged_parts, lins, louts = [None] * CHUNKS, [None] * CHUNKS, [None] * CHUNKS
    y_parts, grad_parts, combine_parts = [None] * CHUNKS, [None] * CHUNKS, [None] * CHUNKS
    slots_x, slots_u = {}, {}
    state = {"gate": token, "x": tree_x, "u": cot_t}

    def exchange(step, held_x, held_u):
        ring = [(i, (i + step) % shard_count) for i in range(shard_count)]
        slots_x[step] = lax.ppermute(held_x, "shard", ring)
        slots_u[step] = lax.ppermute(held_u, "shard", ring)

    def own(index):
        done = own_experts(
            index * per_chunk,
            state["x"],
            state["u"],
            cotangent,
            chunk_weights[index],
            inner_error[0],
            outer_error[0],
            state["gate"],
        )
        merged_parts[index] = (done[0], done[1])
        y_parts[index], grad_parts[index] = done[2], done[3]
        combine_parts[index] = done[4][:, :, 0]
        state["gate"] = done[0][0, 0, :16, :128].astype(bf16)

    def others(index, steps, last):
        done = rest_experts(
            index * per_chunk,
            last,
            [slots_x[step] for step in steps],
            [slots_u[step] for step in steps],
            chunk_weights[index],
            start_in,
            start_out,
            *merged_parts[index],
            state["gate"],
        )
        merged_parts[index] = (done[0], done[1])
        if last:
            lins[index], louts[index] = done[2], done[3]
        state["gate"] = done[0][0, 0, :16, :128].astype(bf16)

    def all_others(index, steps):
        groups = [steps[at : at + 3] for at in range(0, len(steps), 3)]
        for group in groups:
            others(index, group, group is groups[-1])

    steps = list(range(1, shard_count))
    filled = shard_count == 4 and CHUNKS == 4
    def far_weights():
        lines, state["gate"] = lax.optimization_barrier((far, state["gate"]))
        lines = jnp.stack(lines)
        for k in range(CHUNKS - 2):
            gathered(lines[:, k * height : (k + 1) * height], True)

    def pass_on(ups, downs):
        forth = [(i, i + 1) for i in range(shard_count - 1)]
        back = [(i + 1, i) for i in range(shard_count - 1)]
        return (
            tuple(lax.ppermute(up, "shard", forth) for up in ups),
            tuple(lax.ppermute(down, "shard", back) for down in downs),
        )

    def not_before(pair):
        pair, state["gate"] = lax.optimization_barrier((pair, state["gate"]))
        return pair

    late = token
    if filled and paired:
        own(0)
        state["x"], state["u"] = held = not_before((state["x"], state["u"]))
        ups, downs = [held], [held]
        up, down = pass_on(held, held)
        ups.append(up)
        downs.append(down)
        far_weights()
        own(1)
        ups[1], downs[1] = not_before((ups[1], downs[1]))
        up, down = pass_on(ups[1], downs[1])
        ups.append(up)
        downs.append(down)
        slots_x[1], slots_u[1] = (jnp.where(here >= 1, ups[1][k], downs[1][k]) for k in range(2))
        others(0, [1], False)
        own(2)
        others(1, [1], False)
        ups[2], downs[2] = not_before((ups[2], downs[2]))
        up, down = pass_on(ups[2], downs[2])
        ups.append(up)
        downs.append(down)
        others(2, [1], False)
        own(3)
        slots_x[2], slots_u[2] = (
            jnp.where(here == 0, downs[2][k], jnp.where(here == 3, ups[2][k], downs[1][k]))
            for k in range(2)
        )
        slots_x[3], slots_u[3] = (
            jnp.where(
                here == 0,
                downs[3][k],
                jnp.where(here == 1, downs[2][k], jnp.where(here == 2, ups[2][k], ups[3][k])),
            )
            for k in range(2)
        )
        for array in (*ups[3], *downs[3]):
            late = late + array[:16, :128]
    else:
        if paired:
            far_weights()
        for step in steps:
            exchange(step, tree_x, cot_t)
        for index in chunks:
            own(index)
    combined = middle
    second_grad = grad_parts[0]
    for index in chunks:
        combined = combined + y_parts[index]
        if index:
            second_grad = second_grad + grad_parts[index]
    output = combined.astype(bf16)
    combine_grad = jnp.transpose(jnp.concatenate(combine_parts, axis=0))
    logit_low = (
        shares * (combine_grad - jnp.sum(shares * combine_grad, axis=-1, keepdims=True))
    ).astype(bf16)
    grad_router = jnp.einsum("td,te->de", second_low, logit_low, preferred_element_type=jnp.float32)
    second_grad = second_grad + jnp.einsum(
        "te,ed->td", logit_low, router_full, preferred_element_type=jnp.float32
    )
    _, second_pull = jax.vjp(rms_norm, middle, gain_values[1])
    middle_part, gain_two = second_pull(second_grad)
    middle_grad = upstream + middle_part
    middle_low = middle_grad.astype(bf16)
    grad_output = jnp.einsum("tq,td->qd", mixed_low, middle_low, preferred_element_type=jnp.float32)
    group_output = lax.psum_scatter(
        grad_output.astype(bf16), "shard", scatter_dimension=0, tiled=True
    )
    joint_grad = attention_backward(
        (middle_low, output_full, query_rot, key_rot, values, cosine, sine, mask, late)
    )
    grad_joint = jnp.einsum("td,tq->dq", first_low, joint_grad, preferred_element_type=jnp.float32)
    group_joint = lax.psum_scatter(
        grad_joint.astype(bf16), "shard", scatter_dimension=0, tiled=True
    )
    first_grad = (
        nn(joint_grad[:, :QW], query_full)
        + nn(joint_grad[:, QW : QW + HK * HD], key_full)
        + nn(joint_grad[:, QW + HK * HD :], value_full)
    )
    _, first_pull = jax.vjp(rms_norm, hidden, gain_values[0])
    hidden_part, gain_one = first_pull(first_grad)
    input_grad = (middle_grad + hidden_part).astype(bf16)
    grad_gains = jnp.stack([gain_one, gain_two])

    state["gate"] = joint_grad
    if filled and paired:
        others(3, [1, 2, 3], True)
        others(2, [2, 3], True)
        others(0, [2, 3], True)
        others(1, [2, 3], True)
    else:
        for index in chunks:
            all_others(index, steps)

    small_rows = [jnp.transpose(grad_router), jnp.pad(grad_gains, ((0, 6), (0, 0)))]
    start_q, start_o = jnp.transpose(query_start), jnp.transpose(output_start)
    start_p = jnp.swapaxes(pair_start, 1, 2)
    z_part, own_left = left_parts(
        shard_count,
        own_rows,
        (
            first_low, joint_grad, mixed_low, middle_low, start_q, start_p[0], start_p[1], start_o,
            query_error[0], pair_error[0], output_error[0], *small_rows,
        ),
    )
    left_flat, left_out_flat, totals, total_squares, left_lines = left_sync(
        replicas, shard_count, z_part, own_left, lins, louts
    )
    wide, wide_out = left_flat.shape[1], left_out_flat.shape[1]
    lefts = left_flat.reshape(-1, 8, wide)
    lefts_in = lefts[4:].reshape(2, E, 8, wide)
    lefts_out = left_out_flat.reshape(E, 8, wide_out)
    lefts_t = (
        lefts[0, :, :own_rows],
        lefts[1:3, :, :own_rows],
        lefts[3, :, :own_rows],
        lefts_in[..., :own_rows],
        lefts_out[..., :f_rows],
    )
    bases = tuple(jnp.swapaxes(left, -1, -2) for left in lefts_t)

    right_parts = [
        right_experts(index * per_chunk, lefts_in, lefts_out, *merged_parts[index])
        for index in range(CHUNKS)
    ]
    right_rest = right_attention(
        shard_count,
        own_rows,
        (
            left_flat[:32], left_lines, first_low, joint_grad, mixed_low, middle_low,
            query_error[0], pair_error[0], output_error[0],
        ),
    )
    rights = right_sync(replicas, shard_count, right_parts, right_rest)
    hidden_units = inner_error.shape[4]
    step = 2 * hidden_units + D
    by_expert = rights[:, : E * step].reshape(8, E, step)
    rest = rights[:, E * step :]
    kv = HK * HD
    rights_t = (
        rest[:, :QW],
        jnp.stack([rest[:, QW : QW + kv], rest[:, QW + kv : QW + 2 * kv]]),
        rest[:, QW + 2 * kv : QW + 2 * kv + D],
        jnp.transpose(by_expert[:, :, : 2 * hidden_units].reshape(8, E, 2, hidden_units), (2, 1, 0, 3)),
        jnp.transpose(by_expert[:, :, 2 * hidden_units :], (1, 0, 2)),
    )
    right_out = tuple(jnp.swapaxes(right, -1, -2) for right in rights_t)

    feedback_in = feedback_out = None
    squares_experts = []
    for index in range(CHUNKS):
        feedback_in, feedback_out, part = feedback_experts(
            replicas, index * per_chunk, lefts_in, lefts_out, rights, *merged_parts[index],
            feedback_in, feedback_out,
        )
        squares_experts.append(part)
    feedback_q, feedback_p, feedback_o, squares_rest = feedback_attention(
        replicas,
        own_rows,
        (
            left_flat[:32], rest[:, : QW + 2 * kv + D], group_joint, group_output,
            query_error[0], pair_error[0], output_error[0],
        ),
    )
    feedbacks = tuple(
        part[None] for part in (feedback_q, feedback_p, feedback_o, feedback_in, feedback_out)
    )
    squares = squares_sync(replicas, shard_count, squares_experts + [squares_rest])
    flat_squares = jnp.concatenate(
        [squares[0, 3:7], squares[:, 0], squares[:, 1], squares[:, 2]], axis=0
    )

    column_index = lax.axis_index("rep")
    weights_now = (query_weight, pair_weight, output_weight, inner_weight, outer_weight)
    moments_now = (query_moment, pair_moment, output_moment, inner_moment, outer_moment)
    step_rates = (
        STEP_RATE * D ** (-0.5),
        STEP_RATE * D ** (-0.5),
        STEP_RATE * (QW * 4 // TOK_DEV + 1) ** (-0.5),
        STEP_RATE * D ** (-0.5),
        STEP_RATE * (F // 2) ** (-0.5),
    )
    momenta = []
    new_masters = []
    entry_list = []
    for index in range(5):
        left, right = lefts_t[index], rights_t[index]
        columns = right.shape[-1]
        entries = left.shape[-1] * shard_count * columns
        own_columns = columns // replicas
        squared_right = jnp.sum(right * right, axis=(-2, -1))
        scale_norm = jnp.sqrt(squared_right / entries + 1e-06)
        own_right = lax.dynamic_slice_in_dim(
            right, column_index * own_columns, own_columns, axis=right.ndim - 1
        )
        direction = (
            jnp.einsum("...km,...kn->...mn", left, own_right, precision=HIGHEST)
            / scale_norm[..., None, None]
        )
        new_master, new_moment = advance(
            weights_now[index], moments_now[index], direction, step_rates[index], WEIGHT_DECAY
        )
        momenta.append(new_moment)
        new_masters.append(new_master)
        entry_list += [float(replicas * entries)] * (left.size // (8 * left.shape[-1]))
    feedback_rms = jnp.sqrt(flat_squares / jnp.array(entry_list, F32))
    router_total = jnp.transpose(totals[0, :, :own_rows])
    gains_total = totals[1, :2, :own_rows]
    router_square = jnp.sum(total_squares[:, 0])
    gains_square = total_squares[:2, 1]
    router_direction = router_total / jnp.sqrt(
        router_square / (router_total.shape[0] * shard_count * router_total.shape[1]) + 1e-06
    )
    gains_direction = (
        gains_total / jnp.sqrt(gains_square / (gains_total.shape[1] * shard_count) + 1e-06)[:, None]
    )
    router_master, router_momentum = advance(
        router_weight, router_moment, router_direction, STEP_RATE * (8 * D) ** (-0.5), WEIGHT_DECAY
    )
    gains_master, gains_momentum = advance(
        norm_gains, gains_moment, gains_direction, GAIN_RATE, 0.0
    )
    return (
        output,
        input_grad,
        *bases,
        *right_out,
        *feedbacks,
        *momenta,
        router_momentum,
        gains_momentum,
        *new_masters,
        router_master,
        gains_master,
        feedback_rms,
    )


def solution(mesh):
    in_specs = (
        P(("rep", "shard"), None),
        P(("rep", "shard"), None),
        P(("rep", "shard"), None),
        P(("rep", "shard"), None),
        P(("rep", "shard"), None),
        P(("rep", "shard"), None),
        P("shard", "rep"),
        P(None, "shard", "rep"),
        P("shard", "rep"),
        P(None, None, "shard", "rep"),
        P(None, "shard", "rep"),
        P("shard", None),
        P(None, "shard"),
        P("shard", "rep"),
        P(None, "shard", "rep"),
        P("shard", "rep"),
        P(None, None, "shard", "rep"),
        P(None, "shard", "rep"),
        P("shard", None),
        P(None, "shard"),
        P("rep", "shard", None),
        P("rep", None, "shard", None),
        P("rep", "shard", None),
        P("rep", None, None, "shard", None),
        P("rep", None, "shard", None),
        P(),
        P(),
        P(),
        P(),
        P(),
    )
    out_specs = (
        P(("rep", "shard"), None),
        P(("rep", "shard"), None),
        P("shard", None),
        P(None, "shard", None),
        P("shard", None),
        P(None, None, "shard", None),
        P(None, "shard", None),
        P(),
        P(),
        P(),
        P(),
        P(),
        P("rep", "shard", None),
        P("rep", None, "shard", None),
        P("rep", "shard", None),
        P("rep", None, None, "shard", None),
        P("rep", None, "shard", None),
        P("shard", "rep"),
        P(None, "shard", "rep"),
        P("shard", "rep"),
        P(None, None, "shard", "rep"),
        P(None, "shard", "rep"),
        P("shard", None),
        P(None, "shard"),
        P("shard", "rep"),
        P(None, "shard", "rep"),
        P("shard", "rep"),
        P(None, None, "shard", "rep"),
        P(None, "shard", "rep"),
        P("shard", None),
        P(None, "shard"),
        P(),
    )
    return jax.shard_map(
        per_device, mesh=mesh, in_specs=in_specs, out_specs=out_specs, check_vma=False
    )
```

```python
import functools

import jax
import jax.numpy as jnp
from jax import lax
from jax.experimental import pallas as pl
from jax.experimental.pallas import tpu as pltpu
from jax.sharding import PartitionSpec as P

D = 1536
HQ = 12
HK = 2
HD = 128
F = 768
E = 8
TOK_DEV = 512
QW = 1536


EPSILON = 1e-05
ROPE_BASE = 1000000.0
MOMENTUM_DECAY = 0.9
WEIGHT_DECAY = 0.01
STEP_RATE = 4.0
GAIN_RATE = 3.0
HIGHEST = lax.Precision.HIGHEST


def rms_norm(hidden, gain_row):
    return (
        hidden * lax.rsqrt(jnp.mean(hidden * hidden, axis=-1, keepdims=True) + EPSILON) * gain_row
    )


def path_mask(segment, parent_row):
    table_ids = jnp.arange(parent_row.shape[0], dtype=jnp.int32)
    parent_one = jnp.sum(
        jnp.where(segment[:, None] == table_ids[None, :], parent_row[None, :], 0), axis=1
    )
    parent_two = jnp.where(
        parent_one >= 0,
        jnp.sum(
            jnp.where(parent_one[:, None] == table_ids[None, :], parent_row[None, :], 0), axis=1
        ),
        -1,
    )
    token_order = jnp.arange(segment.shape[0], dtype=jnp.int32)
    same_path = (segment[:, None] == segment[None, :]) & (
        token_order[None, :] <= token_order[:, None]
    )
    return (
        same_path
        | (segment[None, :] == parent_one[:, None])
        | (segment[None, :] == parent_two[:, None])
    )


def advance(weight_now, moment_now, direction, step_rate, decay_rate):
    moment_new = MOMENTUM_DECAY * moment_now + (1.0 - MOMENTUM_DECAY) * direction
    return (weight_now - step_rate * (moment_new + decay_rate * weight_now), moment_new)


CHUNKS = 4
PARTS = 2
GELU_C = 0.7978845608028654
GELU_A = 0.044715
MESH = pl.DeviceIdType.MESH
VMEM_LIMIT = 60 * 1024 * 1024
F32 = jnp.float32
BF16 = jnp.bfloat16


def z_slots(block):
    size = lax.axis_size("shard")
    return [block] + [
        lax.ppermute(block, "shard", [(i, (i + step) % size) for i in range(size)])
        for step in range(1, size)
    ]


def nn(a, b, precision=None):
    return jnp.dot(a, b, preferred_element_type=F32, precision=precision)


def nt(a, b, precision=None):
    return lax.dot_general(
        a, b, (((1,), (1,)), ((), ())), preferred_element_type=F32, precision=precision
    )


def tn(a, b):
    return lax.dot_general(a, b, (((0,), (0,)), ((), ())), preferred_element_type=F32)


def up_to(count, unit):
    return -(-count // unit) * unit


def two_terms(value):
    high = value.astype(BF16)
    return high, (value - high.astype(F32)).astype(BF16)


def three_terms(value):
    high = value.astype(BF16)
    rest = value - high.astype(F32)
    middle = rest.astype(BF16)
    low = (rest - middle.astype(F32)).astype(BF16)
    return jnp.concatenate([high.astype(F32), middle.astype(F32), low.astype(F32)], axis=0).astype(BF16)


def folded(value, rows=8):
    return value[:rows] + value[rows : 2 * rows] + value[2 * rows : 3 * rows]


def exact_nn(value, other):
    return folded(nn(three_terms(value), other))


def exact_nt(value, other):
    return folded(nt(three_terms(value), other))


def padded(value, width):
    if value.shape[1] == width:
        return value
    return jnp.concatenate(
        [value, jnp.zeros((value.shape[0], width - value.shape[1]), value.dtype)], axis=1
    )


def params(**more):
    return pltpu.CompilerParams(vmem_limit_bytes=VMEM_LIMIT, **more)


def vmem_specs(count):
    return [pl.BlockSpec(memory_space=pltpu.VMEM)] * count


def struct(shape, dtype=F32):
    return jax.ShapeDtypeStruct(shape, dtype)


def turn_heads(value, cosine, sine):
    return value * cosine + pltpu.roll(value, HD // 2, 1) * sine


def softmax_of(query, key, mask):
    raw = nt(query, key) * HD ** (-0.5)
    masked = jnp.where(mask > 0, raw, -1e30)
    raised = jnp.exp(masked - jnp.max(masked, axis=-1, keepdims=True))
    return raised / jnp.sum(raised, axis=-1, keepdims=True)


def head_lanes(head):
    return pl.ds(pl.multiple_of(head * HD, HD), HD)


def attention_forward_kernel(
    first_ref, query_ref, key_ref, value_ref, output_ref, tokens_ref, cosine_ref, sine_ref, mask_ref,
    qrot_ref, krot_ref, values_ref, mixed_ref, middle_ref,
):
    first = first_ref[...]
    cosine, sine = cosine_ref[...], sine_ref[...]
    values_ref[...] = nt(first, value_ref[...]).astype(BF16)
    keys = nt(first, key_ref[...])
    for g in range(HK):
        span = slice(g * HD, (g + 1) * HD)
        krot_ref[:, span] = turn_heads(keys[:, span], cosine, sine).astype(BF16)
    queries = nt(first, query_ref[...])
    for h in range(HQ):
        span = slice(h * HD, (h + 1) * HD)
        qrot_ref[:, span] = turn_heads(queries[:, span], cosine, sine).astype(BF16)

    @pl.loop(0, HQ)
    def _(head):
        group = head_lanes(head // (HQ // HK))
        share = softmax_of(qrot_ref[:, head_lanes(head)], krot_ref[:, group], mask_ref[...])
        mixed_ref[:, head_lanes(head)] = nn(share.astype(BF16), values_ref[:, group]).astype(BF16)

    middle_ref[...] = tokens_ref[...].astype(F32) + nt(mixed_ref[...], output_ref[...])


def attention_forward(operands):
    length, width = operands[0].shape
    kv = HK * HD
    return pl.pallas_call(
        attention_forward_kernel,
        in_specs=vmem_specs(len(operands)),
        out_specs=vmem_specs(5),
        out_shape=[
            struct((length, HQ * HD), BF16),
            struct((length, kv), BF16),
            struct((length, kv), BF16),
            struct((length, HQ * HD), BF16),
            struct((length, width)),
        ],
        cost_estimate=pl.CostEstimate(
            flops=2 * length * width * (2 * HQ * HD + 2 * kv) + 4 * HQ * HD * length * length,
            bytes_accessed=14 * length * width + 4 * width * HQ * HD,
            transcendentals=HQ * length * length,
        ),
        compiler_params=params(),
        name="attention_forward",
    )(*operands)


def attention_backward_kernel(
    middle_ref, output_ref, qrot_ref, krot_ref, values_ref, cosine_ref, sine_ref, mask_ref, first_ref,
    late_ref, joint_ref, grad_ref, mixed_ref, dk_ref, dv_ref,
):
    cosine, sine = cosine_ref[...], -sine_ref[...]
    mixed_ref[...] = nn(middle_ref[...], output_ref[...]).astype(BF16)
    dk_ref[...] = jnp.zeros_like(dk_ref)
    dv_ref[...] = jnp.zeros_like(dv_ref)

    @pl.loop(0, HQ)
    def _(head):
        lanes, group = head_lanes(head), head_lanes(head // (HQ // HK))
        query, key = qrot_ref[:, lanes], krot_ref[:, group]
        upstream = mixed_ref[:, lanes]
        share = softmax_of(query, key, mask_ref[...])
        grad = nt(upstream, values_ref[:, group])
        score = share * (grad - jnp.sum(share * grad, axis=-1, keepdims=True))
        score = score.astype(BF16)
        turned = nn(score, key) * HD ** (-0.5)
        joint_ref[:, lanes] = turn_heads(turned, cosine, sine).astype(BF16)
        dk_ref[:, group] += tn(score, query)
        dv_ref[:, group] += tn(share.astype(BF16), upstream)

    qw = HQ * HD
    for g in range(HK):
        span = slice(g * HD, (g + 1) * HD)
        turned = dk_ref[:, span] * HD ** (-0.5)
        joint_ref[:, qw + g * HD : qw + (g + 1) * HD] = turn_heads(turned, cosine, sine).astype(BF16)
    joint_ref[:, qw + HK * HD :] = dv_ref[...].astype(BF16)
    block = HK * HD

    @pl.loop(0, joint_ref.shape[1] // block)
    def _(k):
        lanes = pl.ds(pl.multiple_of(k * block, block), block)
        grad_ref[:, lanes] = tn(first_ref[...], joint_ref[:, lanes]).astype(BF16)


def attention_backward(operands):
    length, width = operands[0].shape
    kv = HK * HD
    return pl.pallas_call(
        attention_backward_kernel,
        in_specs=vmem_specs(len(operands)),
        out_specs=vmem_specs(2),
        out_shape=[
            struct((length, HQ * HD + 2 * kv), BF16),
            struct((width, HQ * HD + 2 * kv), BF16),
        ],
        scratch_shapes=[
            pltpu.VMEM((length, HQ * HD), BF16),
            pltpu.VMEM((length, kv), F32),
            pltpu.VMEM((length, kv), F32),
        ],
        cost_estimate=pl.CostEstimate(
            flops=8 * length * width * HQ * HD, bytes_accessed=length * width, transcendentals=0
        ),
        compiler_params=params(),
        name="attention_backward",
    )(*operands)


def weights_of(w1_ref, w2_ref, turned):
    here = lax.axis_index("shard")
    groups, lanes, _, double, span1 = w1_ref.shape
    f_cols = double // 2
    lanes2, _, groups2, _, f_rows, span2 = w2_ref.shape

    def joined(parts):
        return parts[0] if len(parts) == 1 else jnp.concatenate(parts, axis=1)

    def place(k, count):
        return lax.rem(here + (count - k), count) if turned else k

    def both(low, high):
        return joined(
            [
                w1_ref[low:high, place(k, lanes), 0].reshape((high - low) * double, span1)
                for k in range(lanes)
            ]
        )

    def first(a):
        return joined(
            [
                w1_ref[:, place(k, lanes), 0, a * f_cols : (a + 1) * f_cols, :].reshape(
                    groups * f_cols, span1
                )
                for k in range(lanes)
            ]
        )

    def second(low=0, high=groups2):
        if not turned:
            return joined(
                [w2_ref[k, 0, low:high, 0].reshape((high - low) * f_rows, span2) for k in range(lanes2)]
            )
        return jnp.concatenate(
            [
                joined([w2_ref[k, 0, place(g, groups2), 0] for k in range(lanes2)])
                for g in range(low, high)
            ],
            axis=0,
        )

    return groups, f_cols, both, first, second


def share_of(x_ref, expert, width):
    tail = x_ref[width : width + 2 * E, :].astype(F32)
    shares8 = tail[:E] + tail[E:]
    picked = lax.broadcasted_iota(jnp.int32, shares8.shape, 0) == expert
    return jnp.sum(jnp.where(picked, shares8, 0.0), axis=0, keepdims=True)


def hidden_backward(x, w1_ref, w2_ref, turned, br, act_ref, gt_ref, lanes):
    groups, f_cols, both, _, second = weights_of(w1_ref, w2_ref, turned)
    hidden = groups * f_cols
    groups2 = w2_ref.shape[2]
    parts = PARTS if groups % PARTS == 0 and groups2 % PARTS == 0 else 1
    for part in range(parts):
        low, high = part * groups // parts, (part + 1) * groups // parts
        low2, high2 = part * groups2 // parts, (part + 1) * groups2 // parts
        units = nn(both(low, high), x)
        act_grads = nn(second(low2, high2), br)
        hidden_part(low, high, f_cols, hidden, units, act_grads, act_ref, gt_ref, lanes)


def hidden_part(low, high, f_cols, hidden, units, act_grads, act_ref, gt_ref, lanes):
    for r in range(low, high):
        at = r - low
        gate = units[2 * at * f_cols : (2 * at + 1) * f_cols]
        up = units[(2 * at + 1) * f_cols : (2 * at + 2) * f_cols]
        act_grad = act_grads[at * f_cols : (at + 1) * f_cols]
        square = gate * gate
        bent = jnp.tanh(GELU_C * (gate + GELU_A * (square * gate)))
        lifted = 0.5 * (1.0 + bent)
        gelu = gate * lifted
        slope = lifted + 0.5 * gate * (1.0 - bent * bent) * (
            GELU_C * (1.0 + 3.0 * GELU_A * square)
        )
        act_ref[r * f_cols : (r + 1) * f_cols, lanes] = (gelu * up).astype(BF16)
        gt_ref[r * f_cols : (r + 1) * f_cols, lanes] = (act_grad * up * slope).astype(BF16)
        gt_ref[hidden + r * f_cols : hidden + (r + 1) * f_cols, lanes] = (
            act_grad * gelu
        ).astype(BF16)


def start_product(start, matrix):
    high, low = two_terms(start)
    both = jnp.concatenate([high.astype(F32), low.astype(F32)], axis=0).astype(BF16)
    top, rest = two_terms(matrix)
    first = nt(both, top)
    return first[:8] + first[8:] + nt(both, rest)[:8]


def own_kernel(
    first_expert, turned, x_ref, u_ref, up_ref, w1_ref, w2_ref, err_in_ref, err_out_ref, gate_ref,
    min_ref, mout_ref, y_ref, sg_ref, cg_ref, gt_ref, act_ref, br_ref,
):
    expert = first_expert + pl.program_id(0)
    width = up_ref.shape[1]
    _, _, _, first_weight, second_weight = weights_of(w1_ref, w2_ref, turned)
    rows, out_rows = min_ref.shape[2], mout_ref.shape[1]
    hidden = min_ref.shape[3]
    here = lax.axis_index("shard")
    share = share_of(x_ref, expert, width)
    br_ref[...] = (share * u_ref[...].astype(F32)).astype(BF16)
    hidden_backward(
        x_ref[:width, :], w1_ref, w2_ref, turned, br_ref[...], act_ref, gt_ref, slice(None)
    )
    own_x = x_ref[pl.ds(pl.multiple_of(here * rows, 16), rows), :]
    for a in range(2):
        min_ref[a, 0] = err_in_ref[a, 0] + nt(own_x, gt_ref[a * hidden : (a + 1) * hidden, :])
    own_act = act_ref[pl.ds(pl.multiple_of(here * out_rows, 16), out_rows), :]
    mout_ref[0] = err_out_ref[0] + nt(own_act, br_ref[...])
    expert_out = tn(act_ref[...], second_weight())
    cg_ref[0] = jnp.sum(up_ref[...].astype(F32) * expert_out, axis=1, keepdims=True)
    share_col = jnp.transpose(jnp.broadcast_to(share, (8, share.shape[1])))[:, :1]
    added = share_col * expert_out
    grown = tn(gt_ref[:hidden, :], first_weight(0)) + tn(gt_ref[hidden:, :], first_weight(1))

    @pl.when(pl.program_id(0) == 0)
    def _():
        y_ref[...] = added
        sg_ref[...] = grown

    @pl.when(pl.program_id(0) > 0)
    def _():
        y_ref[...] += added
        sg_ref[...] += grown


def rest_kernel(
    first_expert, trees, last, turned, w1_ref, w2_ref, start_in_ref, start_out_ref, min_in_ref,
    mout_in_ref, *rest,
):
    x_refs, u_refs = rest[:trees], rest[trees : 2 * trees]
    min_ref, mout_ref = rest[2 * trees + 1 : 2 * trees + 3]
    gt_ref, act_ref, br_ref = rest[-3:]
    expert = first_expert + pl.program_id(0)
    rows, out_rows = min_ref.shape[2], mout_ref.shape[1]
    hidden, width = min_ref.shape[3], mout_ref.shape[2]
    length = x_refs[0].shape[1]
    here = lax.axis_index("shard")
    for tree in range(trees):
        x_ref = x_refs[tree]
        lanes = slice(tree * length, (tree + 1) * length)
        share = share_of(x_ref, expert, width)
        br_ref[:, lanes] = (share * u_refs[tree][...].astype(F32)).astype(BF16)
        hidden_backward(
            x_ref[:width, :], w1_ref, w2_ref, turned, br_ref[:, lanes], act_ref, gt_ref, lanes
        )
    own_x = jnp.concatenate(
        [x_ref[pl.ds(pl.multiple_of(here * rows, 16), rows), :] for x_ref in x_refs], axis=1
    )
    for a in range(2):
        min_ref[a, 0] = min_in_ref[a, 0] + nt(own_x, gt_ref[a * hidden : (a + 1) * hidden, :])
    own_act = act_ref[pl.ds(pl.multiple_of(here * out_rows, 16), out_rows), :]
    mout_ref[0] = mout_in_ref[0] + nt(own_act, br_ref[...])
    if last:
        lin_ref, lout_ref = rest[2 * trees + 3 : 2 * trees + 5]
        lin_ref[...] = jnp.zeros_like(lin_ref)
        lout_ref[...] = jnp.zeros_like(lout_ref)
        for a in range(2):
            lin_ref[0, a, :, :rows] = start_product(start_in_ref[a, 0], min_ref[a, 0])
        lout_ref[0, :, :out_rows] = start_product(start_out_ref[0], mout_ref[0])


def whole_block(shape):
    return pl.BlockSpec(shape, lambda e: (0,) * len(shape), pipeline_mode=pl.Buffered(1))


def weight_blocks(w1, w2):
    last_block = w2.shape[3] - 1
    return [
        pl.BlockSpec((*w1.shape[:2], 1, *w1.shape[3:]), lambda e: (0, 0, e, 0, 0)),
        pl.BlockSpec(
            (w2.shape[0], 1, w2.shape[2], 1, *w2.shape[4:]), lambda e: (0, e, 0, last_block, 0, 0)
        ),
    ]


def matrix_blocks(first_expert, shape_in, shape_out):
    return [
        pl.BlockSpec(
            (shape_in[0], 1, *shape_in[2:]), lambda e: (0, first_expert + e, 0, 0)
        ),
        pl.BlockSpec((1, *shape_out[1:]), lambda e: (first_expert + e, 0, 0)),
    ]


def own_experts(first_expert, x, u, upstream, weights, err_in, err_out, gate):
    w1, w2, turned = weights
    count = w2.shape[1]
    hidden, rows = err_in.shape[3], err_in.shape[2]
    length, width = upstream.shape
    matrices = matrix_blocks(first_expert, err_in.shape, err_out.shape)
    in_specs = [
        whole_block(x.shape),
        whole_block(u.shape),
        whole_block(upstream.shape),
        *weight_blocks(w1, w2),
        *matrices,
        pl.BlockSpec(memory_space=pl.ANY),
    ]
    operands = [x, u, upstream, w1, w2, err_in, err_out, gate]
    part_in, part_out = (2, count, rows, hidden), (count, *err_out.shape[1:])
    return pl.pallas_call(
        functools.partial(own_kernel, first_expert, turned),
        grid=(count,),
        in_specs=in_specs,
        out_specs=[
            *matrix_blocks(0, part_in, part_out),
            whole_block((length, width)),
            whole_block((length, width)),
            pl.BlockSpec((1, length, 1), lambda e: (e, 0, 0)),
        ],
        out_shape=[
            struct(part_in),
            struct(part_out),
            struct((length, width)),
            struct((length, width)),
            struct((count, length, 1)),
        ],
        scratch_shapes=[
            pltpu.VMEM((2 * hidden, length), BF16),
            pltpu.VMEM((hidden, length), BF16),
            pltpu.VMEM((width, length), BF16),
        ],
        cost_estimate=pl.CostEstimate(
            flops=28 * count * hidden * width * length,
            bytes_accessed=count * (6 * hidden * width + 24 * rows * hidden) + 12 * length * width,
            transcendentals=0,
        ),
        compiler_params=params(),
        name="own_experts",
    )(*operands)


def rest_experts(first_expert, last, xs, us, weights, start_in, start_out, merged_in, merged_out, gate):
    w1, w2, turned = weights
    count, trees = w2.shape[1], len(xs)
    hidden, rows = merged_in.shape[3], merged_in.shape[2]
    out_rows = merged_out.shape[1]
    width, length = merged_out.shape[2], xs[0].shape[1]
    matrices = matrix_blocks(0, merged_in.shape, merged_out.shape)
    wide, wide_out = up_to(rows, 128), up_to(out_rows, 128)
    out_specs = list(matrices)
    out_shape = [struct(merged_in.shape), struct(merged_out.shape)]
    if last:
        out_specs += [
            pl.BlockSpec((1, 2, 8, wide), lambda e: (e, 0, 0, 0)),
            pl.BlockSpec((1, 8, wide_out), lambda e: (e, 0, 0)),
        ]
        out_shape += [struct((count, 2, 8, wide)), struct((count, 8, wide_out))]
    return pl.pallas_call(
        functools.partial(rest_kernel, first_expert, trees, last, turned),
        grid=(count,),
        in_specs=[
            *weight_blocks(w1, w2),
            *matrix_blocks(first_expert, start_in.shape, start_out.shape),
            *matrices,
            *[whole_block(x.shape) for x in (*xs, *us)],
            pl.BlockSpec(memory_space=pl.ANY),
        ],
        out_specs=out_specs,
        out_shape=out_shape,
        scratch_shapes=[
            pltpu.VMEM((2 * hidden, trees * length), BF16),
            pltpu.VMEM((hidden, trees * length), BF16),
            pltpu.VMEM((width, trees * length), BF16),
        ],
        input_output_aliases={4: 0, 5: 1},
        cost_estimate=pl.CostEstimate(
            flops=14 * count * trees * hidden * width * length,
            bytes_accessed=count * (6 * hidden * width + 24 * rows * hidden),
            transcendentals=0,
        ),
        compiler_params=params(),
        name="rest_experts",
    )(w1, w2, start_in, start_out, merged_in, merged_out, *xs, *us, gate)


def open_kernel(reps, shards, pieces, extra, *refs):
    count = len(pieces)
    arrays = count + 1 + extra
    sources, hop_ref = refs[:arrays], refs[arrays]
    targets, from_below, from_above = refs[arrays + 1 : 2 * arrays + 1], refs[2 * arrays + 1], refs[2 * arrays + 2]
    local_sem, up_send, up_recv, down_send, down_recv, chip_send, chip_recv, core_send, core_recv = refs[
        2 * arrays + 3 : -2
    ]
    hop_send, hop_recv = refs[-2:]
    rep, shard = lax.axis_index("rep"), lax.axis_index("shard")
    chips, core = reps // 2, rep % 2
    chip = rep // 2
    total = count + 1 + extra

    def slot(k, which):
        if k > count:
            return targets[k].at[which]
        span = sources[k].shape[1]
        lanes = pl.ds(pl.multiple_of(which * span, span), span)
        height = sources[k].shape[0]
        if k == count:
            return targets[k].at[:, lanes]
        row = pieces[k] + rep * height
        return targets[k].at[pl.ds(pl.multiple_of(row, 16), height), lanes]

    def band(k, which):
        height = sources[k].shape[0]
        row = pieces[k] + which * height
        return targets[k].at[pl.ds(pl.multiple_of(row, 16), height), :]

    barrier = pltpu.get_barrier_semaphore()
    for step in range(1, shards):
        pl.semaphore_signal(
            barrier, inc=1, device_id={"shard": lax.rem(shard + step, shards)}, device_id_type=MESH
        )
    for step in range(1, chips):
        to = lax.rem(chip + step, chips) * 2 + core
        pl.semaphore_signal(barrier, inc=1, device_id={"rep": to}, device_id_type=MESH)
    pl.semaphore_signal(barrier, inc=1, device_id={"rep": rep + 1 - 2 * core}, device_id_type=MESH)
    pl.semaphore_wait(barrier, shards - 1 + chips)

    locals_ = []
    for k in range(total):
        copy = pltpu.make_async_copy(sources[k], slot(k, shard), local_sem.at[k])
        copy.start()
        locals_.append(copy)

    def up_copy(k, step):
        source = sources[k] if step == 0 else slot(k, shard - step)
        return pltpu.make_async_remote_copy(
            src_ref=source,
            dst_ref=slot(k, shard - step),
            send_sem=up_send.at[k, step],
            recv_sem=up_recv.at[k, step],
            device_id={"shard": lax.rem(shard + 1, shards)},
            device_id_type=MESH,
        )

    def down_copy(k, step):
        source = sources[k] if step == 0 else slot(k, shard + step)
        return pltpu.make_async_remote_copy(
            src_ref=source,
            dst_ref=slot(k, shard + step),
            send_sem=down_send.at[k, step],
            recv_sem=down_recv.at[k, step],
            device_id={"shard": lax.rem(shard + shards - 1, shards)},
            device_id_type=MESH,
        )

    def hop(to_above):
        return pltpu.make_async_remote_copy(
            src_ref=hop_ref,
            dst_ref=from_below if to_above else from_above,
            send_sem=hop_send.at[int(to_above)],
            recv_sem=hop_recv.at[int(to_above)],
            device_id={"shard": lax.rem(shard + (1 if to_above else shards - 1), shards)},
            device_id_type=MESH,
        )

    def line_step(group, step):
        @pl.when((shard < shards - 1) & (step <= shard))
        def _():
            for k in group:
                up_copy(k, step).start()

        @pl.when((shard > 0) & (step <= shards - 1 - shard))
        def _():
            for k in group:
                down_copy(k, step).start()

    def line_arrive(group, step):
        @pl.when(step <= shard - 1)
        def _():
            for k in group:
                pltpu.make_async_remote_copy(
                    src_ref=slot(k, shard - 1 - step),
                    dst_ref=slot(k, shard - 1 - step),
                    send_sem=up_send.at[k, step],
                    recv_sem=up_recv.at[k, step],
                    device_id={"shard": lax.rem(shard + 1, shards)},
                    device_id_type=MESH,
                ).wait_recv()

        @pl.when(step <= shards - 2 - shard)
        def _():
            for k in group:
                pltpu.make_async_remote_copy(
                    src_ref=slot(k, shard + 1 + step),
                    dst_ref=slot(k, shard + 1 + step),
                    send_sem=down_send.at[k, step],
                    recv_sem=down_recv.at[k, step],
                    device_id={"shard": lax.rem(shard + 1, shards)},
                    device_id_type=MESH,
                ).wait_recv()

    def line_sent(group, step):
        @pl.when((shard < shards - 1) & (step <= shard))
        def _():
            for k in group:
                up_copy(k, step).wait_send()

        @pl.when((shard > 0) & (step <= shards - 1 - shard))
        def _():
            for k in group:
                down_copy(k, step).wait_send()

    first = list(range(count + 1))
    later = list(range(count + 1, total))
    for step in range(shards - 1):
        line_step(first, step)
        line_arrive(first, step)
    line_step(later, 0)

    @pl.when(shard < shards - 1)
    def _():
        hop(True).start()

    @pl.when(shard > 0)
    def _():
        hop(False).start()

    for copy in locals_:
        copy.wait()

    def chip_copy(k, step):
        to = lax.rem(chip + step, chips) * 2 + core
        return pltpu.make_async_remote_copy(
            src_ref=band(k, rep),
            dst_ref=band(k, rep),
            send_sem=chip_send.at[k, step - 1],
            recv_sem=chip_recv.at[k, step - 1],
            device_id={"rep": to},
            device_id_type=MESH,
        )

    def core_copy(k, step):
        owner = lax.rem(chip + chips - step, chips) * 2 + core
        return pltpu.make_async_remote_copy(
            src_ref=band(k, owner),
            dst_ref=band(k, owner),
            send_sem=core_send.at[k, step],
            recv_sem=core_recv.at[k, step],
            device_id={"rep": rep + 1 - 2 * core},
            device_id_type=MESH,
        )

    for step in range(1, chips):
        for k in range(count):
            chip_copy(k, step).start()
    for k in range(count):
        core_copy(k, 0).start()
    for step in range(1, shards - 1):
        line_arrive(later, step - 1)
        line_step(later, step)
    for step in range(1, chips):
        for k in range(count):
            chip_copy(k, step).wait_recv()
            core_copy(k, step).start()
    if shards > 1:
        line_arrive(later, shards - 2)
    for step in range(chips):
        for k in range(count):
            core_copy(k, step).wait()
            if step:
                chip_copy(k, step).wait_send()
    for step in range(shards - 1):
        line_sent(first + later, step)

    @pl.when(shard < shards - 1)
    def _():
        hop(True).wait_send()
        hop(False).wait_recv()

    @pl.when(shard > 0)
    def _():
        hop(False).wait_send()
        hop(True).wait_recv()


def open_gather(reps, shards, bands, small, lines, hop):
    operands = [operand for _, operand in bands] + [small] + list(lines)
    dma = pltpu.SemaphoreType.DMA
    count, total, chips = len(bands), len(operands), reps // 2
    operands.append(hop)
    span = small.shape[1]
    shapes = [struct((reps * operand.shape[0], shards * span), BF16) for _, operand in bands]
    shapes.append(struct((small.shape[0], shards * span), BF16))
    shapes += [struct((shards, *line.shape), BF16) for line in lines]
    shapes += [struct(hop.shape, BF16)] * 2
    anywhere = pl.BlockSpec(memory_space=pl.ANY)
    return pl.pallas_call(
        functools.partial(open_kernel, reps, shards, [at for at, _ in bands], len(lines)),
        in_specs=[anywhere] * (total + 1),
        out_specs=[anywhere] * (total + 2),
        out_shape=shapes,
        scratch_shapes=[
            dma((total,)),
            dma((total, shards - 1)),
            dma((total, shards - 1)),
            dma((total, shards - 1)),
            dma((total, shards - 1)),
            dma((count, chips)),
            dma((count, chips)),
            dma((count, chips)),
            dma((count, chips)),
            dma((2,)),
            dma((2,)),
        ],
        compiler_params=params(collective_id=4, has_side_effects=True),
        name="open_gather",
    )(*operands)


def packed_rows(value):
    half = value.shape[1] // 2
    return jnp.concatenate([value[:, :half], value[:, half:]], axis=0).astype(BF16)


def unpacked_rows(value):
    value = value.astype(F32)
    return jnp.concatenate([value[:8], value[8:]], axis=1)


def left_parts_kernel(
    shards, rows, wide, first_ref, joint_ref, mixed_ref, middle_ref, sq_ref, sk_ref, sv_ref, so_ref,
    eq_ref, ep_ref, eo_ref, router_ref, gains_ref, z_ref, own_ref,
):
    qw, kv = sq_ref.shape[1], sk_ref.shape[1]
    first = first_ref[...]
    pieces = []
    for start_ref, low in ((sq_ref, 0), (sk_ref, qw), (sv_ref, qw + kv)):
        high = low + start_ref.shape[1]
        pieces.append(exact_nn(exact_nt(start_ref[...], joint_ref[:, low:high]), first))
    pieces.append(exact_nn(exact_nt(so_ref[...], middle_ref[...]), mixed_ref[...]))
    pieces.append(router_ref[...])
    pieces.append(gains_ref[...])
    for shard in range(shards):
        z_ref[shard] = packed_rows(
            jnp.concatenate(
                [padded(piece[:, shard * rows : (shard + 1) * rows], wide) for piece in pieces],
                axis=1,
            )
        )
    errors = (
        start_product(sq_ref[...], eq_ref[...]),
        start_product(sk_ref[...], ep_ref[0]),
        start_product(sv_ref[...], ep_ref[1]),
        start_product(so_ref[...], eo_ref[...]),
    )
    for k, piece in enumerate(errors):
        own_ref[:, k * wide : (k + 1) * wide] = padded(piece, wide)


def left_parts(shards, rows, operands):
    wide = up_to(rows, 128)
    return pl.pallas_call(
        functools.partial(left_parts_kernel, shards, rows, wide),
        in_specs=vmem_specs(len(operands)),
        out_specs=vmem_specs(2),
        out_shape=[struct((shards, 16, 3 * wide), BF16), struct((8, 4 * wide))],
        compiler_params=params(),
        name="left_parts",
    )(*operands)


def greet(reps, shards):
    rep, shard = lax.axis_index("rep"), lax.axis_index("shard")
    barrier = pltpu.get_barrier_semaphore()
    for step in range(1, shards):
        pl.semaphore_signal(
            barrier, inc=1, device_id={"shard": lax.rem(shard + step, shards)}, device_id_type=MESH
        )
    for step in range(1, reps):
        pl.semaphore_signal(
            barrier, inc=1, device_id={"rep": lax.rem(rep + step, reps)}, device_id_type=MESH
        )
    pl.semaphore_wait(barrier, reps + shards - 2)


def start_all(axis, size, source, target, send, recv):
    here = lax.axis_index(axis)
    copies = []
    for step in range(1, size):
        to = lax.rem(here + step, size)
        copy = pltpu.make_async_remote_copy(
            src_ref=source(to),
            dst_ref=target(step),
            send_sem=send.at[step - 1],
            recv_sem=recv.at[step - 1],
            device_id={axis: to},
            device_id_type=MESH,
        )
        copy.start()
        copies.append(copy)
    return copies


def send_all(axis, size, source, target, send, recv):
    for copy in start_all(axis, size, source, target, send, recv):
        copy.wait()


def blocks_on_diagonal(square):
    size = square.shape[0]
    row = lax.broadcasted_iota(jnp.int32, (size, size), 0) // 8
    lane = lax.broadcasted_iota(jnp.int32, (size, size), 1) // 8
    kept = jnp.where(row == lane, square, 0.0)
    total = kept[:8]
    for k in range(1, size // 8):
        total = total + kept[8 * k : 8 * k + 8]
    return total


def spread_on_diagonal(flat):
    size = flat.shape[1]
    tall = jnp.concatenate([flat] * (size // 8), axis=0)
    row = lax.broadcasted_iota(jnp.int32, (size, size), 0) // 8
    lane = lax.broadcasted_iota(jnp.int32, (size, size), 1) // 8
    return jnp.transpose(jnp.where(row == lane, tall, 0.0))


def left_sync_kernel(reps, shards, wide, wide_out, piece, count, *refs):
    z_ref, own_ref = refs[:2]
    lin_refs, lout_refs = refs[2 : 2 + count], refs[2 + count : 2 + 2 * count]
    refs = refs[3 + 2 * count :]
    left_ref, left_out_ref, totals_ref, squares_ref, leftz_ref = refs[:5]
    (zbuf, parts, heard, total, grams, lanes_z, zs, zr, ps, pr, gs, gr, hs, hr, ls, lr) = refs[5:]
    rep, shard = lax.axis_index("rep"), lax.axis_index("shard")
    greet(reps, shards)
    send_all("shard", shards, lambda to: z_ref.at[to], lambda step: zbuf.at[step - 1], zs, zr)
    front = unpacked_rows(z_ref[shard])
    for step in range(shards - 1):
        front = front + unpacked_rows(zbuf[step])
    ins = [ref[e, a] for a in range(2) for ref in lin_refs for e in range(ref.shape[0])]
    outs = [ref[e] for ref in lout_refs for e in range(ref.shape[0])]
    line = jnp.concatenate(
        [front[:, : 4 * wide] + own_ref[...], front[:, 4 * wide :], *ins, *outs], axis=1
    )
    line = padded(line, reps * piece)
    for k in range(reps):
        parts[k] = packed_rows(line[:, k * piece : (k + 1) * piece])
    send_all("rep", reps, lambda to: parts.at[to], lambda step: heard.at[step - 1], ps, pr)
    mine = parts[rep].astype(F32)
    for step in range(reps - 1):
        mine = mine + heard[step].astype(F32)
    total[rep] = mine.astype(BF16)
    send_all("rep", reps, lambda to: total.at[rep], lambda step: total.at[rep], gs, gr)
    line = jnp.concatenate([unpacked_rows(total[k]) for k in range(reps)], axis=1)
    inner = len(ins)
    matrices = [line[:, k * wide : (k + 1) * wide] for k in range(4)]
    matrices += [line[:, (6 + k) * wide : (7 + k) * wide] for k in range(inner)]
    base = (6 + inner) * wide
    outers = [line[:, base + k * wide_out : base + (k + 1) * wide_out] for k in range(len(outs))]
    router, gains = line[:, 4 * wide : 5 * wide], line[:, 5 * wide : 6 * wide]
    size, size_out = up_to(8 * len(matrices), 128), up_to(8 * len(outers), 128)
    stack = jnp.concatenate(
        matrices + [jnp.zeros((size - 8 * len(matrices), wide), F32)], axis=0
    )
    stack_out = jnp.concatenate(
        outers + [jnp.zeros((size_out - 8 * len(outers), wide_out), F32)], axis=0
    )
    gram = blocks_on_diagonal(nt(stack, stack, HIGHEST))
    gram_out = blocks_on_diagonal(nt(stack_out, stack_out, HIGHEST))
    row = lax.broadcasted_iota(jnp.int32, (8, 128), 0)
    lane = lax.broadcasted_iota(jnp.int32, (8, 128), 1)
    more = jnp.where(lane == 0, jnp.sum(router * router, axis=1, keepdims=True), 0.0)
    more = jnp.where(lane == 1, jnp.sum(gains * gains, axis=1, keepdims=True), more)
    grams[shard] = jnp.concatenate([gram, gram_out, more], axis=1)
    lanes_z[shard] = stack[:32]
    sent = start_all("shard", shards, lambda to: grams.at[shard], lambda step: grams.at[shard], hs, hr)
    sent += start_all(
        "shard", shards, lambda to: lanes_z.at[shard], lambda step: lanes_z.at[shard], ls, lr
    )
    for copy in sent:
        copy.wait()
    gram = grams[0]
    for k in range(1, shards):
        gram = gram + grams[k]
    both = size + size_out
    squares_ref[...] = gram[:, both:]
    totals_ref[0] = router
    totals_ref[1] = gains
    where_from = lax.broadcasted_iota(jnp.int32, (both, 1024), 0)
    where_to = lax.broadcasted_iota(jnp.int32, (both, 1024), 1)
    chosen = jnp.where(
        (where_from % 8 == where_to // 128) & (where_from // 8 == where_to % 128), 1.0, 0.0
    ).astype(BF16)
    lines = exact_nn(gram[:, :both], chosen)
    used = (lane < len(matrices)) | ((lane >= size // 8) & (lane < size // 8 + len(outers)))
    table = [
        jnp.where(used, lines[:, 128 * k : 128 * k + 128], jnp.where(row == k, 1.0, 0.0))
        for k in range(8)
    ]
    inverse = [jnp.where(row == k, 1.0, 0.0) for k in range(8)]
    for k in range(8):
        pivot = table[k][k : k + 1]
        over = 1.0 / pivot
        for i in range(k + 1, 8):
            factor = table[i][k : k + 1] * over
            table[i] = table[i] - factor * table[k]
            inverse[i] = inverse[i] - factor * inverse[k]
        inverse[k] = inverse[k] / jnp.sqrt(pivot)
    flat = exact_nt(jnp.concatenate(inverse, axis=1), chosen)
    solve = spread_on_diagonal(flat[:, :size])
    lefts = nn(solve, stack, HIGHEST)
    lefts_out = nn(spread_on_diagonal(flat[:, size:]), stack_out, HIGHEST)
    left_ref[...] = lefts[: left_ref.shape[0]]
    left_out_ref[...] = lefts_out[: left_out_ref.shape[0]]
    for k in range(shards):
        leftz_ref[k] = nn(solve[:32, :32], lanes_z[k], HIGHEST)


def left_sync(reps, shards, z_part, own, lins, louts, late):
    wide, wide_out = lins[0].shape[3], louts[0].shape[2]
    inner, outer = 2 * sum(x.shape[0] for x in lins), sum(x.shape[0] for x in louts)
    piece = up_to(-(-((6 + inner) * wide + outer * wide_out) // reps), 256)
    matrices = 4 + inner
    size, size_out = up_to(8 * matrices, 128), up_to(8 * outer, 128)
    dma = pltpu.SemaphoreType.DMA
    operands = [z_part, own, *lins, *louts, late]
    return pl.pallas_call(
        functools.partial(left_sync_kernel, reps, shards, wide, wide_out, piece, len(lins)),
        in_specs=vmem_specs(len(operands)),
        out_specs=vmem_specs(5),
        out_shape=[
            struct((8 * matrices, wide)),
            struct((8 * outer, wide_out)),
            struct((2, 8, wide)),
            struct((8, 128)),
            struct((shards, 32, wide)),
        ],
        scratch_shapes=[
            pltpu.VMEM((shards - 1, 16, 3 * wide), BF16),
            pltpu.VMEM((reps, 16, piece // 2), BF16),
            pltpu.VMEM((reps - 1, 16, piece // 2), BF16),
            pltpu.VMEM((reps, 16, piece // 2), BF16),
            pltpu.VMEM((shards, 8, size + size_out + 128), F32),
            pltpu.VMEM((shards, 32, wide), F32),
            dma((shards - 1,)),
            dma((shards - 1,)),
            dma((reps - 1,)),
            dma((reps - 1,)),
            dma((reps - 1,)),
            dma((reps - 1,)),
            dma((shards - 1,)),
            dma((shards - 1,)),
            dma((shards - 1,)),
            dma((shards - 1,)),
        ],
        compiler_params=params(collective_id=1, has_side_effects=True),
        name="left_sync",
    )(*operands)


def left_product(left, matrix):
    high, low = two_terms(left)
    both = jnp.concatenate([high.astype(F32), low.astype(F32)], axis=0).astype(BF16)
    top, rest = two_terms(matrix)
    first = nn(both, top)
    return first[:8] + first[8:] + nn(both, rest)[:8]


def right_expert_kernel(left_ref, left_out_ref, min_ref, mout_ref, right_ref):
    rows, out_rows = min_ref.shape[2], mout_ref.shape[1]
    hidden = min_ref.shape[3]

    for a in range(2):
        right_ref[0, :, a * hidden : (a + 1) * hidden] = left_product(
            left_ref[a, 0, :, :rows], min_ref[a, 0]
        )
    right_ref[0, :, 2 * hidden :] = left_product(left_out_ref[0, :, :out_rows], mout_ref[0])


def right_experts(first_expert, lefts, lefts_out, merged_in, merged_out):
    count, rows, hidden = merged_in.shape[1:]
    out_rows, width = merged_out.shape[1:]
    wide, wide_out = lefts.shape[3], lefts_out.shape[2]
    return pl.pallas_call(
        right_expert_kernel,
        grid=(count,),
        in_specs=[
            pl.BlockSpec((2, 1, 8, wide), lambda e: (0, first_expert + e, 0, 0)),
            pl.BlockSpec((1, 8, wide_out), lambda e: (first_expert + e, 0, 0)),
            pl.BlockSpec((2, 1, rows, hidden), lambda e: (0, e, 0, 0)),
            pl.BlockSpec((1, out_rows, width), lambda e: (e, 0, 0)),
        ],
        out_specs=pl.BlockSpec((1, 8, 2 * hidden + width), lambda e: (e, 0, 0)),
        out_shape=struct((count, 8, 2 * hidden + width)),
        compiler_params=params(),
        name="right_experts",
    )(lefts, lefts_out, merged_in, merged_out)


def right_attention_kernel(
    shards, rows, left_ref, leftz_ref, first_ref, joint_ref, mixed_ref, middle_ref, eq_ref, ep_ref,
    eo_ref, right_ref,
):
    qw, kv = eq_ref.shape[1], ep_ref.shape[2]
    width = eo_ref.shape[1]

    def whole(k):
        return jnp.concatenate(
            [leftz_ref[z, 8 * k : 8 * k + 8, :rows] for z in range(shards)], axis=1
        )

    def own(k):
        return left_ref[8 * k : 8 * k + 8, :rows]

    first = first_ref[...]
    at = 0
    for k, error in ((0, eq_ref[...]), (1, ep_ref[0]), (2, ep_ref[1])):
        grown = exact_nn(exact_nt(whole(k), first), joint_ref[:, at : at + error.shape[1]])
        right_ref[:, at : at + error.shape[1]] = grown + left_product(own(k), error)
        at += error.shape[1]
    grown = exact_nn(exact_nt(whole(3), mixed_ref[...]), middle_ref[...])
    right_ref[:, at : at + width] = grown + left_product(own(3), eo_ref[...])


def right_attention(shards, rows, operands):
    width = operands[6].shape[1] + 2 * operands[7].shape[2] + operands[8].shape[1]
    return pl.pallas_call(
        functools.partial(right_attention_kernel, shards, rows),
        in_specs=vmem_specs(len(operands)),
        out_specs=pl.BlockSpec(memory_space=pltpu.VMEM),
        out_shape=struct((8, width)),
        compiler_params=params(),
        name="right_attention",
    )(*operands)


def right_sync_kernel(reps, shards, piece, count, *refs):
    experts_refs, attention_ref, out_ref = refs[:count], refs[count], refs[count + 1]
    parts, heard, across, total, ps, pr, zs, zr, gs, gr = refs[count + 2 :]
    rep, shard = lax.axis_index("rep"), lax.axis_index("shard")
    half = piece // 2
    greet(reps, shards)
    line = jnp.concatenate(
        [ref[e] for ref in experts_refs for e in range(ref.shape[0])] + [attention_ref[...]], axis=1
    )
    line = padded(line, reps * piece)
    for k in range(reps):
        at = k * piece
        parts[k] = jnp.concatenate(
            [line[:, at : at + half], line[:, at + half : at + piece]], axis=0
        ).astype(BF16)
    send_all("rep", reps, lambda to: parts.at[to], lambda step: heard.at[step - 1], ps, pr)
    mine = parts[rep].astype(F32)
    for step in range(reps - 1):
        mine = mine + heard[step].astype(F32)
    across[shard] = mine.astype(BF16)
    send_all("shard", shards, lambda to: across.at[shard], lambda step: across.at[shard], zs, zr)
    summed = across[0].astype(F32)
    for k in range(1, shards):
        summed = summed + across[k].astype(F32)
    total[rep] = summed.astype(BF16)
    send_all("rep", reps, lambda to: total.at[rep], lambda step: total.at[rep], gs, gr)
    for k in range(reps):
        block = total[k].astype(F32)
        out_ref[:, k * piece : k * piece + half] = block[:8]
        out_ref[:, k * piece + half : (k + 1) * piece] = block[8:]


def right_sync(reps, shards, experts, attention):
    columns = sum(part.shape[0] * part.shape[2] for part in experts) + attention.shape[1]
    piece = up_to(-(-columns // reps), 256)
    dma = pltpu.SemaphoreType.DMA
    return pl.pallas_call(
        functools.partial(right_sync_kernel, reps, shards, piece, len(experts)),
        in_specs=vmem_specs(len(experts) + 1),
        out_specs=pl.BlockSpec(memory_space=pltpu.VMEM),
        out_shape=struct((8, reps * piece)),
        scratch_shapes=[
            pltpu.VMEM((reps, 16, piece // 2), BF16),
            pltpu.VMEM((reps - 1, 16, piece // 2), BF16),
            pltpu.VMEM((shards, 16, piece // 2), BF16),
            pltpu.VMEM((reps, 16, piece // 2), BF16),
            dma((reps - 1,)),
            dma((reps - 1,)),
            dma((shards - 1,)),
            dma((shards - 1,)),
            dma((reps - 1,)),
            dma((reps - 1,)),
        ],
        compiler_params=params(collective_id=2, has_side_effects=True),
        name="right_sync",
    )(*experts, attention)


def low_rank(left, right):
    high, low = two_terms(left)
    lefts = jnp.concatenate([high.astype(F32), low.astype(F32)], axis=0).astype(BF16)
    rights = jnp.concatenate([right, right], axis=0).astype(BF16)
    return tn(lefts, rights)


def feedback_expert_kernel(
    replicas, first_expert, left_ref, left_out_ref, right_ref, min_ref, mout_ref, *rest
):
    fin_ref, fout_ref, sq_ref = rest[-3:]
    rows, hidden = min_ref.shape[2:]
    out_rows = mout_ref.shape[1]
    row = lax.broadcasted_iota(jnp.int32, (8, 128), 0)
    lane = lax.broadcasted_iota(jnp.int32, (8, 128), 1)

    @pl.when(pl.program_id(0) == 0)
    def _():
        sq_ref[...] = jnp.zeros_like(sq_ref)

    added = jnp.zeros((8, 128), F32)
    for a in range(2):
        approx = low_rank(
            left_ref[a, 0, :, :rows], right_ref[:, a * hidden : (a + 1) * hidden]
        )
        left_over = min_ref[a, 0] - approx * (1.0 / replicas)
        fin_ref[a, 0] = left_over
        added = jnp.where(lane == a, jnp.sum(left_over * left_over), added)
    approx = low_rank(left_out_ref[0, :, :out_rows], right_ref[:, 2 * hidden :])
    left_over = mout_ref[0] - approx * (1.0 / replicas)
    fout_ref[0] = left_over
    added = jnp.where(lane == 2, jnp.sum(left_over * left_over), added)
    sq_ref[...] += jnp.where(row == first_expert + pl.program_id(0), added, 0.0)


def feedback_experts(
    replicas, first_expert, lefts, lefts_out, rights, merged_in, merged_out, whole_in, whole_out
):
    count, rows, hidden = merged_in.shape[1:]
    out_rows, width = merged_out.shape[1:]
    wide, wide_out = lefts.shape[3], lefts_out.shape[2]
    shapes = (2, E, rows, hidden), (E, out_rows, width)
    operands = [lefts, lefts_out, rights, merged_in, merged_out]
    in_specs = [
        pl.BlockSpec((2, 1, 8, wide), lambda e: (0, first_expert + e, 0, 0)),
        pl.BlockSpec((1, 8, wide_out), lambda e: (first_expert + e, 0, 0)),
        pl.BlockSpec((8, 2 * hidden + width), lambda e: (0, first_expert + e)),
        *matrix_blocks(0, merged_in.shape, merged_out.shape),
    ]
    aliases = {}
    if whole_in is not None:
        operands += [whole_in, whole_out]
        in_specs += [pl.BlockSpec(memory_space=pl.ANY)] * 2
        aliases = {5: 0, 6: 1}
    return pl.pallas_call(
        functools.partial(feedback_expert_kernel, replicas, first_expert),
        grid=(count,),
        in_specs=in_specs,
        out_specs=[
            *matrix_blocks(first_expert, *shapes),
            pl.BlockSpec((8, 128), lambda e: (0, 0)),
        ],
        out_shape=[struct(shapes[0]), struct(shapes[1]), struct((8, 128))],
        input_output_aliases=aliases,
        compiler_params=params(),
        name="feedback_experts",
    )(*operands)


def feedback_attention_kernel(
    replicas, rows, left_ref, right_ref, gj_ref, go_ref, eq_ref, ep_ref, eo_ref, fq_ref, fp_ref,
    fo_ref, sq_ref,
):
    qw, kv = eq_ref.shape[1], ep_ref.shape[2]
    lane = lax.broadcasted_iota(jnp.int32, (8, 128), 1)
    row = lax.broadcasted_iota(jnp.int32, (8, 128), 0)
    added = jnp.zeros((8, 128), F32)
    at = 0
    jobs = (
        (gj_ref, 0, eq_ref, fq_ref),
        (gj_ref, qw, ep_ref.at[0], fp_ref.at[0]),
        (gj_ref, qw + kv, ep_ref.at[1], fp_ref.at[1]),
        (go_ref, 0, eo_ref, fo_ref),
    )
    for k, (grad_ref, low, error_ref, out_ref) in enumerate(jobs):
        width = error_ref.shape[1]
        approx = low_rank(left_ref[8 * k : 8 * k + 8, :rows], right_ref[:, at : at + width])
        merged = grad_ref[:, low : low + width].astype(F32) + error_ref[...]
        left_over = merged - approx * (1.0 / replicas)
        out_ref[...] = left_over
        added = jnp.where(lane == 3 + k, jnp.sum(left_over * left_over), added)
        at += width
    sq_ref[...] = jnp.where(row == 0, added, 0.0)


def feedback_attention(replicas, rows, operands):
    shapes = [operands[k].shape for k in (4, 5, 6)]
    return pl.pallas_call(
        functools.partial(feedback_attention_kernel, replicas, rows),
        in_specs=vmem_specs(len(operands)),
        out_specs=vmem_specs(4),
        out_shape=[struct(shape) for shape in shapes] + [struct((8, 128))],
        compiler_params=params(),
        name="feedback_attention",
    )(*operands)


def squares_sync_kernel(reps, shards, count, *refs):
    out_ref, plane, line, ps, pr, zs, zr = refs[count:]
    rep, shard = lax.axis_index("rep"), lax.axis_index("shard")
    greet(reps, shards)
    added = refs[0][...]
    for ref in refs[1:count]:
        added = added + ref[...]
    plane[rep] = added
    send_all("rep", reps, lambda to: plane.at[rep], lambda step: plane.at[rep], ps, pr)
    summed = plane[0]
    for k in range(1, reps):
        summed = summed + plane[k]
    line[shard] = summed
    send_all("shard", shards, lambda to: line.at[shard], lambda step: line.at[shard], zs, zr)
    summed = line[0]
    for k in range(1, shards):
        summed = summed + line[k]
    out_ref[...] = summed


def squares_sync(reps, shards, parts):
    dma = pltpu.SemaphoreType.DMA
    return pl.pallas_call(
        functools.partial(squares_sync_kernel, reps, shards, len(parts)),
        in_specs=vmem_specs(len(parts)),
        out_specs=pl.BlockSpec(memory_space=pltpu.VMEM),
        out_shape=struct((8, 128)),
        scratch_shapes=[
            pltpu.VMEM((reps, 8, 128), F32),
            pltpu.VMEM((shards, 8, 128), F32),
            dma((reps - 1,)),
            dma((reps - 1,)),
            dma((shards - 1,)),
            dma((shards - 1,)),
        ],
        compiler_params=params(collective_id=3, has_side_effects=True),
        name="squares_sync",
    )(*parts)


def per_device(
    tokens,
    cotangent,
    seg_ids,
    parents,
    positions,
    routes,
    query_weight,
    pair_weight,
    output_weight,
    inner_weight,
    outer_weight,
    router_weight,
    norm_gains,
    query_moment,
    pair_moment,
    output_moment,
    inner_moment,
    outer_moment,
    router_moment,
    gains_moment,
    query_error,
    pair_error,
    output_error,
    inner_error,
    outer_error,
    query_start,
    pair_start,
    output_start,
    inner_start,
    outer_start,
):
    replicas = lax.axis_size("rep")
    shard_count = lax.axis_size("shard")
    here = lax.axis_index("shard")
    both = ("rep", "shard")
    bf16 = jnp.bfloat16
    query_t = jnp.swapaxes(query_weight, 0, 1).astype(bf16)
    pair_t = jnp.swapaxes(pair_weight, 1, 2).astype(bf16)
    output_t = jnp.swapaxes(output_weight, 0, 1).astype(bf16)
    inner_t = jnp.transpose(inner_weight, (1, 0, 3, 2)).astype(bf16)
    outer_low = outer_weight.astype(bf16)
    router_t = jnp.swapaxes(router_weight, 0, 1).astype(bf16)
    gains_low = norm_gains.astype(bf16)
    own_rows = query_t.shape[1]
    q_cols, p_cols, f_cols = query_t.shape[0], pair_t.shape[1], inner_t.shape[2]
    f_rows = outer_low.shape[1]
    small = jnp.concatenate([router_t, gains_low], axis=0)
    small = jnp.pad(small, ((0, 16 - small.shape[0]), (0, 0)))
    per_chunk = E // CHUNKS
    outer_cols = outer_low.shape[2]
    paired = replicas % 2 == 0 and per_chunk == 2 and own_rows == 2 * outer_cols == 2 * f_rows
    paired = paired and 2 * f_cols == f_rows and own_rows % 128 == 0
    paired = paired and q_cols % 16 == 0 and p_cols % 16 == 0 and f_cols % 16 == 0

    def whole_weights(inner_all, outer_all):
        inner_all = inner_all.reshape(replicas, shard_count, per_chunk, 2, f_cols, own_rows)
        w1 = jnp.transpose(inner_all, (2, 3, 0, 4, 1, 5)).reshape(
            1, 1, per_chunk, 2 * replicas * f_cols, shard_count * own_rows
        )
        w2 = jnp.transpose(outer_all, (2, 1, 3, 0, 4)).reshape(
            1, per_chunk, 1, 1, shard_count * f_rows, replicas * outer_cols
        )
        return w1, w2, False

    cot_t = jnp.transpose(cotangent)
    chunk_weights = []
    if paired:
        core = lax.axis_index("rep") % 2
        outer_pairs = outer_low.reshape(CHUNKS, 2, f_rows, outer_cols)
        keep = jnp.where(core == 0, outer_pairs[:, 0], outer_pairs[:, 1])
        give = jnp.where(core == 0, outer_pairs[:, 1], outer_pairs[:, 0])
        got = lax.ppermute(give, "rep", [(i, i + 1 - 2 * (i % 2)) for i in range(replicas)])
        wide_outer = jnp.concatenate(
            [jnp.where(core == 0, keep, got), jnp.where(core == 0, got, keep)], axis=2
        )
        inner_packs = inner_t.reshape(CHUNKS, per_chunk * 2 * f_cols, own_rows)
        packs = [
            jnp.concatenate([inner_packs[k], wide_outer[k]], axis=0) for k in range(CHUNKS)
        ]
        opened = open_gather(
            replicas,
            shard_count,
            [(0, query_t), (0, pair_t[0]), (0, pair_t[1]), (0, output_t)],
            small,
            packs[:1],
            cot_t,
        )
        query_full, key_full, value_full, output_full, small_full = opened[:5]
        height = packs[0].shape[0]
        near = z_slots(packs[1])
        first_line, below_u, above_u = opened[5:]
    else:
        packed = jnp.concatenate(
            [query_t, pair_t.reshape(2 * p_cols, own_rows), output_t, small], axis=0
        )
        spread = lax.all_gather(packed, both).reshape(
            replicas, shard_count, packed.shape[0], own_rows
        )

        def joined(low, high):
            piece = jnp.transpose(spread[:, :, low:high], (0, 2, 1, 3))
            return piece.reshape(-1, shard_count * own_rows)

        at = q_cols + 2 * p_cols
        query_full = joined(0, q_cols)
        key_full, value_full = joined(q_cols, q_cols + p_cols), joined(q_cols + p_cols, at)
        output_full = joined(at, at + q_cols)
        small_full = joined(at + q_cols, packed.shape[0])[: small.shape[0]]
        for index in range(CHUNKS):
            span = slice(index * per_chunk, (index + 1) * per_chunk)
            chunk_weights.append(
                whole_weights(
                    lax.all_gather(inner_t[span], both),
                    lax.all_gather(outer_low[span], both).reshape(
                        replicas, shard_count, per_chunk, f_rows, outer_cols
                    ),
                )
            )
    router_full = small_full[:E]
    gain_values = small_full[E : E + 2].astype(jnp.float32)

    hidden = tokens.astype(jnp.float32)
    length = hidden.shape[0]
    position = positions[0]
    allowed = path_mask(seg_ids[0], parents[0])
    first_low = rms_norm(hidden, gain_values[0]).astype(bf16)
    half_head = HD // 2
    frequency = ROPE_BASE ** (-2.0 * jnp.arange(half_head, dtype=jnp.float32) / HD)
    angles = position.astype(jnp.float32)[:, None] * frequency[None, :]
    cosine = jnp.concatenate([jnp.cos(angles), jnp.cos(angles)], axis=1)
    sine = jnp.concatenate([-jnp.sin(angles), jnp.sin(angles)], axis=1)
    mask = allowed.astype(bf16)
    query_rot, key_rot, values, mixed_low, middle = attention_forward(
        (
            first_low, query_full, key_full, value_full, output_full, tokens, cosine, sine, mask,
        )
    )
    second_low = rms_norm(middle, gain_values[1]).astype(bf16)
    logits = jnp.einsum("td,ed->te", second_low, router_full, preferred_element_type=jnp.float32)
    expert_ids = jnp.arange(E, dtype=jnp.int32)
    route_mask = jnp.any(routes[:, :, None] == expert_ids[None, None, :], axis=1)
    route_top = jnp.max(jnp.where(route_mask, logits, -1e30), axis=-1, keepdims=True)
    raised_gate = jnp.where(route_mask, jnp.exp(logits - route_top), 0.0)
    shares = raised_gate / jnp.sum(raised_gate, axis=-1, keepdims=True)
    shares_t = jnp.transpose(shares)
    shares_high = shares_t.astype(bf16)
    shares_rest = (shares_t - shares_high.astype(jnp.float32)).astype(bf16)
    tree_x = jnp.concatenate([jnp.transpose(second_low), shares_high, shares_rest], axis=0)

    token = tree_x[:16, :128]
    far = None

    def gathered(line, turned):
        part = lax.all_gather(line, "rep")
        w1 = part.reshape(replicas, shard_count, 3, f_rows, own_rows)
        w2 = part.reshape(replicas // 2, 2, shard_count, 3, f_rows, own_rows)
        chunk_weights.append((w1, w2, turned))

    if paired:
        near, held, token = lax.optimization_barrier(
            (near, jnp.concatenate(packs[2:], axis=0), token)
        )
        far = z_slots(held)
        gathered(first_line, False)
        gathered(jnp.stack(near), True)

    upstream = cotangent.astype(jnp.float32)
    start_in = jnp.swapaxes(inner_start, 2, 3)
    start_out = jnp.swapaxes(outer_start, 1, 2)
    chunks = range(CHUNKS)
    merged_parts, lins, louts = [None] * CHUNKS, [None] * CHUNKS, [None] * CHUNKS
    y_parts, grad_parts, combine_parts = [None] * CHUNKS, [None] * CHUNKS, [None] * CHUNKS
    slots_x, slots_u = {}, {}
    state = {"gate": token, "x": tree_x, "u": cot_t}

    def exchange(step, held_x, held_u):
        ring = [(i, (i + step) % shard_count) for i in range(shard_count)]
        slots_x[step] = lax.ppermute(held_x, "shard", ring)
        slots_u[step] = lax.ppermute(held_u, "shard", ring)

    def own(index):
        done = own_experts(
            index * per_chunk,
            state["x"],
            state["u"],
            cotangent,
            chunk_weights[index],
            inner_error[0],
            outer_error[0],
            state["gate"],
        )
        merged_parts[index] = (done[0], done[1])
        y_parts[index], grad_parts[index] = done[2], done[3]
        combine_parts[index] = done[4][:, :, 0]
        state["gate"] = done[0][0, 0, :16, :128].astype(bf16)

    def others(index, steps, last):
        done = rest_experts(
            index * per_chunk,
            last,
            [slots_x[step] for step in steps],
            [slots_u[step] for step in steps],
            chunk_weights[index],
            start_in,
            start_out,
            *merged_parts[index],
            state["gate"],
        )
        merged_parts[index] = (done[0], done[1])
        if last:
            lins[index], louts[index] = done[2], done[3]
        state["gate"] = done[0][0, 0, :16, :128].astype(bf16)

    def all_others(index, steps):
        groups = [steps[at : at + 3] for at in range(0, len(steps), 3)]
        for group in groups:
            others(index, group, group is groups[-1])

    steps = list(range(1, shard_count))
    filled = shard_count == 4 and CHUNKS == 4
    def far_weights():
        lines, state["gate"] = lax.optimization_barrier((far, state["gate"]))
        lines = jnp.stack(lines)
        for k in range(CHUNKS - 2):
            gathered(lines[:, k * height : (k + 1) * height], True)

    def pass_on(ups, downs):
        forth = [(i, i + 1) for i in range(shard_count - 1)]
        back = [(i + 1, i) for i in range(shard_count - 1)]
        return (
            tuple(lax.ppermute(up, "shard", forth) for up in ups),
            tuple(lax.ppermute(down, "shard", back) for down in downs),
        )

    def not_before(pair):
        pair, state["gate"] = lax.optimization_barrier((pair, state["gate"]))
        return pair

    late = token
    if filled and paired:
        own(0)
        state["x"], state["u"] = held = not_before((state["x"], state["u"]))
        ups, downs = [held], [held]
        up, down = pass_on(held[:1], held[:1])
        ups.append((up[0], below_u))
        downs.append((down[0], above_u))
        far_weights()
        own(1)
        ups[1], downs[1] = not_before((ups[1], downs[1]))
        up, down = pass_on(ups[1], downs[1])
        ups.append(up)
        downs.append(down)
        slots_x[1], slots_u[1] = (jnp.where(here >= 1, ups[1][k], downs[1][k]) for k in range(2))
        others(0, [1], False)
        own(2)
        others(1, [1], False)
        ups[2], downs[2] = not_before((ups[2], downs[2]))
        up, down = pass_on(ups[2], downs[2])
        ups.append(up)
        downs.append(down)
        others(2, [1], False)
        own(3)
        slots_x[2], slots_u[2] = (
            jnp.where(here == 0, downs[2][k], jnp.where(here == 3, ups[2][k], downs[1][k]))
            for k in range(2)
        )
        slots_x[3], slots_u[3] = (
            jnp.where(
                here == 0,
                downs[3][k],
                jnp.where(here == 1, downs[2][k], jnp.where(here == 2, ups[2][k], ups[3][k])),
            )
            for k in range(2)
        )
        for array in (*ups[3], *downs[3]):
            late = late + array[:16, :128]
    else:
        if paired:
            far_weights()
        for step in steps:
            exchange(step, tree_x, cot_t)
        for index in chunks:
            own(index)
    combined = middle
    second_grad = grad_parts[0]
    for index in chunks:
        combined = combined + y_parts[index]
        if index:
            second_grad = second_grad + grad_parts[index]
    output = combined.astype(bf16)
    combine_grad = jnp.transpose(jnp.concatenate(combine_parts, axis=0))
    logit_low = (
        shares * (combine_grad - jnp.sum(shares * combine_grad, axis=-1, keepdims=True))
    ).astype(bf16)
    grad_router = jnp.einsum("td,te->de", second_low, logit_low, preferred_element_type=jnp.float32)
    second_grad = second_grad + jnp.einsum(
        "te,ed->td", logit_low, router_full, preferred_element_type=jnp.float32
    )
    _, second_pull = jax.vjp(rms_norm, middle, gain_values[1])
    middle_part, gain_two = second_pull(second_grad)
    middle_grad = upstream + middle_part
    middle_low = middle_grad.astype(bf16)
    grad_output = jnp.einsum("tq,td->qd", mixed_low, middle_low, preferred_element_type=jnp.float32)
    group_output = lax.psum_scatter(
        grad_output.astype(bf16), "shard", scatter_dimension=0, tiled=True
    )
    joint_grad, grad_joint = attention_backward(
        (
            middle_low, output_full, query_rot, key_rot, values, cosine, sine, mask, first_low,
            late,
        )
    )
    group_joint = lax.psum_scatter(
        grad_joint, "shard", scatter_dimension=0, tiled=True
    )
    first_grad = (
        nn(joint_grad[:, :QW], query_full)
        + nn(joint_grad[:, QW : QW + HK * HD], key_full)
        + nn(joint_grad[:, QW + HK * HD :], value_full)
    )
    _, first_pull = jax.vjp(rms_norm, hidden, gain_values[0])
    hidden_part, gain_one = first_pull(first_grad)
    input_grad = (middle_grad + hidden_part).astype(bf16)
    grad_gains = jnp.stack([gain_one, gain_two])

    state["gate"] = joint_grad
    if filled and paired:
        others(3, [1, 2, 3], True)
        others(2, [2, 3], True)
        others(0, [2, 3], True)
        others(1, [2, 3], True)
    else:
        for index in chunks:
            all_others(index, steps)

    small_rows = [jnp.transpose(grad_router), jnp.pad(grad_gains, ((0, 6), (0, 0)))]
    start_q, start_o = jnp.transpose(query_start), jnp.transpose(output_start)
    start_p = jnp.swapaxes(pair_start, 1, 2)
    z_part, own_left = left_parts(
        shard_count,
        own_rows,
        (
            first_low, joint_grad, mixed_low, middle_low, start_q, start_p[0], start_p[1], start_o,
            query_error[0], pair_error[0], output_error[0], *small_rows,
        ),
    )
    left_flat, left_out_flat, totals, total_squares, left_lines = left_sync(
        replicas, shard_count, z_part, own_left, lins, louts, group_joint[:16, :128]
    )
    wide, wide_out = left_flat.shape[1], left_out_flat.shape[1]
    lefts = left_flat.reshape(-1, 8, wide)
    lefts_in = lefts[4:].reshape(2, E, 8, wide)
    lefts_out = left_out_flat.reshape(E, 8, wide_out)
    lefts_t = (
        lefts[0, :, :own_rows],
        lefts[1:3, :, :own_rows],
        lefts[3, :, :own_rows],
        lefts_in[..., :own_rows],
        lefts_out[..., :f_rows],
    )
    bases = tuple(jnp.swapaxes(left, -1, -2) for left in lefts_t)

    right_parts = [
        right_experts(index * per_chunk, lefts_in, lefts_out, *merged_parts[index])
        for index in range(CHUNKS)
    ]
    right_rest = right_attention(
        shard_count,
        own_rows,
        (
            left_flat[:32], left_lines, first_low, joint_grad, mixed_low, middle_low,
            query_error[0], pair_error[0], output_error[0],
        ),
    )
    rights = right_sync(replicas, shard_count, right_parts, right_rest)
    hidden_units = inner_error.shape[4]
    step = 2 * hidden_units + D
    by_expert = rights[:, : E * step].reshape(8, E, step)
    rest = rights[:, E * step :]
    kv = HK * HD
    rights_t = (
        rest[:, :QW],
        jnp.stack([rest[:, QW : QW + kv], rest[:, QW + kv : QW + 2 * kv]]),
        rest[:, QW + 2 * kv : QW + 2 * kv + D],
        jnp.transpose(by_expert[:, :, : 2 * hidden_units].reshape(8, E, 2, hidden_units), (2, 1, 0, 3)),
        jnp.transpose(by_expert[:, :, 2 * hidden_units :], (1, 0, 2)),
    )
    right_out = tuple(jnp.swapaxes(right, -1, -2) for right in rights_t)

    feedback_in = feedback_out = None
    squares_experts = []
    for index in range(CHUNKS):
        feedback_in, feedback_out, part = feedback_experts(
            replicas, index * per_chunk, lefts_in, lefts_out, rights, *merged_parts[index],
            feedback_in, feedback_out,
        )
        squares_experts.append(part)
    feedback_q, feedback_p, feedback_o, squares_rest = feedback_attention(
        replicas,
        own_rows,
        (
            left_flat[:32], rest[:, : QW + 2 * kv + D], group_joint, group_output,
            query_error[0], pair_error[0], output_error[0],
        ),
    )
    feedbacks = tuple(
        part[None] for part in (feedback_q, feedback_p, feedback_o, feedback_in, feedback_out)
    )
    squares = squares_sync(replicas, shard_count, squares_experts + [squares_rest])
    flat_squares = jnp.concatenate(
        [squares[0, 3:7], squares[:, 0], squares[:, 1], squares[:, 2]], axis=0
    )

    column_index = lax.axis_index("rep")
    weights_now = (query_weight, pair_weight, output_weight, inner_weight, outer_weight)
    moments_now = (query_moment, pair_moment, output_moment, inner_moment, outer_moment)
    step_rates = (
        STEP_RATE * D ** (-0.5),
        STEP_RATE * D ** (-0.5),
        STEP_RATE * (QW * 4 // TOK_DEV + 1) ** (-0.5),
        STEP_RATE * D ** (-0.5),
        STEP_RATE * (F // 2) ** (-0.5),
    )
    momenta = []
    new_masters = []
    entry_list = []
    for index in range(5):
        left, right = lefts_t[index], rights_t[index]
        columns = right.shape[-1]
        entries = left.shape[-1] * shard_count * columns
        own_columns = columns // replicas
        squared_right = jnp.sum(right * right, axis=(-2, -1))
        scale_norm = jnp.sqrt(squared_right / entries + 1e-06)
        own_right = lax.dynamic_slice_in_dim(
            right, column_index * own_columns, own_columns, axis=right.ndim - 1
        )
        direction = (
            jnp.einsum("...km,...kn->...mn", left, own_right, precision=lax.Precision.HIGH)
            / scale_norm[..., None, None]
        )
        new_master, new_moment = advance(
            weights_now[index], moments_now[index], direction, step_rates[index], WEIGHT_DECAY
        )
        momenta.append(new_moment)
        new_masters.append(new_master)
        entry_list += [float(replicas * entries)] * (left.size // (8 * left.shape[-1]))
    feedback_rms = jnp.sqrt(flat_squares / jnp.array(entry_list, F32))
    router_total = jnp.transpose(totals[0, :, :own_rows])
    gains_total = totals[1, :2, :own_rows]
    router_square = jnp.sum(total_squares[:, 0])
    gains_square = total_squares[:2, 1]
    router_direction = router_total / jnp.sqrt(
        router_square / (router_total.shape[0] * shard_count * router_total.shape[1]) + 1e-06
    )
    gains_direction = (
        gains_total / jnp.sqrt(gains_square / (gains_total.shape[1] * shard_count) + 1e-06)[:, None]
    )
    router_master, router_momentum = advance(
        router_weight, router_moment, router_direction, STEP_RATE * (8 * D) ** (-0.5), WEIGHT_DECAY
    )
    gains_master, gains_momentum = advance(
        norm_gains, gains_moment, gains_direction, GAIN_RATE, 0.0
    )
    return (
        output,
        input_grad,
        *bases,
        *right_out,
        *feedbacks,
        *momenta,
        router_momentum,
        gains_momentum,
        *new_masters,
        router_master,
        gains_master,
        feedback_rms,
    )


def solution(mesh):
    in_specs = (
        P(("rep", "shard"), None),
        P(("rep", "shard"), None),
        P(("rep", "shard"), None),
        P(("rep", "shard"), None),
        P(("rep", "shard"), None),
        P(("rep", "shard"), None),
        P("shard", "rep"),
        P(None, "shard", "rep"),
        P("shard", "rep"),
        P(None, None, "shard", "rep"),
        P(None, "shard", "rep"),
        P("shard", None),
        P(None, "shard"),
        P("shard", "rep"),
        P(None, "shard", "rep"),
        P("shard", "rep"),
        P(None, None, "shard", "rep"),
        P(None, "shard", "rep"),
        P("shard", None),
        P(None, "shard"),
        P("rep", "shard", None),
        P("rep", None, "shard", None),
        P("rep", "shard", None),
        P("rep", None, None, "shard", None),
        P("rep", None, "shard", None),
        P(),
        P(),
        P(),
        P(),
        P(),
    )
    out_specs = (
        P(("rep", "shard"), None),
        P(("rep", "shard"), None),
        P("shard", None),
        P(None, "shard", None),
        P("shard", None),
        P(None, None, "shard", None),
        P(None, "shard", None),
        P(),
        P(),
        P(),
        P(),
        P(),
        P("rep", "shard", None),
        P("rep", None, "shard", None),
        P("rep", "shard", None),
        P("rep", None, None, "shard", None),
        P("rep", None, "shard", None),
        P("shard", "rep"),
        P(None, "shard", "rep"),
        P("shard", "rep"),
        P(None, None, "shard", "rep"),
        P(None, "shard", "rep"),
        P("shard", None),
        P(None, "shard"),
        P("shard", "rep"),
        P(None, "shard", "rep"),
        P("shard", "rep"),
        P(None, None, "shard", "rep"),
        P(None, "shard", "rep"),
        P("shard", None),
        P(None, "shard"),
        P(),
    )
    return jax.shard_map(
        per_device, mesh=mesh, in_specs=in_specs, out_specs=out_specs, check_vma=False
    )
```

```python
import functools

import jax
import jax.numpy as jnp
from jax import lax
from jax.experimental import pallas as pl
from jax.experimental.pallas import tpu as pltpu
from jax.sharding import PartitionSpec as P

D = 1536
HQ = 12
HK = 2
HD = 128
F = 768
E = 8
TOK_DEV = 512
QW = 1536


EPSILON = 1e-05
ROPE_BASE = 1000000.0
MOMENTUM_DECAY = 0.9
WEIGHT_DECAY = 0.01
STEP_RATE = 4.0
GAIN_RATE = 3.0
HIGHEST = lax.Precision.HIGHEST


def rms_norm(hidden, gain_row):
    return (
        hidden * lax.rsqrt(jnp.mean(hidden * hidden, axis=-1, keepdims=True) + EPSILON) * gain_row
    )


def path_mask(segment, parent_row):
    table_ids = jnp.arange(parent_row.shape[0], dtype=jnp.int32)
    parent_one = jnp.sum(
        jnp.where(segment[:, None] == table_ids[None, :], parent_row[None, :], 0), axis=1
    )
    parent_two = jnp.where(
        parent_one >= 0,
        jnp.sum(
            jnp.where(parent_one[:, None] == table_ids[None, :], parent_row[None, :], 0), axis=1
        ),
        -1,
    )
    token_order = jnp.arange(segment.shape[0], dtype=jnp.int32)
    same_path = (segment[:, None] == segment[None, :]) & (
        token_order[None, :] <= token_order[:, None]
    )
    return (
        same_path
        | (segment[None, :] == parent_one[:, None])
        | (segment[None, :] == parent_two[:, None])
    )


def advance(weight_now, moment_now, direction, step_rate, decay_rate):
    moment_new = MOMENTUM_DECAY * moment_now + (1.0 - MOMENTUM_DECAY) * direction
    return (weight_now - step_rate * (moment_new + decay_rate * weight_now), moment_new)


CHUNKS = 4
PARTS = 2
GELU_C = 0.7978845608028654
GELU_A = 0.044715
MESH = pl.DeviceIdType.MESH
VMEM_LIMIT = 60 * 1024 * 1024
F32 = jnp.float32
BF16 = jnp.bfloat16


def z_slots(block):
    size = lax.axis_size("shard")
    return [block] + [
        lax.ppermute(block, "shard", [(i, (i + step) % size) for i in range(size)])
        for step in range(1, size)
    ]


def nn(a, b, precision=None):
    return jnp.dot(a, b, preferred_element_type=F32, precision=precision)


def nt(a, b, precision=None):
    return lax.dot_general(
        a, b, (((1,), (1,)), ((), ())), preferred_element_type=F32, precision=precision
    )


def tn(a, b):
    return lax.dot_general(a, b, (((0,), (0,)), ((), ())), preferred_element_type=F32)


def up_to(count, unit):
    return -(-count // unit) * unit


def two_terms(value):
    high = value.astype(BF16)
    return high, (value - high.astype(F32)).astype(BF16)


def three_terms(value):
    high = value.astype(BF16)
    rest = value - high.astype(F32)
    middle = rest.astype(BF16)
    low = (rest - middle.astype(F32)).astype(BF16)
    return jnp.concatenate([high.astype(F32), middle.astype(F32), low.astype(F32)], axis=0).astype(BF16)


def folded(value, rows=8):
    return value[:rows] + value[rows : 2 * rows] + value[2 * rows : 3 * rows]


def exact_nn(value, other):
    return folded(nn(three_terms(value), other))


def exact_nt(value, other):
    return folded(nt(three_terms(value), other))


def padded(value, width):
    if value.shape[1] == width:
        return value
    return jnp.concatenate(
        [value, jnp.zeros((value.shape[0], width - value.shape[1]), value.dtype)], axis=1
    )


def params(**more):
    return pltpu.CompilerParams(vmem_limit_bytes=VMEM_LIMIT, **more)


def vmem_specs(count):
    return [pl.BlockSpec(memory_space=pltpu.VMEM)] * count


def struct(shape, dtype=F32):
    return jax.ShapeDtypeStruct(shape, dtype)


def turn_heads(value, cosine, sine):
    return value * cosine + pltpu.roll(value, HD // 2, 1) * sine


def softmax_of(query, key, mask):
    raw = nt(query, key) * HD ** (-0.5)
    masked = jnp.where(mask > 0, raw, -1e30)
    raised = jnp.exp(masked - jnp.max(masked, axis=-1, keepdims=True))
    return raised / jnp.sum(raised, axis=-1, keepdims=True)


def head_lanes(head):
    return pl.ds(pl.multiple_of(head * HD, HD), HD)


def attention_forward_kernel(
    first_ref, query_ref, key_ref, value_ref, output_ref, tokens_ref, cosine_ref, sine_ref, mask_ref,
    qrot_ref, krot_ref, values_ref, mixed_ref, middle_ref,
):
    first = first_ref[...]
    cosine, sine = cosine_ref[...], sine_ref[...]
    values_ref[...] = nt(first, value_ref[...]).astype(BF16)
    keys = nt(first, key_ref[...])
    for g in range(HK):
        span = slice(g * HD, (g + 1) * HD)
        krot_ref[:, span] = turn_heads(keys[:, span], cosine, sine).astype(BF16)
    queries = nt(first, query_ref[...])
    for h in range(HQ):
        span = slice(h * HD, (h + 1) * HD)
        qrot_ref[:, span] = turn_heads(queries[:, span], cosine, sine).astype(BF16)

    @pl.loop(0, HQ, unroll=2)
    def _(head):
        group = head_lanes(head // (HQ // HK))
        share = softmax_of(qrot_ref[:, head_lanes(head)], krot_ref[:, group], mask_ref[...])
        mixed_ref[:, head_lanes(head)] = nn(share.astype(BF16), values_ref[:, group]).astype(BF16)

    middle_ref[...] = tokens_ref[...].astype(F32) + nt(mixed_ref[...], output_ref[...])


def attention_forward(operands):
    length, width = operands[0].shape
    kv = HK * HD
    return pl.pallas_call(
        attention_forward_kernel,
        in_specs=vmem_specs(len(operands)),
        out_specs=vmem_specs(5),
        out_shape=[
            struct((length, HQ * HD), BF16),
            struct((length, kv), BF16),
            struct((length, kv), BF16),
            struct((length, HQ * HD), BF16),
            struct((length, width)),
        ],
        cost_estimate=pl.CostEstimate(
            flops=2 * length * width * (2 * HQ * HD + 2 * kv) + 4 * HQ * HD * length * length,
            bytes_accessed=14 * length * width + 4 * width * HQ * HD,
            transcendentals=HQ * length * length,
        ),
        compiler_params=params(),
        name="attention_forward",
    )(*operands)


def attention_backward_kernel(
    middle_ref, output_ref, qrot_ref, krot_ref, values_ref, cosine_ref, sine_ref, mask_ref, first_ref,
    late_ref, joint_ref, grad_ref, mixed_ref, dk_ref, dv_ref,
):
    cosine, sine = cosine_ref[...], -sine_ref[...]
    mixed_ref[...] = nn(middle_ref[...], output_ref[...]).astype(BF16)
    dk_ref[...] = jnp.zeros_like(dk_ref)
    dv_ref[...] = jnp.zeros_like(dv_ref)

    @pl.loop(0, HQ, unroll=2)
    def _(head):
        lanes, group = head_lanes(head), head_lanes(head // (HQ // HK))
        query, key = qrot_ref[:, lanes], krot_ref[:, group]
        upstream = mixed_ref[:, lanes]
        share = softmax_of(query, key, mask_ref[...])
        grad = nt(upstream, values_ref[:, group])
        score = share * (grad - jnp.sum(share * grad, axis=-1, keepdims=True))
        score = score.astype(BF16)
        turned = nn(score, key) * HD ** (-0.5)
        joint_ref[:, lanes] = turn_heads(turned, cosine, sine).astype(BF16)
        dk_ref[:, group] += tn(score, query)
        dv_ref[:, group] += tn(share.astype(BF16), upstream)

    qw = HQ * HD
    for g in range(HK):
        span = slice(g * HD, (g + 1) * HD)
        turned = dk_ref[:, span] * HD ** (-0.5)
        joint_ref[:, qw + g * HD : qw + (g + 1) * HD] = turn_heads(turned, cosine, sine).astype(BF16)
    joint_ref[:, qw + HK * HD :] = dv_ref[...].astype(BF16)
    block = HK * HD

    @pl.loop(0, joint_ref.shape[1] // block)
    def _(k):
        lanes = pl.ds(pl.multiple_of(k * block, block), block)
        grad_ref[:, lanes] = tn(first_ref[...], joint_ref[:, lanes]).astype(BF16)


def attention_backward(operands):
    length, width = operands[0].shape
    kv = HK * HD
    return pl.pallas_call(
        attention_backward_kernel,
        in_specs=vmem_specs(len(operands)),
        out_specs=vmem_specs(2),
        out_shape=[
            struct((length, HQ * HD + 2 * kv), BF16),
            struct((width, HQ * HD + 2 * kv), BF16),
        ],
        scratch_shapes=[
            pltpu.VMEM((length, HQ * HD), BF16),
            pltpu.VMEM((length, kv), F32),
            pltpu.VMEM((length, kv), F32),
        ],
        cost_estimate=pl.CostEstimate(
            flops=8 * length * width * HQ * HD, bytes_accessed=length * width, transcendentals=0
        ),
        compiler_params=params(),
        name="attention_backward",
    )(*operands)


def weights_of(w1_ref, w2_ref, turned):
    here = lax.axis_index("shard")
    groups, lanes, _, double, span1 = w1_ref.shape
    f_cols = double // 2
    lanes2, _, groups2, _, f_rows, span2 = w2_ref.shape

    def joined(parts):
        return parts[0] if len(parts) == 1 else jnp.concatenate(parts, axis=1)

    def place(k, count):
        return lax.rem(here + (count - k), count) if turned else k

    def both(low, high):
        return joined(
            [
                w1_ref[low:high, place(k, lanes), 0].reshape((high - low) * double, span1)
                for k in range(lanes)
            ]
        )

    def first(a):
        return joined(
            [
                w1_ref[:, place(k, lanes), 0, a * f_cols : (a + 1) * f_cols, :].reshape(
                    groups * f_cols, span1
                )
                for k in range(lanes)
            ]
        )

    def second(low=0, high=groups2):
        if not turned:
            return joined(
                [w2_ref[k, 0, low:high, 0].reshape((high - low) * f_rows, span2) for k in range(lanes2)]
            )
        return jnp.concatenate(
            [
                joined([w2_ref[k, 0, place(g, groups2), 0] for k in range(lanes2)])
                for g in range(low, high)
            ],
            axis=0,
        )

    return groups, f_cols, both, first, second


def share_of(x_ref, expert, width):
    tail = x_ref[width : width + 2 * E, :].astype(F32)
    shares8 = tail[:E] + tail[E:]
    picked = lax.broadcasted_iota(jnp.int32, shares8.shape, 0) == expert
    return jnp.sum(jnp.where(picked, shares8, 0.0), axis=0, keepdims=True)


def hidden_backward(x, w1_ref, w2_ref, turned, br, act_ref, gt_ref, lanes):
    groups, f_cols, both, _, second = weights_of(w1_ref, w2_ref, turned)
    hidden = groups * f_cols
    groups2 = w2_ref.shape[2]
    parts = PARTS if groups % PARTS == 0 and groups2 % PARTS == 0 else 1
    for part in range(parts):
        low, high = part * groups // parts, (part + 1) * groups // parts
        low2, high2 = part * groups2 // parts, (part + 1) * groups2 // parts
        units = nn(both(low, high), x)
        act_grads = nn(second(low2, high2), br)
        hidden_part(low, high, f_cols, hidden, units, act_grads, act_ref, gt_ref, lanes)


def hidden_part(low, high, f_cols, hidden, units, act_grads, act_ref, gt_ref, lanes):
    for r in range(low, high):
        at = r - low
        gate = units[2 * at * f_cols : (2 * at + 1) * f_cols]
        up = units[(2 * at + 1) * f_cols : (2 * at + 2) * f_cols]
        act_grad = act_grads[at * f_cols : (at + 1) * f_cols]
        square = gate * gate
        bent = jnp.tanh(GELU_C * (gate + GELU_A * (square * gate)))
        lifted = 0.5 * (1.0 + bent)
        gelu = gate * lifted
        slope = lifted + 0.5 * gate * (1.0 - bent * bent) * (
            GELU_C * (1.0 + 3.0 * GELU_A * square)
        )
        act_ref[r * f_cols : (r + 1) * f_cols, lanes] = (gelu * up).astype(BF16)
        gt_ref[r * f_cols : (r + 1) * f_cols, lanes] = (act_grad * up * slope).astype(BF16)
        gt_ref[hidden + r * f_cols : hidden + (r + 1) * f_cols, lanes] = (
            act_grad * gelu
        ).astype(BF16)


def start_product(start, matrix):
    high, low = two_terms(start)
    both = jnp.concatenate([high.astype(F32), low.astype(F32)], axis=0).astype(BF16)
    top, rest = two_terms(matrix)
    first = nt(both, top)
    return first[:8] + first[8:] + nt(both, rest)[:8]


def own_kernel(
    first_expert, turned, x_ref, u_ref, up_ref, w1_ref, w2_ref, err_in_ref, err_out_ref, gate_ref,
    min_ref, mout_ref, y_ref, sg_ref, cg_ref, gt_ref, act_ref, br_ref,
):
    expert = first_expert + pl.program_id(0)
    width = up_ref.shape[1]
    _, _, _, first_weight, second_weight = weights_of(w1_ref, w2_ref, turned)
    rows, out_rows = min_ref.shape[2], mout_ref.shape[1]
    hidden = min_ref.shape[3]
    here = lax.axis_index("shard")
    share = share_of(x_ref, expert, width)
    br_ref[...] = (share * u_ref[...].astype(F32)).astype(BF16)
    hidden_backward(
        x_ref[:width, :], w1_ref, w2_ref, turned, br_ref[...], act_ref, gt_ref, slice(None)
    )
    own_x = x_ref[pl.ds(pl.multiple_of(here * rows, 16), rows), :]
    for a in range(2):
        min_ref[a, 0] = err_in_ref[a, 0] + nt(own_x, gt_ref[a * hidden : (a + 1) * hidden, :])
    own_act = act_ref[pl.ds(pl.multiple_of(here * out_rows, 16), out_rows), :]
    mout_ref[0] = err_out_ref[0] + nt(own_act, br_ref[...])
    expert_out = tn(act_ref[...], second_weight())
    cg_ref[0] = jnp.sum(up_ref[...].astype(F32) * expert_out, axis=1, keepdims=True)
    share_col = jnp.transpose(jnp.broadcast_to(share, (8, share.shape[1])))[:, :1]
    added = share_col * expert_out
    grown = tn(gt_ref[:hidden, :], first_weight(0)) + tn(gt_ref[hidden:, :], first_weight(1))

    @pl.when(pl.program_id(0) == 0)
    def _():
        y_ref[...] = added
        sg_ref[...] = grown

    @pl.when(pl.program_id(0) > 0)
    def _():
        y_ref[...] += added
        sg_ref[...] += grown


def rest_kernel(
    first_expert, trees, last, turned, w1_ref, w2_ref, start_in_ref, start_out_ref, min_in_ref,
    mout_in_ref, *rest,
):
    x_refs, u_refs = rest[:trees], rest[trees : 2 * trees]
    min_ref, mout_ref = rest[2 * trees + 1 : 2 * trees + 3]
    gt_ref, act_ref, br_ref = rest[-3:]
    expert = first_expert + pl.program_id(0)
    rows, out_rows = min_ref.shape[2], mout_ref.shape[1]
    hidden, width = min_ref.shape[3], mout_ref.shape[2]
    length = x_refs[0].shape[1]
    here = lax.axis_index("shard")
    for tree in range(trees):
        x_ref = x_refs[tree]
        lanes = slice(tree * length, (tree + 1) * length)
        share = share_of(x_ref, expert, width)
        br_ref[:, lanes] = (share * u_refs[tree][...].astype(F32)).astype(BF16)
        hidden_backward(
            x_ref[:width, :], w1_ref, w2_ref, turned, br_ref[:, lanes], act_ref, gt_ref, lanes
        )
    own_x = jnp.concatenate(
        [x_ref[pl.ds(pl.multiple_of(here * rows, 16), rows), :] for x_ref in x_refs], axis=1
    )
    for a in range(2):
        min_ref[a, 0] = min_in_ref[a, 0] + nt(own_x, gt_ref[a * hidden : (a + 1) * hidden, :])
    own_act = act_ref[pl.ds(pl.multiple_of(here * out_rows, 16), out_rows), :]
    mout_ref[0] = mout_in_ref[0] + nt(own_act, br_ref[...])
    if last:
        lin_ref, lout_ref = rest[2 * trees + 3 : 2 * trees + 5]
        lin_ref[...] = jnp.zeros_like(lin_ref)
        lout_ref[...] = jnp.zeros_like(lout_ref)
        for a in range(2):
            lin_ref[0, a, :, :rows] = start_product(start_in_ref[a, 0], min_ref[a, 0])
        lout_ref[0, :, :out_rows] = start_product(start_out_ref[0], mout_ref[0])


def whole_block(shape):
    return pl.BlockSpec(shape, lambda e: (0,) * len(shape), pipeline_mode=pl.Buffered(1))


def weight_blocks(w1, w2):
    last_block = w2.shape[3] - 1
    return [
        pl.BlockSpec((*w1.shape[:2], 1, *w1.shape[3:]), lambda e: (0, 0, e, 0, 0)),
        pl.BlockSpec(
            (w2.shape[0], 1, w2.shape[2], 1, *w2.shape[4:]), lambda e: (0, e, 0, last_block, 0, 0)
        ),
    ]


def matrix_blocks(first_expert, shape_in, shape_out):
    return [
        pl.BlockSpec(
            (shape_in[0], 1, *shape_in[2:]), lambda e: (0, first_expert + e, 0, 0)
        ),
        pl.BlockSpec((1, *shape_out[1:]), lambda e: (first_expert + e, 0, 0)),
    ]


def own_experts(first_expert, x, u, upstream, weights, err_in, err_out, gate):
    w1, w2, turned = weights
    count = w2.shape[1]
    hidden, rows = err_in.shape[3], err_in.shape[2]
    length, width = upstream.shape
    matrices = matrix_blocks(first_expert, err_in.shape, err_out.shape)
    in_specs = [
        whole_block(x.shape),
        whole_block(u.shape),
        whole_block(upstream.shape),
        *weight_blocks(w1, w2),
        *matrices,
        pl.BlockSpec(memory_space=pl.ANY),
    ]
    operands = [x, u, upstream, w1, w2, err_in, err_out, gate]
    part_in, part_out = (2, count, rows, hidden), (count, *err_out.shape[1:])
    return pl.pallas_call(
        functools.partial(own_kernel, first_expert, turned),
        grid=(count,),
        in_specs=in_specs,
        out_specs=[
            *matrix_blocks(0, part_in, part_out),
            whole_block((length, width)),
            whole_block((length, width)),
            pl.BlockSpec((1, length, 1), lambda e: (e, 0, 0)),
        ],
        out_shape=[
            struct(part_in),
            struct(part_out),
            struct((length, width)),
            struct((length, width)),
            struct((count, length, 1)),
        ],
        scratch_shapes=[
            pltpu.VMEM((2 * hidden, length), BF16),
            pltpu.VMEM((hidden, length), BF16),
            pltpu.VMEM((width, length), BF16),
        ],
        cost_estimate=pl.CostEstimate(
            flops=28 * count * hidden * width * length,
            bytes_accessed=count * (6 * hidden * width + 24 * rows * hidden) + 12 * length * width,
            transcendentals=0,
        ),
        compiler_params=params(),
        name="own_experts",
    )(*operands)


def rest_experts(first_expert, last, xs, us, weights, start_in, start_out, merged_in, merged_out, gate):
    w1, w2, turned = weights
    count, trees = w2.shape[1], len(xs)
    hidden, rows = merged_in.shape[3], merged_in.shape[2]
    out_rows = merged_out.shape[1]
    width, length = merged_out.shape[2], xs[0].shape[1]
    matrices = matrix_blocks(0, merged_in.shape, merged_out.shape)
    wide, wide_out = up_to(rows, 128), up_to(out_rows, 128)
    out_specs = list(matrices)
    out_shape = [struct(merged_in.shape), struct(merged_out.shape)]
    if last:
        out_specs += [
            pl.BlockSpec((1, 2, 8, wide), lambda e: (e, 0, 0, 0)),
            pl.BlockSpec((1, 8, wide_out), lambda e: (e, 0, 0)),
        ]
        out_shape += [struct((count, 2, 8, wide)), struct((count, 8, wide_out))]
    return pl.pallas_call(
        functools.partial(rest_kernel, first_expert, trees, last, turned),
        grid=(count,),
        in_specs=[
            *weight_blocks(w1, w2),
            *matrix_blocks(first_expert, start_in.shape, start_out.shape),
            *matrices,
            *[whole_block(x.shape) for x in (*xs, *us)],
            pl.BlockSpec(memory_space=pl.ANY),
        ],
        out_specs=out_specs,
        out_shape=out_shape,
        scratch_shapes=[
            pltpu.VMEM((2 * hidden, trees * length), BF16),
            pltpu.VMEM((hidden, trees * length), BF16),
            pltpu.VMEM((width, trees * length), BF16),
        ],
        input_output_aliases={4: 0, 5: 1},
        cost_estimate=pl.CostEstimate(
            flops=14 * count * trees * hidden * width * length,
            bytes_accessed=count * (6 * hidden * width + 24 * rows * hidden),
            transcendentals=0,
        ),
        compiler_params=params(),
        name="rest_experts",
    )(w1, w2, start_in, start_out, merged_in, merged_out, *xs, *us, gate)


def open_kernel(reps, shards, pieces, extra, *refs):
    count = len(pieces)
    arrays = count + 1 + extra
    sources, hop_ref = refs[:arrays], refs[arrays]
    targets, from_below, from_above = refs[arrays + 1 : 2 * arrays + 1], refs[2 * arrays + 1], refs[2 * arrays + 2]
    local_sem, up_send, up_recv, down_send, down_recv, chip_send, chip_recv, core_send, core_recv = refs[
        2 * arrays + 3 : -2
    ]
    hop_send, hop_recv = refs[-2:]
    rep, shard = lax.axis_index("rep"), lax.axis_index("shard")
    chips, core = reps // 2, rep % 2
    chip = rep // 2
    total = count + 1 + extra

    def slot(k, which):
        if k > count:
            return targets[k].at[which]
        span = sources[k].shape[1]
        lanes = pl.ds(pl.multiple_of(which * span, span), span)
        height = sources[k].shape[0]
        if k == count:
            return targets[k].at[:, lanes]
        row = pieces[k] + rep * height
        return targets[k].at[pl.ds(pl.multiple_of(row, 16), height), lanes]

    def band(k, which):
        height = sources[k].shape[0]
        row = pieces[k] + which * height
        return targets[k].at[pl.ds(pl.multiple_of(row, 16), height), :]

    barrier = pltpu.get_barrier_semaphore()
    for step in range(1, shards):
        pl.semaphore_signal(
            barrier, inc=1, device_id={"shard": lax.rem(shard + step, shards)}, device_id_type=MESH
        )
    for step in range(1, chips):
        to = lax.rem(chip + step, chips) * 2 + core
        pl.semaphore_signal(barrier, inc=1, device_id={"rep": to}, device_id_type=MESH)
    pl.semaphore_signal(barrier, inc=1, device_id={"rep": rep + 1 - 2 * core}, device_id_type=MESH)
    pl.semaphore_wait(barrier, shards - 1 + chips)

    locals_ = []
    for k in range(total):
        copy = pltpu.make_async_copy(sources[k], slot(k, shard), local_sem.at[k])
        copy.start()
        locals_.append(copy)

    def up_copy(k, step):
        source = sources[k] if step == 0 else slot(k, shard - step)
        return pltpu.make_async_remote_copy(
            src_ref=source,
            dst_ref=slot(k, shard - step),
            send_sem=up_send.at[k, step],
            recv_sem=up_recv.at[k, step],
            device_id={"shard": lax.rem(shard + 1, shards)},
            device_id_type=MESH,
        )

    def down_copy(k, step):
        source = sources[k] if step == 0 else slot(k, shard + step)
        return pltpu.make_async_remote_copy(
            src_ref=source,
            dst_ref=slot(k, shard + step),
            send_sem=down_send.at[k, step],
            recv_sem=down_recv.at[k, step],
            device_id={"shard": lax.rem(shard + shards - 1, shards)},
            device_id_type=MESH,
        )

    def hop(to_above):
        return pltpu.make_async_remote_copy(
            src_ref=hop_ref,
            dst_ref=from_below if to_above else from_above,
            send_sem=hop_send.at[int(to_above)],
            recv_sem=hop_recv.at[int(to_above)],
            device_id={"shard": lax.rem(shard + (1 if to_above else shards - 1), shards)},
            device_id_type=MESH,
        )

    def line_step(group, step):
        @pl.when((shard < shards - 1) & (step <= shard))
        def _():
            for k in group:
                up_copy(k, step).start()

        @pl.when((shard > 0) & (step <= shards - 1 - shard))
        def _():
            for k in group:
                down_copy(k, step).start()

    def line_arrive(group, step):
        @pl.when(step <= shard - 1)
        def _():
            for k in group:
                pltpu.make_async_remote_copy(
                    src_ref=slot(k, shard - 1 - step),
                    dst_ref=slot(k, shard - 1 - step),
                    send_sem=up_send.at[k, step],
                    recv_sem=up_recv.at[k, step],
                    device_id={"shard": lax.rem(shard + 1, shards)},
                    device_id_type=MESH,
                ).wait_recv()

        @pl.when(step <= shards - 2 - shard)
        def _():
            for k in group:
                pltpu.make_async_remote_copy(
                    src_ref=slot(k, shard + 1 + step),
                    dst_ref=slot(k, shard + 1 + step),
                    send_sem=down_send.at[k, step],
                    recv_sem=down_recv.at[k, step],
                    device_id={"shard": lax.rem(shard + 1, shards)},
                    device_id_type=MESH,
                ).wait_recv()

    def line_sent(group, step):
        @pl.when((shard < shards - 1) & (step <= shard))
        def _():
            for k in group:
                up_copy(k, step).wait_send()

        @pl.when((shard > 0) & (step <= shards - 1 - shard))
        def _():
            for k in group:
                down_copy(k, step).wait_send()

    first = list(range(count + 1))
    later = list(range(count + 1, total))
    for step in range(shards - 1):
        line_step(first, step)
        line_arrive(first, step)
    line_step(later, 0)

    @pl.when(shard < shards - 1)
    def _():
        hop(True).start()

    @pl.when(shard > 0)
    def _():
        hop(False).start()

    for copy in locals_:
        copy.wait()

    def chip_copy(k, step):
        to = lax.rem(chip + step, chips) * 2 + core
        return pltpu.make_async_remote_copy(
            src_ref=band(k, rep),
            dst_ref=band(k, rep),
            send_sem=chip_send.at[k, step - 1],
            recv_sem=chip_recv.at[k, step - 1],
            device_id={"rep": to},
            device_id_type=MESH,
        )

    def core_copy(k, step):
        owner = lax.rem(chip + chips - step, chips) * 2 + core
        return pltpu.make_async_remote_copy(
            src_ref=band(k, owner),
            dst_ref=band(k, owner),
            send_sem=core_send.at[k, step],
            recv_sem=core_recv.at[k, step],
            device_id={"rep": rep + 1 - 2 * core},
            device_id_type=MESH,
        )

    for step in range(1, chips):
        for k in range(count):
            chip_copy(k, step).start()
    for k in range(count):
        core_copy(k, 0).start()
    for step in range(1, shards - 1):
        line_arrive(later, step - 1)
        line_step(later, step)
    for step in range(1, chips):
        for k in range(count):
            chip_copy(k, step).wait_recv()
            core_copy(k, step).start()
    if shards > 1:
        line_arrive(later, shards - 2)
    for step in range(chips):
        for k in range(count):
            core_copy(k, step).wait()
            if step:
                chip_copy(k, step).wait_send()
    for step in range(shards - 1):
        line_sent(first + later, step)

    @pl.when(shard < shards - 1)
    def _():
        hop(True).wait_send()
        hop(False).wait_recv()

    @pl.when(shard > 0)
    def _():
        hop(False).wait_send()
        hop(True).wait_recv()


def open_gather(reps, shards, bands, small, lines, hop):
    operands = [operand for _, operand in bands] + [small] + list(lines)
    dma = pltpu.SemaphoreType.DMA
    count, total, chips = len(bands), len(operands), reps // 2
    operands.append(hop)
    span = small.shape[1]
    shapes = [struct((reps * operand.shape[0], shards * span), BF16) for _, operand in bands]
    shapes.append(struct((small.shape[0], shards * span), BF16))
    shapes += [struct((shards, *line.shape), BF16) for line in lines]
    shapes += [struct(hop.shape, BF16)] * 2
    anywhere = pl.BlockSpec(memory_space=pl.ANY)
    return pl.pallas_call(
        functools.partial(open_kernel, reps, shards, [at for at, _ in bands], len(lines)),
        in_specs=[anywhere] * (total + 1),
        out_specs=[anywhere] * (total + 2),
        out_shape=shapes,
        scratch_shapes=[
            dma((total,)),
            dma((total, shards - 1)),
            dma((total, shards - 1)),
            dma((total, shards - 1)),
            dma((total, shards - 1)),
            dma((count, chips)),
            dma((count, chips)),
            dma((count, chips)),
            dma((count, chips)),
            dma((2,)),
            dma((2,)),
        ],
        compiler_params=params(collective_id=4, has_side_effects=True),
        name="open_gather",
    )(*operands)


def packed_rows(value):
    half = value.shape[1] // 2
    return jnp.concatenate([value[:, :half], value[:, half:]], axis=0).astype(BF16)


def unpacked_rows(value):
    value = value.astype(F32)
    return jnp.concatenate([value[:8], value[8:]], axis=1)


def left_parts_kernel(
    shards, rows, wide, first_ref, joint_ref, mixed_ref, middle_ref, sq_ref, sk_ref, sv_ref, so_ref,
    eq_ref, ep_ref, eo_ref, router_ref, gains_ref, z_ref, own_ref,
):
    qw, kv = sq_ref.shape[1], sk_ref.shape[1]
    first = first_ref[...]
    pieces = []
    for start_ref, low in ((sq_ref, 0), (sk_ref, qw), (sv_ref, qw + kv)):
        high = low + start_ref.shape[1]
        pieces.append(exact_nn(exact_nt(start_ref[...], joint_ref[:, low:high]), first))
    pieces.append(exact_nn(exact_nt(so_ref[...], middle_ref[...]), mixed_ref[...]))
    pieces.append(router_ref[...])
    pieces.append(gains_ref[...])
    for shard in range(shards):
        z_ref[shard] = packed_rows(
            jnp.concatenate(
                [padded(piece[:, shard * rows : (shard + 1) * rows], wide) for piece in pieces],
                axis=1,
            )
        )
    errors = (
        start_product(sq_ref[...], eq_ref[...]),
        start_product(sk_ref[...], ep_ref[0]),
        start_product(sv_ref[...], ep_ref[1]),
        start_product(so_ref[...], eo_ref[...]),
    )
    for k, piece in enumerate(errors):
        own_ref[:, k * wide : (k + 1) * wide] = padded(piece, wide)


def left_parts(shards, rows, operands):
    wide = up_to(rows, 128)
    return pl.pallas_call(
        functools.partial(left_parts_kernel, shards, rows, wide),
        in_specs=vmem_specs(len(operands)),
        out_specs=vmem_specs(2),
        out_shape=[struct((shards, 16, 3 * wide), BF16), struct((8, 4 * wide))],
        compiler_params=params(),
        name="left_parts",
    )(*operands)


def greet(reps, shards):
    rep, shard = lax.axis_index("rep"), lax.axis_index("shard")
    barrier = pltpu.get_barrier_semaphore()
    for step in range(1, shards):
        pl.semaphore_signal(
            barrier, inc=1, device_id={"shard": lax.rem(shard + step, shards)}, device_id_type=MESH
        )
    for step in range(1, reps):
        pl.semaphore_signal(
            barrier, inc=1, device_id={"rep": lax.rem(rep + step, reps)}, device_id_type=MESH
        )
    pl.semaphore_wait(barrier, reps + shards - 2)


def start_all(axis, size, source, target, send, recv):
    here = lax.axis_index(axis)
    copies = []
    for step in range(1, size):
        to = lax.rem(here + step, size)
        copy = pltpu.make_async_remote_copy(
            src_ref=source(to),
            dst_ref=target(step),
            send_sem=send.at[step - 1],
            recv_sem=recv.at[step - 1],
            device_id={axis: to},
            device_id_type=MESH,
        )
        copy.start()
        copies.append(copy)
    return copies


def send_all(axis, size, source, target, send, recv):
    for copy in start_all(axis, size, source, target, send, recv):
        copy.wait()


def blocks_on_diagonal(square):
    size = square.shape[0]
    row = lax.broadcasted_iota(jnp.int32, (size, size), 0) // 8
    lane = lax.broadcasted_iota(jnp.int32, (size, size), 1) // 8
    kept = jnp.where(row == lane, square, 0.0)
    total = kept[:8]
    for k in range(1, size // 8):
        total = total + kept[8 * k : 8 * k + 8]
    return total


def spread_on_diagonal(flat):
    size = flat.shape[1]
    tall = jnp.concatenate([flat] * (size // 8), axis=0)
    row = lax.broadcasted_iota(jnp.int32, (size, size), 0) // 8
    lane = lax.broadcasted_iota(jnp.int32, (size, size), 1) // 8
    return jnp.transpose(jnp.where(row == lane, tall, 0.0))


def left_sync_kernel(reps, shards, wide, wide_out, piece, count, *refs):
    z_ref, own_ref = refs[:2]
    lin_refs, lout_refs = refs[2 : 2 + count], refs[2 + count : 2 + 2 * count]
    refs = refs[3 + 2 * count :]
    left_ref, left_out_ref, totals_ref, squares_ref, leftz_ref = refs[:5]
    (zbuf, parts, heard, total, grams, lanes_z, zs, zr, ps, pr, gs, gr, hs, hr, ls, lr) = refs[5:]
    rep, shard = lax.axis_index("rep"), lax.axis_index("shard")
    greet(reps, shards)
    send_all("shard", shards, lambda to: z_ref.at[to], lambda step: zbuf.at[step - 1], zs, zr)
    front = unpacked_rows(z_ref[shard])
    for step in range(shards - 1):
        front = front + unpacked_rows(zbuf[step])
    ins = [ref[e, a] for a in range(2) for ref in lin_refs for e in range(ref.shape[0])]
    outs = [ref[e] for ref in lout_refs for e in range(ref.shape[0])]
    line = jnp.concatenate(
        [front[:, : 4 * wide] + own_ref[...], front[:, 4 * wide :], *ins, *outs], axis=1
    )
    line = padded(line, reps * piece)
    for k in range(reps):
        parts[k] = packed_rows(line[:, k * piece : (k + 1) * piece])
    send_all("rep", reps, lambda to: parts.at[to], lambda step: heard.at[step - 1], ps, pr)
    mine = parts[rep].astype(F32)
    for step in range(reps - 1):
        mine = mine + heard[step].astype(F32)
    total[rep] = mine.astype(BF16)
    send_all("rep", reps, lambda to: total.at[rep], lambda step: total.at[rep], gs, gr)
    line = jnp.concatenate([unpacked_rows(total[k]) for k in range(reps)], axis=1)
    inner = len(ins)
    matrices = [line[:, k * wide : (k + 1) * wide] for k in range(4)]
    matrices += [line[:, (6 + k) * wide : (7 + k) * wide] for k in range(inner)]
    base = (6 + inner) * wide
    outers = [line[:, base + k * wide_out : base + (k + 1) * wide_out] for k in range(len(outs))]
    router, gains = line[:, 4 * wide : 5 * wide], line[:, 5 * wide : 6 * wide]
    size, size_out = up_to(8 * len(matrices), 128), up_to(8 * len(outers), 128)
    stack = jnp.concatenate(
        matrices + [jnp.zeros((size - 8 * len(matrices), wide), F32)], axis=0
    )
    stack_out = jnp.concatenate(
        outers + [jnp.zeros((size_out - 8 * len(outers), wide_out), F32)], axis=0
    )
    gram = blocks_on_diagonal(nt(stack, stack, HIGHEST))
    gram_out = blocks_on_diagonal(nt(stack_out, stack_out, HIGHEST))
    row = lax.broadcasted_iota(jnp.int32, (8, 128), 0)
    lane = lax.broadcasted_iota(jnp.int32, (8, 128), 1)
    more = jnp.where(lane == 0, jnp.sum(router * router, axis=1, keepdims=True), 0.0)
    more = jnp.where(lane == 1, jnp.sum(gains * gains, axis=1, keepdims=True), more)
    grams[shard] = jnp.concatenate([gram, gram_out, more], axis=1)
    lanes_z[shard] = stack[:32]
    sent = start_all("shard", shards, lambda to: grams.at[shard], lambda step: grams.at[shard], hs, hr)
    sent += start_all(
        "shard", shards, lambda to: lanes_z.at[shard], lambda step: lanes_z.at[shard], ls, lr
    )
    for copy in sent:
        copy.wait()
    gram = grams[0]
    for k in range(1, shards):
        gram = gram + grams[k]
    both = size + size_out
    squares_ref[...] = gram[:, both:]
    totals_ref[0] = router
    totals_ref[1] = gains
    where_from = lax.broadcasted_iota(jnp.int32, (both, 1024), 0)
    where_to = lax.broadcasted_iota(jnp.int32, (both, 1024), 1)
    chosen = jnp.where(
        (where_from % 8 == where_to // 128) & (where_from // 8 == where_to % 128), 1.0, 0.0
    ).astype(BF16)
    lines = exact_nn(gram[:, :both], chosen)
    used = (lane < len(matrices)) | ((lane >= size // 8) & (lane < size // 8 + len(outers)))
    table = [
        jnp.where(used, lines[:, 128 * k : 128 * k + 128], jnp.where(row == k, 1.0, 0.0))
        for k in range(8)
    ]
    inverse = [jnp.where(row == k, 1.0, 0.0) for k in range(8)]
    for k in range(8):
        pivot = table[k][k : k + 1]
        over = 1.0 / pivot
        for i in range(k + 1, 8):
            factor = table[i][k : k + 1] * over
            table[i] = table[i] - factor * table[k]
            inverse[i] = inverse[i] - factor * inverse[k]
        inverse[k] = inverse[k] / jnp.sqrt(pivot)
    flat = exact_nt(jnp.concatenate(inverse, axis=1), chosen)
    solve = spread_on_diagonal(flat[:, :size])
    lefts = nn(solve, stack, HIGHEST)
    lefts_out = nn(spread_on_diagonal(flat[:, size:]), stack_out, HIGHEST)
    left_ref[...] = lefts[: left_ref.shape[0]]
    left_out_ref[...] = lefts_out[: left_out_ref.shape[0]]
    for k in range(shards):
        leftz_ref[k] = nn(solve[:32, :32], lanes_z[k], HIGHEST)


def left_sync(reps, shards, z_part, own, lins, louts, late):
    wide, wide_out = lins[0].shape[3], louts[0].shape[2]
    inner, outer = 2 * sum(x.shape[0] for x in lins), sum(x.shape[0] for x in louts)
    piece = up_to(-(-((6 + inner) * wide + outer * wide_out) // reps), 256)
    matrices = 4 + inner
    size, size_out = up_to(8 * matrices, 128), up_to(8 * outer, 128)
    dma = pltpu.SemaphoreType.DMA
    operands = [z_part, own, *lins, *louts, late]
    return pl.pallas_call(
        functools.partial(left_sync_kernel, reps, shards, wide, wide_out, piece, len(lins)),
        in_specs=vmem_specs(len(operands)),
        out_specs=vmem_specs(5),
        out_shape=[
            struct((8 * matrices, wide)),
            struct((8 * outer, wide_out)),
            struct((2, 8, wide)),
            struct((8, 128)),
            struct((shards, 32, wide)),
        ],
        scratch_shapes=[
            pltpu.VMEM((shards - 1, 16, 3 * wide), BF16),
            pltpu.VMEM((reps, 16, piece // 2), BF16),
            pltpu.VMEM((reps - 1, 16, piece // 2), BF16),
            pltpu.VMEM((reps, 16, piece // 2), BF16),
            pltpu.VMEM((shards, 8, size + size_out + 128), F32),
            pltpu.VMEM((shards, 32, wide), F32),
            dma((shards - 1,)),
            dma((shards - 1,)),
            dma((reps - 1,)),
            dma((reps - 1,)),
            dma((reps - 1,)),
            dma((reps - 1,)),
            dma((shards - 1,)),
            dma((shards - 1,)),
            dma((shards - 1,)),
            dma((shards - 1,)),
        ],
        compiler_params=params(collective_id=1, has_side_effects=True),
        name="left_sync",
    )(*operands)


def left_product(left, matrix):
    high, low = two_terms(left)
    both = jnp.concatenate([high.astype(F32), low.astype(F32)], axis=0).astype(BF16)
    top, rest = two_terms(matrix)
    first = nn(both, top)
    return first[:8] + first[8:] + nn(both, rest)[:8]


def right_expert_kernel(left_ref, left_out_ref, min_ref, mout_ref, right_ref):
    rows, out_rows = min_ref.shape[2], mout_ref.shape[1]
    hidden = min_ref.shape[3]

    for a in range(2):
        right_ref[0, :, a * hidden : (a + 1) * hidden] = left_product(
            left_ref[a, 0, :, :rows], min_ref[a, 0]
        )
    right_ref[0, :, 2 * hidden :] = left_product(left_out_ref[0, :, :out_rows], mout_ref[0])


def right_experts(first_expert, lefts, lefts_out, merged_in, merged_out):
    count, rows, hidden = merged_in.shape[1:]
    out_rows, width = merged_out.shape[1:]
    wide, wide_out = lefts.shape[3], lefts_out.shape[2]
    return pl.pallas_call(
        right_expert_kernel,
        grid=(count,),
        in_specs=[
            pl.BlockSpec((2, 1, 8, wide), lambda e: (0, first_expert + e, 0, 0)),
            pl.BlockSpec((1, 8, wide_out), lambda e: (first_expert + e, 0, 0)),
            pl.BlockSpec((2, 1, rows, hidden), lambda e: (0, e, 0, 0)),
            pl.BlockSpec((1, out_rows, width), lambda e: (e, 0, 0)),
        ],
        out_specs=pl.BlockSpec((1, 8, 2 * hidden + width), lambda e: (e, 0, 0)),
        out_shape=struct((count, 8, 2 * hidden + width)),
        compiler_params=params(),
        name="right_experts",
    )(lefts, lefts_out, merged_in, merged_out)


def right_attention_kernel(
    shards, rows, left_ref, leftz_ref, first_ref, joint_ref, mixed_ref, middle_ref, eq_ref, ep_ref,
    eo_ref, right_ref,
):
    qw, kv = eq_ref.shape[1], ep_ref.shape[2]
    width = eo_ref.shape[1]

    def whole(k):
        return jnp.concatenate(
            [leftz_ref[z, 8 * k : 8 * k + 8, :rows] for z in range(shards)], axis=1
        )

    def own(k):
        return left_ref[8 * k : 8 * k + 8, :rows]

    first = first_ref[...]
    at = 0
    for k, error in ((0, eq_ref[...]), (1, ep_ref[0]), (2, ep_ref[1])):
        grown = exact_nn(exact_nt(whole(k), first), joint_ref[:, at : at + error.shape[1]])
        right_ref[:, at : at + error.shape[1]] = grown + left_product(own(k), error)
        at += error.shape[1]
    grown = exact_nn(exact_nt(whole(3), mixed_ref[...]), middle_ref[...])
    right_ref[:, at : at + width] = grown + left_product(own(3), eo_ref[...])


def right_attention(shards, rows, operands):
    width = operands[6].shape[1] + 2 * operands[7].shape[2] + operands[8].shape[1]
    return pl.pallas_call(
        functools.partial(right_attention_kernel, shards, rows),
        in_specs=vmem_specs(len(operands)),
        out_specs=pl.BlockSpec(memory_space=pltpu.VMEM),
        out_shape=struct((8, width)),
        compiler_params=params(),
        name="right_attention",
    )(*operands)


def right_sync_kernel(reps, shards, piece, count, *refs):
    experts_refs, attention_ref, out_ref = refs[:count], refs[count], refs[count + 1]
    parts, heard, across, total, ps, pr, zs, zr, gs, gr = refs[count + 2 :]
    rep, shard = lax.axis_index("rep"), lax.axis_index("shard")
    half = piece // 2
    greet(reps, shards)
    line = jnp.concatenate(
        [ref[e] for ref in experts_refs for e in range(ref.shape[0])] + [attention_ref[...]], axis=1
    )
    line = padded(line, reps * piece)
    for k in range(reps):
        at = k * piece
        parts[k] = jnp.concatenate(
            [line[:, at : at + half], line[:, at + half : at + piece]], axis=0
        ).astype(BF16)
    send_all("rep", reps, lambda to: parts.at[to], lambda step: heard.at[step - 1], ps, pr)
    mine = parts[rep].astype(F32)
    for step in range(reps - 1):
        mine = mine + heard[step].astype(F32)
    across[shard] = mine.astype(BF16)
    send_all("shard", shards, lambda to: across.at[shard], lambda step: across.at[shard], zs, zr)
    summed = across[0].astype(F32)
    for k in range(1, shards):
        summed = summed + across[k].astype(F32)
    total[rep] = summed.astype(BF16)
    send_all("rep", reps, lambda to: total.at[rep], lambda step: total.at[rep], gs, gr)
    for k in range(reps):
        block = total[k].astype(F32)
        out_ref[:, k * piece : k * piece + half] = block[:8]
        out_ref[:, k * piece + half : (k + 1) * piece] = block[8:]


def right_sync(reps, shards, experts, attention):
    columns = sum(part.shape[0] * part.shape[2] for part in experts) + attention.shape[1]
    piece = up_to(-(-columns // reps), 256)
    dma = pltpu.SemaphoreType.DMA
    return pl.pallas_call(
        functools.partial(right_sync_kernel, reps, shards, piece, len(experts)),
        in_specs=vmem_specs(len(experts) + 1),
        out_specs=pl.BlockSpec(memory_space=pltpu.VMEM),
        out_shape=struct((8, reps * piece)),
        scratch_shapes=[
            pltpu.VMEM((reps, 16, piece // 2), BF16),
            pltpu.VMEM((reps - 1, 16, piece // 2), BF16),
            pltpu.VMEM((shards, 16, piece // 2), BF16),
            pltpu.VMEM((reps, 16, piece // 2), BF16),
            dma((reps - 1,)),
            dma((reps - 1,)),
            dma((shards - 1,)),
            dma((shards - 1,)),
            dma((reps - 1,)),
            dma((reps - 1,)),
        ],
        compiler_params=params(collective_id=2, has_side_effects=True),
        name="right_sync",
    )(*experts, attention)


def low_rank(left, right):
    high, low = two_terms(left)
    lefts = jnp.concatenate([high.astype(F32), low.astype(F32)], axis=0).astype(BF16)
    rights = jnp.concatenate([right, right], axis=0).astype(BF16)
    return tn(lefts, rights)


def feedback_expert_kernel(
    replicas, first_expert, left_ref, left_out_ref, right_ref, min_ref, mout_ref, *rest
):
    fin_ref, fout_ref, sq_ref = rest[-3:]
    rows, hidden = min_ref.shape[2:]
    out_rows = mout_ref.shape[1]
    row = lax.broadcasted_iota(jnp.int32, (8, 128), 0)
    lane = lax.broadcasted_iota(jnp.int32, (8, 128), 1)

    @pl.when(pl.program_id(0) == 0)
    def _():
        sq_ref[...] = jnp.zeros_like(sq_ref)

    added = jnp.zeros((8, 128), F32)
    for a in range(2):
        approx = low_rank(
            left_ref[a, 0, :, :rows], right_ref[:, a * hidden : (a + 1) * hidden]
        )
        left_over = min_ref[a, 0] - approx * (1.0 / replicas)
        fin_ref[a, 0] = left_over
        added = jnp.where(lane == a, jnp.sum(left_over * left_over), added)
    approx = low_rank(left_out_ref[0, :, :out_rows], right_ref[:, 2 * hidden :])
    left_over = mout_ref[0] - approx * (1.0 / replicas)
    fout_ref[0] = left_over
    added = jnp.where(lane == 2, jnp.sum(left_over * left_over), added)
    sq_ref[...] += jnp.where(row == first_expert + pl.program_id(0), added, 0.0)


def feedback_experts(
    replicas, first_expert, lefts, lefts_out, rights, merged_in, merged_out, whole_in, whole_out
):
    count, rows, hidden = merged_in.shape[1:]
    out_rows, width = merged_out.shape[1:]
    wide, wide_out = lefts.shape[3], lefts_out.shape[2]
    shapes = (2, E, rows, hidden), (E, out_rows, width)
    operands = [lefts, lefts_out, rights, merged_in, merged_out]
    in_specs = [
        pl.BlockSpec((2, 1, 8, wide), lambda e: (0, first_expert + e, 0, 0)),
        pl.BlockSpec((1, 8, wide_out), lambda e: (first_expert + e, 0, 0)),
        pl.BlockSpec((8, 2 * hidden + width), lambda e: (0, first_expert + e)),
        *matrix_blocks(0, merged_in.shape, merged_out.shape),
    ]
    aliases = {}
    if whole_in is not None:
        operands += [whole_in, whole_out]
        in_specs += [pl.BlockSpec(memory_space=pl.ANY)] * 2
        aliases = {5: 0, 6: 1}
    return pl.pallas_call(
        functools.partial(feedback_expert_kernel, replicas, first_expert),
        grid=(count,),
        in_specs=in_specs,
        out_specs=[
            *matrix_blocks(first_expert, *shapes),
            pl.BlockSpec((8, 128), lambda e: (0, 0)),
        ],
        out_shape=[struct(shapes[0]), struct(shapes[1]), struct((8, 128))],
        input_output_aliases=aliases,
        compiler_params=params(),
        name="feedback_experts",
    )(*operands)


def feedback_attention_kernel(
    replicas, rows, left_ref, right_ref, gj_ref, go_ref, eq_ref, ep_ref, eo_ref, fq_ref, fp_ref,
    fo_ref, sq_ref,
):
    qw, kv = eq_ref.shape[1], ep_ref.shape[2]
    lane = lax.broadcasted_iota(jnp.int32, (8, 128), 1)
    row = lax.broadcasted_iota(jnp.int32, (8, 128), 0)
    added = jnp.zeros((8, 128), F32)
    at = 0
    jobs = (
        (gj_ref, 0, eq_ref, fq_ref),
        (gj_ref, qw, ep_ref.at[0], fp_ref.at[0]),
        (gj_ref, qw + kv, ep_ref.at[1], fp_ref.at[1]),
        (go_ref, 0, eo_ref, fo_ref),
    )
    for k, (grad_ref, low, error_ref, out_ref) in enumerate(jobs):
        width = error_ref.shape[1]
        approx = low_rank(left_ref[8 * k : 8 * k + 8, :rows], right_ref[:, at : at + width])
        merged = grad_ref[:, low : low + width].astype(F32) + error_ref[...]
        left_over = merged - approx * (1.0 / replicas)
        out_ref[...] = left_over
        added = jnp.where(lane == 3 + k, jnp.sum(left_over * left_over), added)
        at += width
    sq_ref[...] = jnp.where(row == 0, added, 0.0)


def feedback_attention(replicas, rows, operands):
    shapes = [operands[k].shape for k in (4, 5, 6)]
    return pl.pallas_call(
        functools.partial(feedback_attention_kernel, replicas, rows),
        in_specs=vmem_specs(len(operands)),
        out_specs=vmem_specs(4),
        out_shape=[struct(shape) for shape in shapes] + [struct((8, 128))],
        compiler_params=params(),
        name="feedback_attention",
    )(*operands)


def squares_sync_kernel(reps, shards, count, *refs):
    out_ref, plane, line, ps, pr, zs, zr = refs[count:]
    rep, shard = lax.axis_index("rep"), lax.axis_index("shard")
    greet(reps, shards)
    added = refs[0][...]
    for ref in refs[1:count]:
        added = added + ref[...]
    plane[rep] = added
    send_all("rep", reps, lambda to: plane.at[rep], lambda step: plane.at[rep], ps, pr)
    summed = plane[0]
    for k in range(1, reps):
        summed = summed + plane[k]
    line[shard] = summed
    send_all("shard", shards, lambda to: line.at[shard], lambda step: line.at[shard], zs, zr)
    summed = line[0]
    for k in range(1, shards):
        summed = summed + line[k]
    out_ref[...] = summed


def squares_sync(reps, shards, parts):
    dma = pltpu.SemaphoreType.DMA
    return pl.pallas_call(
        functools.partial(squares_sync_kernel, reps, shards, len(parts)),
        in_specs=vmem_specs(len(parts)),
        out_specs=pl.BlockSpec(memory_space=pltpu.VMEM),
        out_shape=struct((8, 128)),
        scratch_shapes=[
            pltpu.VMEM((reps, 8, 128), F32),
            pltpu.VMEM((shards, 8, 128), F32),
            dma((reps - 1,)),
            dma((reps - 1,)),
            dma((shards - 1,)),
            dma((shards - 1,)),
        ],
        compiler_params=params(collective_id=3, has_side_effects=True),
        name="squares_sync",
    )(*parts)


def per_device(
    tokens,
    cotangent,
    seg_ids,
    parents,
    positions,
    routes,
    query_weight,
    pair_weight,
    output_weight,
    inner_weight,
    outer_weight,
    router_weight,
    norm_gains,
    query_moment,
    pair_moment,
    output_moment,
    inner_moment,
    outer_moment,
    router_moment,
    gains_moment,
    query_error,
    pair_error,
    output_error,
    inner_error,
    outer_error,
    query_start,
    pair_start,
    output_start,
    inner_start,
    outer_start,
):
    replicas = lax.axis_size("rep")
    shard_count = lax.axis_size("shard")
    here = lax.axis_index("shard")
    both = ("rep", "shard")
    bf16 = jnp.bfloat16
    query_t = jnp.swapaxes(query_weight, 0, 1).astype(bf16)
    pair_t = jnp.swapaxes(pair_weight, 1, 2).astype(bf16)
    output_t = jnp.swapaxes(output_weight, 0, 1).astype(bf16)
    inner_t = jnp.transpose(inner_weight, (1, 0, 3, 2)).astype(bf16)
    outer_low = outer_weight.astype(bf16)
    router_t = jnp.swapaxes(router_weight, 0, 1).astype(bf16)
    gains_low = norm_gains.astype(bf16)
    own_rows = query_t.shape[1]
    q_cols, p_cols, f_cols = query_t.shape[0], pair_t.shape[1], inner_t.shape[2]
    f_rows = outer_low.shape[1]
    small = jnp.concatenate([router_t, gains_low], axis=0)
    small = jnp.pad(small, ((0, 16 - small.shape[0]), (0, 0)))
    per_chunk = E // CHUNKS
    outer_cols = outer_low.shape[2]
    paired = replicas % 2 == 0 and per_chunk == 2 and own_rows == 2 * outer_cols == 2 * f_rows
    paired = paired and 2 * f_cols == f_rows and own_rows % 128 == 0
    paired = paired and q_cols % 16 == 0 and p_cols % 16 == 0 and f_cols % 16 == 0

    def whole_weights(inner_all, outer_all):
        inner_all = inner_all.reshape(replicas, shard_count, per_chunk, 2, f_cols, own_rows)
        w1 = jnp.transpose(inner_all, (2, 3, 0, 4, 1, 5)).reshape(
            1, 1, per_chunk, 2 * replicas * f_cols, shard_count * own_rows
        )
        w2 = jnp.transpose(outer_all, (2, 1, 3, 0, 4)).reshape(
            1, per_chunk, 1, 1, shard_count * f_rows, replicas * outer_cols
        )
        return w1, w2, False

    cot_t = jnp.transpose(cotangent)
    chunk_weights = []
    if paired:
        core = lax.axis_index("rep") % 2
        outer_pairs = outer_low.reshape(CHUNKS, 2, f_rows, outer_cols)
        keep = jnp.where(core == 0, outer_pairs[:, 0], outer_pairs[:, 1])
        give = jnp.where(core == 0, outer_pairs[:, 1], outer_pairs[:, 0])
        got = lax.ppermute(give, "rep", [(i, i + 1 - 2 * (i % 2)) for i in range(replicas)])
        wide_outer = jnp.concatenate(
            [jnp.where(core == 0, keep, got), jnp.where(core == 0, got, keep)], axis=2
        )
        inner_packs = inner_t.reshape(CHUNKS, per_chunk * 2 * f_cols, own_rows)
        packs = [
            jnp.concatenate([inner_packs[k], wide_outer[k]], axis=0) for k in range(CHUNKS)
        ]
        opened = open_gather(
            replicas,
            shard_count,
            [(0, query_t), (0, pair_t[0]), (0, pair_t[1]), (0, output_t)],
            small,
            packs[:1],
            cot_t,
        )
        query_full, key_full, value_full, output_full, small_full = opened[:5]
        height = packs[0].shape[0]
        near = z_slots(packs[1])
        first_line, below_u, above_u = opened[5:]
    else:
        packed = jnp.concatenate(
            [query_t, pair_t.reshape(2 * p_cols, own_rows), output_t, small], axis=0
        )
        spread = lax.all_gather(packed, both).reshape(
            replicas, shard_count, packed.shape[0], own_rows
        )

        def joined(low, high):
            piece = jnp.transpose(spread[:, :, low:high], (0, 2, 1, 3))
            return piece.reshape(-1, shard_count * own_rows)

        at = q_cols + 2 * p_cols
        query_full = joined(0, q_cols)
        key_full, value_full = joined(q_cols, q_cols + p_cols), joined(q_cols + p_cols, at)
        output_full = joined(at, at + q_cols)
        small_full = joined(at + q_cols, packed.shape[0])[: small.shape[0]]
        for index in range(CHUNKS):
            span = slice(index * per_chunk, (index + 1) * per_chunk)
            chunk_weights.append(
                whole_weights(
                    lax.all_gather(inner_t[span], both),
                    lax.all_gather(outer_low[span], both).reshape(
                        replicas, shard_count, per_chunk, f_rows, outer_cols
                    ),
                )
            )
    router_full = small_full[:E]
    gain_values = small_full[E : E + 2].astype(jnp.float32)

    hidden = tokens.astype(jnp.float32)
    length = hidden.shape[0]
    position = positions[0]
    allowed = path_mask(seg_ids[0], parents[0])
    first_low = rms_norm(hidden, gain_values[0]).astype(bf16)
    half_head = HD // 2
    frequency = ROPE_BASE ** (-2.0 * jnp.arange(half_head, dtype=jnp.float32) / HD)
    angles = position.astype(jnp.float32)[:, None] * frequency[None, :]
    cosine = jnp.concatenate([jnp.cos(angles), jnp.cos(angles)], axis=1)
    sine = jnp.concatenate([-jnp.sin(angles), jnp.sin(angles)], axis=1)
    mask = allowed.astype(bf16)
    query_rot, key_rot, values, mixed_low, middle = attention_forward(
        (
            first_low, query_full, key_full, value_full, output_full, tokens, cosine, sine, mask,
        )
    )
    second_low = rms_norm(middle, gain_values[1]).astype(bf16)
    logits = jnp.einsum("td,ed->te", second_low, router_full, preferred_element_type=jnp.float32)
    expert_ids = jnp.arange(E, dtype=jnp.int32)
    route_mask = jnp.any(routes[:, :, None] == expert_ids[None, None, :], axis=1)
    route_top = jnp.max(jnp.where(route_mask, logits, -1e30), axis=-1, keepdims=True)
    raised_gate = jnp.where(route_mask, jnp.exp(logits - route_top), 0.0)
    shares = raised_gate / jnp.sum(raised_gate, axis=-1, keepdims=True)
    shares_t = jnp.transpose(shares)
    shares_high = shares_t.astype(bf16)
    shares_rest = (shares_t - shares_high.astype(jnp.float32)).astype(bf16)
    tree_x = jnp.concatenate([jnp.transpose(second_low), shares_high, shares_rest], axis=0)

    token = tree_x[:16, :128]
    far = None

    def gathered(line, turned):
        part = lax.all_gather(line, "rep")
        w1 = part.reshape(replicas, shard_count, 3, f_rows, own_rows)
        w2 = part.reshape(replicas // 2, 2, shard_count, 3, f_rows, own_rows)
        chunk_weights.append((w1, w2, turned))

    if paired:
        near, held, token = lax.optimization_barrier(
            (near, jnp.concatenate(packs[2:], axis=0), token)
        )
        far = z_slots(held)
        gathered(first_line, False)
        gathered(jnp.stack(near), True)

    upstream = cotangent.astype(jnp.float32)
    start_in = jnp.swapaxes(inner_start, 2, 3)
    start_out = jnp.swapaxes(outer_start, 1, 2)
    chunks = range(CHUNKS)
    merged_parts, lins, louts = [None] * CHUNKS, [None] * CHUNKS, [None] * CHUNKS
    y_parts, grad_parts, combine_parts = [None] * CHUNKS, [None] * CHUNKS, [None] * CHUNKS
    slots_x, slots_u = {}, {}
    state = {"gate": token, "x": tree_x, "u": cot_t}

    def exchange(step, held_x, held_u):
        ring = [(i, (i + step) % shard_count) for i in range(shard_count)]
        slots_x[step] = lax.ppermute(held_x, "shard", ring)
        slots_u[step] = lax.ppermute(held_u, "shard", ring)

    def own(index):
        done = own_experts(
            index * per_chunk,
            state["x"],
            state["u"],
            cotangent,
            chunk_weights[index],
            inner_error[0],
            outer_error[0],
            state["gate"],
        )
        merged_parts[index] = (done[0], done[1])
        y_parts[index], grad_parts[index] = done[2], done[3]
        combine_parts[index] = done[4][:, :, 0]
        state["gate"] = done[0][0, 0, :16, :128].astype(bf16)

    def others(index, steps, last):
        done = rest_experts(
            index * per_chunk,
            last,
            [slots_x[step] for step in steps],
            [slots_u[step] for step in steps],
            chunk_weights[index],
            start_in,
            start_out,
            *merged_parts[index],
            state["gate"],
        )
        merged_parts[index] = (done[0], done[1])
        if last:
            lins[index], louts[index] = done[2], done[3]
        state["gate"] = done[0][0, 0, :16, :128].astype(bf16)

    def all_others(index, steps):
        groups = [steps[at : at + 3] for at in range(0, len(steps), 3)]
        for group in groups:
            others(index, group, group is groups[-1])

    steps = list(range(1, shard_count))
    filled = shard_count == 4 and CHUNKS == 4
    def far_weights():
        lines, state["gate"] = lax.optimization_barrier((far, state["gate"]))
        lines = jnp.stack(lines)
        for k in range(CHUNKS - 2):
            gathered(lines[:, k * height : (k + 1) * height], True)

    def pass_on(ups, downs):
        forth = [(i, i + 1) for i in range(shard_count - 1)]
        back = [(i + 1, i) for i in range(shard_count - 1)]
        return (
            tuple(lax.ppermute(up, "shard", forth) for up in ups),
            tuple(lax.ppermute(down, "shard", back) for down in downs),
        )

    def not_before(pair):
        pair, state["gate"] = lax.optimization_barrier((pair, state["gate"]))
        return pair

    late = token
    if filled and paired:
        own(0)
        state["x"], state["u"] = held = not_before((state["x"], state["u"]))
        ups, downs = [held], [held]
        up, down = pass_on(held[:1], held[:1])
        ups.append((up[0], below_u))
        downs.append((down[0], above_u))
        far_weights()
        own(1)
        ups[1], downs[1] = not_before((ups[1], downs[1]))
        up, down = pass_on(ups[1], downs[1])
        ups.append(up)
        downs.append(down)
        slots_x[1], slots_u[1] = (jnp.where(here >= 1, ups[1][k], downs[1][k]) for k in range(2))
        others(0, [1], False)
        own(2)
        others(1, [1], False)
        ups[2], downs[2] = not_before((ups[2], downs[2]))
        up, down = pass_on(ups[2], downs[2])
        ups.append(up)
        downs.append(down)
        others(2, [1], False)
        own(3)
        slots_x[2], slots_u[2] = (
            jnp.where(here == 0, downs[2][k], jnp.where(here == 3, ups[2][k], downs[1][k]))
            for k in range(2)
        )
        slots_x[3], slots_u[3] = (
            jnp.where(
                here == 0,
                downs[3][k],
                jnp.where(here == 1, downs[2][k], jnp.where(here == 2, ups[2][k], ups[3][k])),
            )
            for k in range(2)
        )
        for array in (*ups[3], *downs[3]):
            late = late + array[:16, :128]
    else:
        if paired:
            far_weights()
        for step in steps:
            exchange(step, tree_x, cot_t)
        for index in chunks:
            own(index)
    combined = middle
    second_grad = grad_parts[0]
    for index in chunks:
        combined = combined + y_parts[index]
        if index:
            second_grad = second_grad + grad_parts[index]
    output = combined.astype(bf16)
    combine_grad = jnp.transpose(jnp.concatenate(combine_parts, axis=0))
    logit_low = (
        shares * (combine_grad - jnp.sum(shares * combine_grad, axis=-1, keepdims=True))
    ).astype(bf16)
    grad_router = jnp.einsum("td,te->de", second_low, logit_low, preferred_element_type=jnp.float32)
    second_grad = second_grad + jnp.einsum(
        "te,ed->td", logit_low, router_full, preferred_element_type=jnp.float32
    )
    _, second_pull = jax.vjp(rms_norm, middle, gain_values[1])
    middle_part, gain_two = second_pull(second_grad)
    middle_grad = upstream + middle_part
    middle_low = middle_grad.astype(bf16)
    grad_output = jnp.einsum("tq,td->qd", mixed_low, middle_low, preferred_element_type=jnp.float32)
    group_output = lax.psum_scatter(
        grad_output.astype(bf16), "shard", scatter_dimension=0, tiled=True
    )
    joint_grad, grad_joint = attention_backward(
        (
            middle_low, output_full, query_rot, key_rot, values, cosine, sine, mask, first_low,
            late,
        )
    )
    group_joint = lax.psum_scatter(
        grad_joint, "shard", scatter_dimension=0, tiled=True
    )
    first_grad = (
        nn(joint_grad[:, :QW], query_full)
        + nn(joint_grad[:, QW : QW + HK * HD], key_full)
        + nn(joint_grad[:, QW + HK * HD :], value_full)
    )
    _, first_pull = jax.vjp(rms_norm, hidden, gain_values[0])
    hidden_part, gain_one = first_pull(first_grad)
    input_grad = (middle_grad + hidden_part).astype(bf16)
    grad_gains = jnp.stack([gain_one, gain_two])

    state["gate"] = joint_grad
    if filled and paired:
        others(3, [1, 2, 3], True)
        others(2, [2, 3], True)
        others(0, [2, 3], True)
        others(1, [2, 3], True)
    else:
        for index in chunks:
            all_others(index, steps)

    small_rows = [jnp.transpose(grad_router), jnp.pad(grad_gains, ((0, 6), (0, 0)))]
    start_q, start_o = jnp.transpose(query_start), jnp.transpose(output_start)
    start_p = jnp.swapaxes(pair_start, 1, 2)
    z_part, own_left = left_parts(
        shard_count,
        own_rows,
        (
            first_low, joint_grad, mixed_low, middle_low, start_q, start_p[0], start_p[1], start_o,
            query_error[0], pair_error[0], output_error[0], *small_rows,
        ),
    )
    left_flat, left_out_flat, totals, total_squares, left_lines = left_sync(
        replicas, shard_count, z_part, own_left, lins, louts, group_joint[:16, :128]
    )
    wide, wide_out = left_flat.shape[1], left_out_flat.shape[1]
    lefts = left_flat.reshape(-1, 8, wide)
    lefts_in = lefts[4:].reshape(2, E, 8, wide)
    lefts_out = left_out_flat.reshape(E, 8, wide_out)
    lefts_t = (
        lefts[0, :, :own_rows],
        lefts[1:3, :, :own_rows],
        lefts[3, :, :own_rows],
        lefts_in[..., :own_rows],
        lefts_out[..., :f_rows],
    )
    bases = tuple(jnp.swapaxes(left, -1, -2) for left in lefts_t)

    right_parts = [
        right_experts(index * per_chunk, lefts_in, lefts_out, *merged_parts[index])
        for index in range(CHUNKS)
    ]
    right_rest = right_attention(
        shard_count,
        own_rows,
        (
            left_flat[:32], left_lines, first_low, joint_grad, mixed_low, middle_low,
            query_error[0], pair_error[0], output_error[0],
        ),
    )
    rights = right_sync(replicas, shard_count, right_parts, right_rest)
    hidden_units = inner_error.shape[4]
    step = 2 * hidden_units + D
    by_expert = rights[:, : E * step].reshape(8, E, step)
    rest = rights[:, E * step :]
    kv = HK * HD
    rights_t = (
        rest[:, :QW],
        jnp.stack([rest[:, QW : QW + kv], rest[:, QW + kv : QW + 2 * kv]]),
        rest[:, QW + 2 * kv : QW + 2 * kv + D],
        jnp.transpose(by_expert[:, :, : 2 * hidden_units].reshape(8, E, 2, hidden_units), (2, 1, 0, 3)),
        jnp.transpose(by_expert[:, :, 2 * hidden_units :], (1, 0, 2)),
    )
    right_out = tuple(jnp.swapaxes(right, -1, -2) for right in rights_t)

    feedback_in = feedback_out = None
    squares_experts = []
    for index in range(CHUNKS):
        feedback_in, feedback_out, part = feedback_experts(
            replicas, index * per_chunk, lefts_in, lefts_out, rights, *merged_parts[index],
            feedback_in, feedback_out,
        )
        squares_experts.append(part)
    feedback_q, feedback_p, feedback_o, squares_rest = feedback_attention(
        replicas,
        own_rows,
        (
            left_flat[:32], rest[:, : QW + 2 * kv + D], group_joint, group_output,
            query_error[0], pair_error[0], output_error[0],
        ),
    )
    feedbacks = tuple(
        part[None] for part in (feedback_q, feedback_p, feedback_o, feedback_in, feedback_out)
    )
    squares = squares_sync(replicas, shard_count, squares_experts + [squares_rest])
    flat_squares = jnp.concatenate(
        [squares[0, 3:7], squares[:, 0], squares[:, 1], squares[:, 2]], axis=0
    )

    column_index = lax.axis_index("rep")
    weights_now = (query_weight, pair_weight, output_weight, inner_weight, outer_weight)
    moments_now = (query_moment, pair_moment, output_moment, inner_moment, outer_moment)
    step_rates = (
        STEP_RATE * D ** (-0.5),
        STEP_RATE * D ** (-0.5),
        STEP_RATE * (QW * 4 // TOK_DEV + 1) ** (-0.5),
        STEP_RATE * D ** (-0.5),
        STEP_RATE * (F // 2) ** (-0.5),
    )
    momenta = []
    new_masters = []
    entry_list = []
    for index in range(5):
        left, right = lefts_t[index], rights_t[index]
        columns = right.shape[-1]
        entries = left.shape[-1] * shard_count * columns
        own_columns = columns // replicas
        squared_right = jnp.sum(right * right, axis=(-2, -1))
        scale_norm = jnp.sqrt(squared_right / entries + 1e-06)
        own_right = lax.dynamic_slice_in_dim(
            right, column_index * own_columns, own_columns, axis=right.ndim - 1
        )
        direction = (
            jnp.einsum("...km,...kn->...mn", left, own_right, precision=lax.Precision.HIGH)
            / scale_norm[..., None, None]
        )
        new_master, new_moment = advance(
            weights_now[index], moments_now[index], direction, step_rates[index], WEIGHT_DECAY
        )
        momenta.append(new_moment)
        new_masters.append(new_master)
        entry_list += [float(replicas * entries)] * (left.size // (8 * left.shape[-1]))
    feedback_rms = jnp.sqrt(flat_squares / jnp.array(entry_list, F32))
    router_total = jnp.transpose(totals[0, :, :own_rows])
    gains_total = totals[1, :2, :own_rows]
    router_square = jnp.sum(total_squares[:, 0])
    gains_square = total_squares[:2, 1]
    router_direction = router_total / jnp.sqrt(
        router_square / (router_total.shape[0] * shard_count * router_total.shape[1]) + 1e-06
    )
    gains_direction = (
        gains_total / jnp.sqrt(gains_square / (gains_total.shape[1] * shard_count) + 1e-06)[:, None]
    )
    router_master, router_momentum = advance(
        router_weight, router_moment, router_direction, STEP_RATE * (8 * D) ** (-0.5), WEIGHT_DECAY
    )
    gains_master, gains_momentum = advance(
        norm_gains, gains_moment, gains_direction, GAIN_RATE, 0.0
    )
    return (
        output,
        input_grad,
        *bases,
        *right_out,
        *feedbacks,
        *momenta,
        router_momentum,
        gains_momentum,
        *new_masters,
        router_master,
        gains_master,
        feedback_rms,
    )


def solution(mesh):
    in_specs = (
        P(("rep", "shard"), None),
        P(("rep", "shard"), None),
        P(("rep", "shard"), None),
        P(("rep", "shard"), None),
        P(("rep", "shard"), None),
        P(("rep", "shard"), None),
        P("shard", "rep"),
        P(None, "shard", "rep"),
        P("shard", "rep"),
        P(None, None, "shard", "rep"),
        P(None, "shard", "rep"),
        P("shard", None),
        P(None, "shard"),
        P("shard", "rep"),
        P(None, "shard", "rep"),
        P("shard", "rep"),
        P(None, None, "shard", "rep"),
        P(None, "shard", "rep"),
        P("shard", None),
        P(None, "shard"),
        P("rep", "shard", None),
        P("rep", None, "shard", None),
        P("rep", "shard", None),
        P("rep", None, None, "shard", None),
        P("rep", None, "shard", None),
        P(),
        P(),
        P(),
        P(),
        P(),
    )
    out_specs = (
        P(("rep", "shard"), None),
        P(("rep", "shard"), None),
        P("shard", None),
        P(None, "shard", None),
        P("shard", None),
        P(None, None, "shard", None),
        P(None, "shard", None),
        P(),
        P(),
        P(),
        P(),
        P(),
        P("rep", "shard", None),
        P("rep", None, "shard", None),
        P("rep", "shard", None),
        P("rep", None, None, "shard", None),
        P("rep", None, "shard", None),
        P("shard", "rep"),
        P(None, "shard", "rep"),
        P("shard", "rep"),
        P(None, None, "shard", "rep"),
        P(None, "shard", "rep"),
        P("shard", None),
        P(None, "shard"),
        P("shard", "rep"),
        P(None, "shard", "rep"),
        P("shard", "rep"),
        P(None, None, "shard", "rep"),
        P(None, "shard", "rep"),
        P("shard", None),
        P(None, "shard"),
        P(),
    )
    return jax.shard_map(
        per_device, mesh=mesh, in_specs=in_specs, out_specs=out_specs, check_vma=False
    )
```
